32 devices in a mesh: dp: 4 (over y, core), mp: 8 (over z, x).
Axes of the slice: x: 2, y: 2, z: 4, core: 2. Of those that a mesh axis runs over, the one named last changes fastest.
Arguments:
- block_input: bfloat16 [4096, 768], P(('dp', 'mp')), may hold values from -6 to 6
- mixer_gain: float32 [768], replicated, may hold values from 0.5 to 1.5
- in_weight: bfloat16 [768, 2304], P(None, 'mp'), may hold values from -0.21875 to 0.21875
- in_bias: float32 [2304], P('mp'), may hold values from -1.75 to 1.75
- short_taps: float32 [3, 2304], P(None, 'mp'), may hold values from -3.5 to 3.5
- skip_gain: float32 [768], P('mp'), may hold values from -6 to 6
- out_weight: bfloat16 [768, 768], P('mp'), may hold values from -0.21875 to 0.21875
- out_bias: float32 [768], replicated, may hold values from -1.75 to 1.75
- ffn_gain: float32 [768], replicated, may hold values from 0.5 to 1.5
- up_weight: bfloat16 [768, 3072], P(None, 'mp'), may hold values from -0.21875 to 0.21875
- up_bias: bfloat16 [3072], P('mp'), may hold values from -1.75 to 1.75
- down_weight: bfloat16 [3072, 768], P('mp'), may hold values from -0.109375 to 0.109375
- down_bias: float32 [768], replicated, may hold values from -1.75 to 1.75
- embed_weight: float32 [33, 64], replicated, may hold values from -6 to 6
- embed_bias: float32 [64], replicated, may hold values from -3 to 3
- embed_freq: float32 [64], replicated, may hold values from 1 to 3
- hidden_weight: float32 [64, 64], replicated, may hold values from -1.75 to 1.75
- hidden_bias: float32 [64], replicated, may hold values from -3 to 3
- hidden_freq: float32 [64], replicated, may hold values from 1 to 3
- filter_weight: float32 [64, 768], replicated, may hold values from -0.0625 to 0.0625
- decay_rate: float32 [768], replicated, may hold values from 0.5 to 3
- out_grad: bfloat16 [4096, 768], P(('dp', 'mp')), may hold values from -6 to 6
- sequence_lengths: int32 [9], replicated, may hold values from 256 to 1024, as said below
- sequence_rank: int32 [9], replicated, may hold values from 0 to 3, as said below
- sequence_offset: int32 [9], replicated, may hold values from 0 to 768, as said below
Outputs:
- block_output: bfloat16 [4096, 768], P(('dp', 'mp'))
- input_grad: float32 [4096, 768], P(('dp', 'mp'))
- penalty: float32 [], replicated
- mixer_gain_grad: float32 [768], replicated
- in_weight_grad: float32 [768, 2304], P(None, 'mp')
- in_bias_grad: float32 [2304], P('mp')
- short_taps_grad: float32 [3, 2304], P(None, 'mp')
- skip_gain_grad: float32 [768], P('mp')
- out_weight_grad: float32 [768, 768], P('mp')
- out_bias_grad: float32 [768], replicated
- ffn_gain_grad: float32 [768], replicated
- up_weight_grad: float32 [768, 3072], P(None, 'mp')
- up_bias_grad: float32 [3072], P('mp')
- down_weight_grad: float32 [3072, 768], P('mp')
- down_bias_grad: float32 [768], replicated
- embed_weight_grad: float32 [33, 64], replicated
- embed_bias_grad: float32 [64], replicated
- embed_freq_grad: float32 [64], replicated
- hidden_weight_grad: float32 [64, 64], replicated
- hidden_bias_grad: float32 [64], replicated
- hidden_freq_grad: float32 [64], replicated
- filter_weight_grad: float32 [64, 768], replicated
- decay_rate_grad: float32 [768], replicated
The draws below stay inside these ranges and needn't reach their ends.
Inputs may be any that keep to these rules, and one draw needn't show every extreme that they name: `sequence_lengths`: 1 sequence have 1024 tokens, the others 256. `sequence_rank`: every pack holds one sequence of 1024 tokens or one to four of 256 tokens, and at least one sequence. `sequence_offset`: a multiple of 256; the sequences of one pack do not intersect and end by slot 1024; unused slots are padding.
All inputs are finite; a program needn't handle non-finite values.
Results may differ from the reference program's by a relative error of at most 0.02.
Values may be sent and summed in bfloat16 or wider, within the bound.
A program may use at most 128 MiB of HBM per device.

```python
import math
import jax
import jax.numpy as jnp
from jax import lax

D = 768
FF = 3072
FILT = 64
BANDS = 16
EMB = 33
LONG = 1024
SHORT = 256
NLONG = 1
NSHORT = 8
NSEQ = 9
TOKENS = 4096
N_DP = 4


def layout_draw(key):
    rank_key = jax.random.fold_in(key, 11)
    slot_key = jax.random.fold_in(key, 12)
    order_key = jax.random.fold_in(key, 13)
    spare = N_DP - NLONG
    ranks = jax.random.permutation(rank_key, N_DP).astype(jnp.int32)
    others = jax.random.permutation(slot_key, 3 * spare - 1).astype(jnp.int32)
    others = others + (others >= 2).astype(jnp.int32)
    extra = jnp.concatenate([jnp.full((1,), 2, jnp.int32), others])[:NSHORT - spare]
    short_index = jnp.concatenate([jnp.arange(spare, dtype=jnp.int32), extra // 3])
    short_slot = jnp.concatenate([jnp.zeros((spare,), jnp.int32), extra % 3 + 1])
    lengths = jnp.concatenate([jnp.full((NLONG,), LONG, jnp.int32), jnp.full((NSHORT,), SHORT, jnp.int32)])
    owners = jnp.concatenate([ranks[:NLONG], ranks[NLONG:][short_index]])
    offsets = jnp.concatenate([jnp.zeros((NLONG,), jnp.int32), short_slot * SHORT])
    shuffle = jax.random.permutation(order_key, NSEQ).astype(jnp.int32)
    return (lengths[shuffle], owners[shuffle], offsets[shuffle])


def draw_sequence_lengths(key, part):
    return layout_draw(key)[0]


def draw_sequence_rank(key, part):
    return layout_draw(key)[1]


def draw_sequence_offset(key, part):
    return layout_draw(key)[2]


def block_scale(key, shape, split, smallest, largest):
    def one(dim, parts):
        steps = jax.random.uniform(jax.random.fold_in(jax.random.fold_in(key, 6), dim), (parts,), jnp.float32, smallest / len(split), largest / len(split))
        return jnp.repeat(jnp.exp(steps), shape[dim] // parts).reshape((-1,) + (1,) * (len(shape) - dim - 1))

    level = one(*split[0])
    for cut in split[1:]:
        level = level * one(*cut)
    return level


def bell_draw(stream_key, dims, scale, limit, shards=(), held_as=jnp.bfloat16):
    factor_of = block_scale(stream_key, dims, shards, -0.22, 0.18) if shards else 1.0
    values = jax.random.normal(stream_key, dims, jnp.float32) * scale * factor_of
    return jnp.minimum(jnp.maximum(values, -limit), limit).astype(held_as)


def setup_inputs(seed: int = 0) -> dict:
    keys = jax.random.split(jax.random.key(seed), 26)
    block_input = bell_draw(keys[0], (TOKENS, D), 1.0, 6.0, ((0, 32),))
    mixer_gain = jnp.clip(1.0 + 0.1 * jax.random.normal(keys[1], (D,), jnp.float32), 0.5, 1.5)
    in_weight = bell_draw(keys[2], (D, 3 * D), D ** -0.5, 0.21875, ((1, 8),))
    in_bias = bell_draw(keys[3], (3 * D,), 0.3, 1.75, ((0, 8),), jnp.float32)
    short_taps = bell_draw(keys[4], (3, 3 * D), 0.6, 3.5, ((1, 8),), jnp.float32)
    skip_gain = bell_draw(keys[5], (D,), 1.0, 6.0, ((0, 8),), jnp.float32)
    out_weight = bell_draw(keys[6], (D, D), D ** -0.5, 0.21875, ((0, 8),))
    out_bias = bell_draw(keys[7], (D,), 0.3, 1.75, (), jnp.float32)
    ffn_gain = jnp.clip(1.0 + 0.1 * jax.random.normal(keys[8], (D,), jnp.float32), 0.5, 1.5)
    up_weight = bell_draw(keys[9], (D, FF), D ** -0.5, 0.21875, ((1, 8),))
    up_bias = bell_draw(keys[10], (FF,), 0.3, 1.75, ((0, 8),))
    down_weight = bell_draw(keys[11], (FF, D), FF ** -0.5, 0.109375, ((0, 8),))
    down_bias = bell_draw(keys[12], (D,), 0.3, 1.75, (), jnp.float32)
    embed_weight = bell_draw(keys[13], (EMB, FILT), 1.0, 6.0, (), jnp.float32)
    embed_bias = bell_draw(keys[14], (FILT,), 0.5, 3.0, (), jnp.float32)
    embed_freq = jnp.clip(jnp.exp(jax.random.uniform(keys[15], (FILT,), jnp.float32, math.log(1.0), math.log(3.0))), 1.0, 3.0)
    hidden_weight = bell_draw(keys[16], (FILT, FILT), 0.3, 1.75, (), jnp.float32)
    hidden_bias = bell_draw(keys[17], (FILT,), 0.5, 3.0, (), jnp.float32)
    hidden_freq = jnp.clip(jnp.exp(jax.random.uniform(keys[18], (FILT,), jnp.float32, math.log(1.0), math.log(3.0))), 1.0, 3.0)
    filter_weight = bell_draw(keys[19], (FILT, D), (LONG * FILT // 8) ** -0.5, 0.0625, (), jnp.float32)
    decay_rate = jnp.clip(jnp.exp(jax.random.uniform(keys[20], (D,), jnp.float32, math.log(0.5), math.log(3.0))), 0.5, 3.0)
    out_grad = bell_draw(keys[21], (TOKENS, D), 1.0, 6.0, ((0, 32),))
    sequence_lengths = draw_sequence_lengths(jax.random.fold_in(keys[25], 71), 0)
    sequence_rank = draw_sequence_rank(jax.random.fold_in(keys[25], 71), 0)
    sequence_offset = draw_sequence_offset(jax.random.fold_in(keys[25], 71), 0)
    return {"block_input": block_input, "mixer_gain": mixer_gain, "in_weight": in_weight, "in_bias": in_bias, "short_taps": short_taps, "skip_gain": skip_gain, "out_weight": out_weight, "out_bias": out_bias, "ffn_gain": ffn_gain, "up_weight": up_weight, "up_bias": up_bias, "down_weight": down_weight, "down_bias": down_bias, "embed_weight": embed_weight, "embed_bias": embed_bias, "embed_freq": embed_freq, "hidden_weight": hidden_weight, "hidden_bias": hidden_bias, "hidden_freq": hidden_freq, "filter_weight": filter_weight, "decay_rate": decay_rate, "out_grad": out_grad, "sequence_lengths": sequence_lengths, "sequence_rank": sequence_rank, "sequence_offset": sequence_offset}


precise = lax.Precision.HIGHEST

@jax.custom_vjp
def low(v):
    return lax.optimization_barrier(v.astype(jnp.bfloat16)).astype(jnp.float32)

@jax.custom_vjp
def low_back(v):
    return v

def low_keep(v):
    return (low(v), None)

def low_pass(kept, grad):
    return (grad,)

def back_keep(v):
    return (v, None)

def back_low(kept, grad):
    return (low(grad),)
low.defvjp(low_keep, low_pass)
low_back.defvjp(back_keep, back_low)

def matmul_high(left, right):
    return jnp.dot(left, right, precision=precise, preferred_element_type=jnp.float32)

def layer_norm(values, scaling):
    center = values - lax.optimization_barrier(jnp.mean(values, axis=-1, keepdims=True))
    spread = lax.optimization_barrier(jnp.mean(center * center, axis=-1, keepdims=True))
    return center * lax.rsqrt(spread + 1e-05) * scaling

def filter_values(embed_weight, embed_bias, embed_freq, hidden_weight, hidden_bias, hidden_freq, filter_weight, decay_rate, places):
    scaled = places / LONG
    harmonic = jnp.arange(1, BANDS + 1, dtype=jnp.float32)
    angles = 2.0 * math.pi * scaled[:, None] * harmonic[None, :]
    embedding = jnp.concatenate([scaled[:, None], jnp.cos(angles), jnp.sin(angles)], 1)
    first_layer = jnp.sin(embed_freq * (matmul_high(embedding, embed_weight) + embed_bias))
    second_layer = jnp.sin(hidden_freq * (matmul_high(first_layer, hidden_weight) + hidden_bias))
    kernel = matmul_high(second_layer, filter_weight) * jnp.exp(-scaled[:, None] * decay_rate[None, :])
    penalty = jnp.sum(scaled[:, None] * kernel * kernel) / D
    return (kernel, penalty)

def long_conv(kernel, signal, segment):
    length, channel_count = signal.shape
    block_rows = min(length, 128)
    block_count = length // block_rows
    padded_kernel = jnp.concatenate([jnp.zeros((block_rows, channel_count), jnp.float32), kernel, jnp.zeros((block_rows, channel_count), jnp.float32)], 0)
    padded_signal = jnp.concatenate([jnp.zeros((length, channel_count), jnp.float32), signal], 0)
    padded_segment = jnp.concatenate([jnp.full((length,), -2, jnp.int32), segment.astype(jnp.int32)], 0)
    own_segment = segment.astype(jnp.int32).reshape(block_count, block_rows)

    def visit(running, lag_block):
        window = lax.dynamic_slice_in_dim(padded_kernel, lag_block * block_rows, 2 * block_rows, 0)
        rolled = jnp.concatenate([window[block_rows:], window[:block_rows]], 0).T
        tiled_kernel = jnp.tile(rolled, (1, block_rows))[:, :block_rows * (2 * block_rows - 1)]
        toeplitz = tiled_kernel.reshape(channel_count, block_rows, 2 * block_rows - 1)[:, :, :block_rows]
        start_row = length - lag_block * block_rows
        shifted = lax.dynamic_slice_in_dim(padded_signal, start_row, length, 0).reshape(block_count, block_rows, channel_count)
        shifted_segment = lax.dynamic_slice_in_dim(padded_segment, start_row, length, 0).reshape(block_count, block_rows)
        same_segment = (own_segment[:, :, None] == shifted_segment[:, None, :]).astype(jnp.float32)
        added = jnp.einsum('cst,isc,its->itc', toeplitz, shifted, same_segment, precision=precise)
        return (running + added.reshape(length, channel_count), None)
    running, _ = lax.scan(visit, jnp.zeros((length, channel_count), jnp.float32), jnp.arange(block_count, dtype=jnp.int32))
    return running

def short_conv(values, taps, position):
    one_back = jnp.concatenate([jnp.zeros_like(values[:1]), values[:-1]], 0) * (position >= 1).astype(jnp.float32)[:, None]
    two_back = jnp.concatenate([jnp.zeros_like(values[:2]), values[:-2]], 0) * (position >= 2).astype(jnp.float32)[:, None]
    return taps[0] * values + taps[1] * one_back + taps[2] * two_back

def mixer(projected, taps, kernel, skip, segment, position, valid_rows):
    shortened = short_conv(projected, taps, position)
    grouped = shortened.reshape(shortened.shape[0], -1, 3)
    outer_gate = grouped[:, :, 0]
    inner_gate = grouped[:, :, 1]
    value_part = grouped[:, :, 2]
    signal = low(value_part * inner_gate * valid_rows[:, None])
    return (long_conv(kernel, signal, segment) + skip * signal) * outer_gate

def pack_layout(lengths, owners, offsets, rank, length):
    slot_index = jnp.arange(length, dtype=jnp.int32)
    inside = (owners[:, None] == rank) & (slot_index[None, :] >= offsets[:, None]) & (slot_index[None, :] < offsets[:, None] + lengths[:, None])
    valid_rows = jnp.any(inside, 0)
    identity = jnp.arange(lengths.shape[0], dtype=jnp.int32)
    segment = jnp.where(valid_rows, lax.optimization_barrier(jnp.sum(jnp.where(inside, identity[:, None], 0), 0)), -1).astype(jnp.int32)
    position = lax.optimization_barrier(jnp.sum(jnp.where(inside, slot_index[None, :] - offsets[:, None], 0), 0)).astype(jnp.int32)
    return (segment, position, valid_rows.astype(jnp.float32))

def pack_forward(weights, kernel, row_values, segment, position, valid_rows):
    mixer_gain, in_weight, in_bias, short_taps, skip_gain, out_weight, out_bias, ffn_gain, up_weight, up_bias, down_weight, down_bias = weights
    normed = low(layer_norm(row_values, mixer_gain))
    projected = low_back(matmul_high(normed, in_weight) + in_bias)
    mixed = low(mixer(projected, short_taps, low_back(kernel), skip_gain, segment, position, valid_rows))
    branch = low_back(matmul_high(mixed, out_weight) + out_bias)
    middle = row_values + branch
    normed_two = low(layer_norm(middle, ffn_gain))
    hidden = low_back(matmul_high(normed_two, up_weight) + up_bias)
    active = low(jax.nn.gelu(hidden, approximate=True))
    return middle + low_back(matmul_high(active, down_weight) + down_bias)

def forward(weights, filters, block_input, lengths, owners, offsets):
    kernel, penalty = filter_values(*filters, jnp.arange(LONG, dtype=jnp.float32))
    rounded = low(kernel)
    packs = block_input.reshape(N_DP, LONG, D)
    checked = jax.checkpoint(pack_forward)

    def visit(running, item):
        row_values, rank = item
        segment, position, valid_rows = pack_layout(lengths, owners, offsets, rank, LONG)
        return (running, checked(weights, rounded, row_values, segment, position, valid_rows))
    _, outputs = lax.scan(visit, jnp.zeros((), jnp.float32), (packs, jnp.arange(N_DP, dtype=jnp.int32)))
    return (outputs.reshape(N_DP * LONG, D), penalty)

def reference(block_input, mixer_gain, in_weight, in_bias, short_taps, skip_gain, out_weight, out_bias, ffn_gain, up_weight, up_bias, down_weight, down_bias, embed_weight, embed_bias, embed_freq, hidden_weight, hidden_bias, hidden_freq, filter_weight, decay_rate, out_grad, sequence_lengths, sequence_rank, sequence_offset):
    weights = tuple((weight.astype(jnp.float32) for weight in (mixer_gain, in_weight, in_bias, short_taps, skip_gain, out_weight, out_bias, ffn_gain, up_weight, up_bias, down_weight, down_bias)))
    filters = tuple((weight.astype(jnp.float32) for weight in (embed_weight, embed_bias, embed_freq, hidden_weight, hidden_bias, hidden_freq, filter_weight, decay_rate)))

    def objective(weights, filters, inputs):
        return forward(weights, filters, inputs, sequence_lengths, sequence_rank, sequence_offset)
    (output, penalty), pullback = jax.vjp(objective, weights, filters, block_input.astype(jnp.float32))
    weight_grads, filter_grads, input_grad = pullback((out_grad.astype(jnp.float32), jnp.ones((), jnp.float32)))
    return (output.astype(jnp.bfloat16), input_grad, penalty, weight_grads[0], weight_grads[1], weight_grads[2], weight_grads[3], weight_grads[4], weight_grads[5], weight_grads[6], weight_grads[7], weight_grads[8], weight_grads[9], weight_grads[10], weight_grads[11], filter_grads[0], filter_grads[1], filter_grads[2], filter_grads[3], filter_grads[4], filter_grads[5], filter_grads[6], filter_grads[7])
```

```python
import math

import jax
import jax.numpy as jnp
import numpy as np
from jax import lax
from jax.sharding import PartitionSpec as P

D = 768
BANDS = 16
LONG = 1024


precise = lax.Precision.HIGHEST


def matmul_high(left, right):
    return jnp.dot(left, right, precision=precise, preferred_element_type=jnp.float32)


def matmul(left, right):
    return jnp.dot(left, right, preferred_element_type=jnp.float32)


def inner_rows(left, right):
    return lax.dot_general(
        left, right, (((0,), (0,)), ((), ())), preferred_element_type=jnp.float32
    )


def outer_cols(left, right):
    return lax.dot_general(
        left, right, (((1,), (1,)), ((), ())), preferred_element_type=jnp.float32
    )


def layer_norm(values, scaling):
    center = values - jnp.mean(values, axis=-1, keepdims=True)
    spread = jnp.mean(center * center, axis=-1, keepdims=True)
    return center * lax.rsqrt(spread + 1e-05) * scaling


def activation(values):
    return jax.nn.gelu(values, approximate=True)


def filter_values(
    embed_weight,
    embed_bias,
    embed_freq,
    hidden_weight,
    hidden_bias,
    hidden_freq,
    filter_weight,
    decay_rate,
    places,
):
    scaled = places / LONG
    harmonic = jnp.arange(1, BANDS + 1, dtype=jnp.float32)
    angles = 2.0 * math.pi * scaled[:, None] * harmonic[None, :]
    embedding = jnp.concatenate([scaled[:, None], jnp.cos(angles), jnp.sin(angles)], 1)
    first_layer = jnp.sin(embed_freq * (matmul_high(embedding, embed_weight) + embed_bias))
    second_layer = jnp.sin(hidden_freq * (matmul_high(first_layer, hidden_weight) + hidden_bias))
    kernel = matmul_high(second_layer, filter_weight) * jnp.exp(
        -scaled[:, None] * decay_rate[None, :]
    )
    penalty = jnp.sum(scaled[:, None] * kernel * kernel) / D
    return (kernel, penalty)


BLOCK = 256
BINS = 2 * BLOCK


def wave_table(shift):
    bins = np.arange(BLOCK)[:, None]
    angle = np.pi * (2 * bins + 1) * (np.arange(BLOCK)[None, :] + shift) / BINS
    return np.concatenate([np.cos(angle), -np.sin(angle)], 0)


NEAR = wave_table(0)
FAR = wave_table(-BLOCK)


def low_dot(left, right):
    return jnp.dot(
        jnp.asarray(left, jnp.bfloat16),
        right.astype(jnp.bfloat16),
        preferred_element_type=jnp.float32,
    )


def times(left, right):
    lr, li, rr, ri = left[:BLOCK], left[BLOCK:], right[:BLOCK], right[BLOCK:]
    return jnp.concatenate([lr * rr - li * ri, lr * ri + li * rr], 0)


def times_conj(left, right):
    lr, li, rr, ri = left[:BLOCK], left[BLOCK:], right[:BLOCK], right[BLOCK:]
    return jnp.concatenate([lr * rr + li * ri, lr * ri - li * rr], 0)


def blocks_of(values):
    return [values[i : i + BLOCK] for i in range(0, values.shape[0], BLOCK)]


def kernel_spectra(kernel):
    parts = blocks_of(kernel)
    first = [low_dot(NEAR, parts[0])]
    return first + [
        low_dot(np.concatenate([NEAR, FAR], 1), jnp.concatenate([now, before], 0))
        for now, before in zip(parts[1:], parts[:-1])
    ]


@jax.custom_vjp
def long_conv(kernel, signal, joined):
    return long_conv_keep(kernel, signal, joined)[0]


def long_conv_keep(kernel, signal, joined):
    spectra = kernel_spectra(kernel)
    waves = [low_dot(NEAR, part) for part in blocks_of(signal)]
    out = []
    for i in range(len(waves)):
        total = sum(joined[i, p] * times(spectra[i - p], waves[p]) for p in range(i + 1))
        out.append(low_dot(NEAR.T / BLOCK, total))
    return jnp.concatenate(out, 0), (spectra, waves, joined)


def long_conv_back(kept, grad):
    spectra, waves, joined = kept
    count = len(waves)
    back = [low_dot(NEAR, part) for part in blocks_of(grad)]
    signal_grad = []
    for p in range(count):
        total = sum(
            joined[i, p] * times_conj(spectra[i - p], back[i]) for i in range(p, count)
        )
        signal_grad.append(low_dot(NEAR.T / BLOCK, total))
    spectra_grad = []
    for d in range(count):
        spectra_grad.append(
            sum(joined[i, i - d] * times_conj(waves[i - d], back[i]) for i in range(d, count))
        )
    kernel_grad = []
    for d in range(count):
        part = low_dot(NEAR.T / BLOCK, spectra_grad[d])
        if d + 1 < count:
            part = part + low_dot(FAR.T / BLOCK, spectra_grad[d + 1])
        kernel_grad.append(part)
    return (
        jnp.concatenate(kernel_grad, 0),
        jnp.concatenate(signal_grad, 0),
        jnp.zeros_like(joined),
    )


long_conv.defvjp(long_conv_keep, long_conv_back)


def short_conv(values, taps, position):
    one_back = (
        jnp.concatenate([jnp.zeros_like(values[:1]), values[:-1]], 0)
        * (position >= 1).astype(jnp.float32)[:, None]
    )
    two_back = (
        jnp.concatenate([jnp.zeros_like(values[:2]), values[:-2]], 0)
        * (position >= 2).astype(jnp.float32)[:, None]
    )
    return taps[0] * values + taps[1] * one_back + taps[2] * two_back


def mixer(projected, taps, kernel, skip, segment, position, valid_rows):
    shortened = short_conv(projected, taps, position)
    grouped = shortened.reshape(shortened.shape[0], -1, 3)
    outer_gate = grouped[:, :, 0]
    inner_gate = grouped[:, :, 1]
    value_part = grouped[:, :, 2]
    signal = (
        (value_part * inner_gate * valid_rows[:, None]).astype(jnp.bfloat16).astype(jnp.float32)
    )
    block_segment = segment[::BLOCK]
    joined = (
        (block_segment[:, None] == block_segment[None, :]) & (block_segment >= 0)[:, None]
    ).astype(jnp.float32)
    return (long_conv(kernel, signal, joined) + skip * signal) * outer_gate


def pack_layout(lengths, owners, offsets, rank, length):
    slot_index = jnp.arange(length, dtype=jnp.int32)
    inside = (
        (owners[:, None] == rank)
        & (slot_index[None, :] >= offsets[:, None])
        & (slot_index[None, :] < offsets[:, None] + lengths[:, None])
    )
    valid_rows = jnp.any(inside, 0)
    identity = jnp.arange(lengths.shape[0], dtype=jnp.int32)
    segment = jnp.where(valid_rows, jnp.sum(jnp.where(inside, identity[:, None], 0), 0), -1)
    position = jnp.sum(jnp.where(inside, slot_index[None, :] - offsets[:, None], 0), 0)
    return (segment, position, valid_rows.astype(jnp.float32))


def per_device(
    block_input,
    mixer_gain,
    in_weight,
    in_bias,
    short_taps,
    skip_gain,
    out_weight,
    out_bias,
    ffn_gain,
    up_weight,
    up_bias,
    down_weight,
    down_bias,
    embed_weight,
    embed_bias,
    embed_freq,
    hidden_weight,
    hidden_bias,
    hidden_freq,
    filter_weight,
    decay_rate,
    out_grad,
    sequence_lengths,
    sequence_rank,
    sequence_offset,
):
    model_rank = lax.axis_index("mp")
    data_rank = lax.axis_index("dp")
    model_count = lax.axis_size("mp")
    first_rank = (data_rank == 0).astype(jnp.float32)
    segment, position, valid_rows = pack_layout(
        sequence_lengths, sequence_rank, sequence_offset, data_rank, LONG
    )
    filters = (
        embed_weight,
        embed_bias,
        embed_freq,
        hidden_weight,
        hidden_bias,
        hidden_freq,
        filter_weight,
        decay_rate,
    )
    row_values = block_input.astype(jnp.float32)
    normed, norm_back = jax.vjp(layer_norm, row_values, mixer_gain)
    gathered = lax.all_gather(normed.astype(jnp.bfloat16), "mp", axis=0, tiled=True)
    projected = matmul(gathered, in_weight) + in_bias
    channel_count = in_weight.shape[1] // 3
    places = jnp.arange(LONG, dtype=jnp.float32)
    own_channels = model_rank * channel_count
    local_filters = filters[:6] + (
        lax.dynamic_slice_in_dim(filter_weight, own_channels, channel_count, 1),
        lax.dynamic_slice_in_dim(decay_rate, own_channels, channel_count, 0),
    )

    def own_filter(parameters):
        return filter_values(*parameters, places)

    (kernel, penalty_part), filter_back = jax.vjp(own_filter, local_filters)
    kernel_low = kernel.astype(jnp.bfloat16)

    def mix_local(projected, taps, kernel_values, skip):
        return mixer(projected, taps, kernel_values, skip, segment, position, valid_rows)

    mixed, mixer_back = jax.vjp(
        mix_local, projected, short_taps, kernel_low.astype(jnp.float32), skip_gain
    )
    mixed_low = mixed.astype(jnp.bfloat16)
    branch = (
        lax.psum_scatter(
            matmul(mixed_low, out_weight).astype(jnp.bfloat16),
            "mp",
            scatter_dimension=0,
            tiled=True,
        ).astype(jnp.float32)
        + out_bias
    )
    middle = row_values + branch
    normed_two, ffn_norm_back = jax.vjp(layer_norm, middle, ffn_gain)
    normed_two_low = normed_two.astype(jnp.bfloat16)
    seed = out_grad.astype(jnp.float32)
    gathered_two = lax.all_gather(normed_two_low, "mp", axis=0, tiled=True)
    hidden = matmul(gathered_two, up_weight) + up_bias.astype(jnp.float32)
    active, gelu_back = jax.vjp(activation, hidden)
    active_low = active.astype(jnp.bfloat16)
    update = (
        lax.psum_scatter(
            matmul(active_low, down_weight).astype(jnp.bfloat16),
            "mp",
            scatter_dimension=0,
            tiled=True,
        ).astype(jnp.float32)
        + down_bias
    )
    received = lax.all_gather(out_grad, "mp", axis=0, tiled=True)
    weight_total = inner_rows(active_low, received)
    active_total = outer_cols(received, down_weight)
    down_weight_sum = weight_total
    hidden_grad = gelu_back(active_total)[0].astype(jnp.bfloat16)
    up_bias_sum = jnp.sum(hidden_grad.astype(jnp.float32), 0)
    up_weight_sum = inner_rows(gathered_two, hidden_grad)
    normed_two_grad = lax.psum_scatter(
        outer_cols(hidden_grad, up_weight).astype(jnp.bfloat16),
        "mp",
        scatter_dimension=0,
        tiled=True,
    ).astype(jnp.float32)
    block_output = (middle + update).astype(jnp.bfloat16)
    down_bias_part = jnp.sum(seed, 0)
    middle_norm_grad, ffn_gain_part = ffn_norm_back(normed_two_grad)
    middle_grad = seed + middle_norm_grad
    branch_grad = middle_grad.astype(jnp.bfloat16)
    out_bias_part = jnp.sum(branch_grad.astype(jnp.float32), 0)
    received = lax.all_gather(branch_grad, "mp", axis=0, tiled=True)
    weight_total = inner_rows(mixed_low, received)
    mixed_total = outer_cols(received, out_weight)
    projected_grad, taps_part, kernel_grad, skip_part = mixer_back(mixed_total)
    projected_low = projected_grad.astype(jnp.bfloat16)
    in_bias_part = jnp.sum(projected_low.astype(jnp.float32), 0)
    in_weight_part = inner_rows(gathered, projected_low)
    normed_grad = lax.psum_scatter(
        outer_cols(projected_low, in_weight).astype(jnp.bfloat16),
        "mp",
        scatter_dimension=0,
        tiled=True,
    ).astype(jnp.float32)
    input_part, mixer_gain_part = norm_back(normed_grad)
    input_grad = middle_grad + input_part
    (filter_parts,) = filter_back((kernel_grad, first_rank))
    channel_sums = (
        lax.psum(in_weight_part.astype(jnp.bfloat16), "dp").astype(jnp.float32),
        lax.psum(in_bias_part.astype(jnp.bfloat16), "dp").astype(jnp.float32),
        lax.psum(taps_part.astype(jnp.bfloat16), "dp").astype(jnp.float32),
        lax.psum(skip_part.astype(jnp.bfloat16), "dp").astype(jnp.float32),
        lax.psum(weight_total.astype(jnp.bfloat16), "dp").astype(jnp.float32),
        lax.psum(up_weight_sum.astype(jnp.bfloat16), "dp").astype(jnp.float32),
        lax.psum(up_bias_sum.astype(jnp.bfloat16), "dp").astype(jnp.float32),
        lax.psum(down_weight_sum.astype(jnp.bfloat16), "dp").astype(jnp.float32),
    )
    shared = lax.psum(
        (
            mixer_gain_part,
            ffn_gain_part,
            out_bias_part,
            down_bias_part,
            penalty_part * first_rank,
            filter_parts[0],
            filter_parts[1],
            filter_parts[2],
            filter_parts[3],
            filter_parts[4],
            filter_parts[5],
        ),
        ("dp", "mp"),
    )
    filter_weight_grad = lax.all_gather(
        lax.psum(filter_parts[6], "dp"), "mp", axis=1, tiled=True
    )
    decay_grad = lax.all_gather(lax.psum(filter_parts[7], "dp"), "mp", axis=0, tiled=True)
    return (
        block_output,
        input_grad,
        shared[4],
        shared[0],
        channel_sums[0],
        channel_sums[1],
        channel_sums[2],
        channel_sums[3],
        channel_sums[4],
        shared[2],
        shared[1],
        channel_sums[5],
        channel_sums[6],
        channel_sums[7],
        shared[3],
        shared[5],
        shared[6],
        shared[7],
        shared[8],
        shared[9],
        shared[10],
        filter_weight_grad,
        decay_grad,
    )


def solution(mesh):
    placed = (
        P(("dp", "mp"), None),
        P(),
        P(None, "mp"),
        P("mp"),
        P(None, "mp"),
        P("mp"),
        P("mp", None),
        P(),
        P(),
        P(None, "mp"),
        P("mp"),
        P("mp", None),
        P(),
        P(),
        P(),
        P(),
        P(),
        P(),
        P(),
        P(),
        P(),
        P(("dp", "mp"), None),
        P(),
        P(),
        P(),
    )
    return jax.shard_map(
        per_device,
        mesh=mesh,
        in_specs=placed,
        out_specs=(
            P(("dp", "mp"), None),
            P(("dp", "mp"), None),
            P(),
            P(),
            P(None, "mp"),
            P("mp"),
            P(None, "mp"),
            P("mp"),
            P("mp", None),
            P(),
            P(),
            P(None, "mp"),
            P("mp"),
            P("mp", None),
            P(),
            P(),
            P(),
            P(),
            P(),
            P(),
            P(),
            P(),
            P(),
        ),
        check_vma=False,
    )
```

```python
import functools
import math
import types

import jax
import jax.numpy as jnp
import numpy as np
from jax import lax
from jax.experimental import pallas as pl
from jax.experimental.pallas import tpu as pltpu
from jax.sharding import PartitionSpec as P

D = 768
BANDS = 16
EMB = 2 * BANDS + 1
FILT = 64
LONG = 1024
BLOCK = 256
BINS = 2 * BLOCK
COUNT = LONG // BLOCK
LANES = 128
WIDE = 3 * LANES
MESH = pl.DeviceIdType.MESH
BF16 = jnp.bfloat16
F32 = jnp.float32
EPS = 1e-05
ROOT = math.sqrt(2.0 / math.pi)
CUBE = 0.044715

PAY_VEC, PAY_PEN, PAY_HID, PAY_EMB, PAY_ROWS = 0, 18, 24, 88, 128
SHARD_DECAY, SHARD_PAR, SHARD_ROWS = 64, 72, 96


def wave_table(shift):
    bins = np.arange(BLOCK)[:, None]
    angle = np.pi * (2 * bins + 1) * (np.arange(BLOCK)[None, :] + shift) / BINS
    return np.concatenate([np.cos(angle), -np.sin(angle)], 0)


NEAR, FAR = wave_table(0), wave_table(-BLOCK)
WAVES = np.concatenate([NEAR, FAR], 1)
UNWAVES = np.concatenate([NEAR.T, FAR.T], 1) / BLOCK


def position_features():
    tau = np.arange(LONG) / LONG
    angles = 2.0 * np.pi * np.arange(1, BANDS + 1)[:, None] * tau[None, :]
    return np.concatenate([tau[None, :], np.cos(angles), np.sin(angles)], 0)


def dot(left, right, dims=((1,), (0,)), precision=None):
    return lax.dot_general(
        left, right, (dims, ((), ())), precision=precision, preferred_element_type=F32
    )


def dot_nt(left, right, precision=None):
    return dot(left, right, ((1,), (1,)), precision)


def dot_tn(left, right, precision=None):
    return dot(left, right, ((0,), (0,)), precision)


HIGH = lax.Precision.HIGHEST


def sin_cos(angle):
    turns = jnp.floor(angle * (2.0 / math.pi) + 0.5)
    rest = angle - turns * 1.5703125
    rest = rest - turns * 4.837512969970703125e-4
    rest = rest - turns * 7.54978995489188e-8
    square = rest * rest
    sine = rest + rest * square * (
        -1.6666654611e-1 + square * (8.3321608736e-3 + square * -1.9515295891e-4)
    )
    cosine = (
        1.0
        - 0.5 * square
        + square
        * square
        * (4.166664568298827e-2 + square * (-1.388731625493765e-3 + square * 2.443315711809948e-5))
    )
    half = jnp.floor(turns * 0.5)
    odd = turns - 2.0 * half
    sign = 1.0 - 2.0 * (half - 2.0 * jnp.floor(half * 0.5))
    swapped = odd > 0.5
    return (
        jnp.where(swapped, cosine, sine) * sign,
        jnp.where(swapped, -sine, cosine) * sign,
    )


def norm_parts(values):
    center = values - jnp.mean(values, axis=-1, keepdims=True)
    scale = lax.rsqrt(jnp.mean(center * center, axis=-1, keepdims=True) + EPS)
    return center * scale, scale


def norm_back(grad, gain, unit, scale):
    inner = grad * gain
    return scale * (
        inner
        - jnp.mean(inner, axis=-1, keepdims=True)
        - unit * jnp.mean(inner * unit, axis=-1, keepdims=True)
    )


def column(row):
    size = row.shape[1]
    same = lax.broadcasted_iota(jnp.int32, (size, size), 0) == lax.broadcasted_iota(
        jnp.int32, (size, size), 1
    )
    return jnp.sum(jnp.where(same, row, 0.0), axis=1, keepdims=True)


def fused(s, names, *refs):
    r = types.SimpleNamespace(**dict(zip(names, refs)))
    ranks, halves, inner, rows = s.ranks, s.halves, s.inner, s.rows
    channels, hidden = s.channels, s.hidden
    dp, mp = lax.axis_index("dp"), lax.axis_index("mp")
    y, c = dp // 2, dp % 2
    q, j = mp // halves, mp % halves
    other, across = 1 - c, 1 - q
    outer = halves // inner

    def device(yy, cc, qq, jj):
        return (yy * 2 + cc, qq * halves + jj)

    def ahead(k):
        return ((j // inner + k // inner) % outer) * inner + (j % inner + k % inner) % inner

    def behind(k):
        return ((j // inner + outer - k // inner) % outer) * inner + (
            j % inner + inner - k % inner
        ) % inner

    sibling = device(y, other, q, j)
    partner = device(y, other, across, j)
    moved = c != q

    def remote(src, dst, send, recv, target):
        return pltpu.make_async_remote_copy(
            src_ref=src,
            dst_ref=dst,
            send_sem=send,
            recv_sem=recv,
            device_id=target,
            device_id_type=MESH,
        )

    def block_rows(cc, jj):
        return pl.ds(pl.multiple_of((cc * halves + jj) * rows, rows), rows)

    mine = block_rows(c, j)

    barrier = pltpu.get_barrier_semaphore()
    greeted = [sibling, partner]
    for k in range(1, halves):
        greeted += [device(y, c, q, ahead(k)), device(y, other, q, ahead(k))]
    for dy in range(ranks):
        for dq in range(2):
            if dy or dq:
                greeted.append(device((y + dy) % ranks, c, (q + dq) % 2, j))
    for target in greeted:
        pl.semaphore_signal(barrier, inc=1, device_id=target, device_id_type=MESH)

    par = r.par_own
    par[...] = jnp.zeros_like(par)
    par[0:1, 0 : 3 * channels] = r.in_bias[...]
    par[1:4, 0 : 3 * channels] = r.short_taps[...]
    par[4:5, 0:channels] = r.skip_gain[...]
    par[5:6, 0:hidden] = r.up_bias[...].astype(F32)

    pl.semaphore_wait(barrier, len(greeted))

    takes = [
        (r.x_any, r.x_in),
        (par, r.par_in),
        (r.win_any, r.win),
        (r.og_any, r.og_in),
        (r.wout_any, r.wout.at[pl.ds(0, channels)]),
        (r.wup_any, r.wup),
        (r.wdn_any, r.wdn),
    ]

    def take(i):
        src, dst = takes[i]
        return remote(src, dst, r.take_send.at[i], r.take_recv.at[i], partner)

    def take_local(i):
        src, dst = takes[i]
        return pltpu.make_async_copy(src, dst, r.take_local.at[i])

    @pl.when(moved)
    def _():
        for i in range(len(takes)):
            take(i).start()

    @pl.when(jnp.logical_not(moved))
    def _():
        for i in range(len(takes)):
            take_local(i).start()

    def taken(*which):
        @pl.when(moved)
        def _():
            for i in which:
                take(i).wait_recv()

        @pl.when(jnp.logical_not(moved))
        def _():
            for i in which:
                take_local(i).wait()

    pack = y * 2 + q
    segments = []
    for i in range(COUNT):
        found = jnp.int32(-1)
        for k in range(s.sequences):
            start = r.offsets[k]
            hit = (
                (r.owners[k] == pack)
                & (start <= i * BLOCK)
                & (start + r.lengths[k] > i * BLOCK)
            )
            found = jnp.where(hit, jnp.int32(k), found)
        segments.append(found)
    valid = [jnp.where(seg >= 0, jnp.float32(1), jnp.float32(0)) for seg in segments]
    joined = [
        [valid[i] * jnp.where(segments[i] == segments[p], jnp.float32(1), jnp.float32(0)) for p in range(i + 1)]
        for i in range(COUNT)
    ]
    follows = [jnp.float32(0)] + [joined[i][i - 1] for i in range(1, COUNT)]

    row_index = lax.broadcasted_iota(jnp.int32, (3 * channels, WIDE), 0)
    lane_index = lax.broadcasted_iota(jnp.int32, (3 * channels, WIDE), 1)
    within = lane_index % LANES
    order = jnp.where(
        (row_index == 3 * within + lane_index // LANES) & (within < channels), 1.0, 0.0
    )
    r.order[...] = order.astype(BF16)
    r.order_wide[...] = order

    features = r.features[...]
    embed_freq, embed_bias = column(r.embed_freq[...]), column(r.embed_bias[...])
    hidden_freq, hidden_bias = column(r.hidden_freq[...]), column(r.hidden_bias[...])
    first_sum = dot_tn(r.embed_weight[...], features, HIGH) + embed_bias
    first, first_cos = sin_cos(embed_freq * first_sum)
    r.first_sum[...] = first_sum
    r.first[...] = first
    r.first_cos[...] = first_cos
    second_sum = dot_tn(r.hidden_weight[...], first, HIGH) + hidden_bias
    second, second_cos = sin_cos(hidden_freq * second_sum)
    r.second_sum[...] = second_sum
    r.second[...] = second
    r.second_cos[...] = second_cos
    shard = c * halves + j
    pick_row = lax.broadcasted_iota(jnp.int32, (D, LANES), 0)
    pick_lane = lax.broadcasted_iota(jnp.int32, (D, LANES), 1)
    pick = jnp.where((pick_row == shard * channels + pick_lane) & (pick_lane < channels), 1.0, 0.0)
    own_filter = dot(r.filter_weight[...], pick, precision=HIGH)
    own_decay = dot(jnp.broadcast_to(r.decay_rate[...], (8, D)), pick, precision=HIGH)[0:1]
    r.own_filter[...] = own_filter
    r.own_decay[...] = jnp.broadcast_to(own_decay, (8, LANES))
    r.spread[...] = jnp.zeros_like(r.spread)
    for i in range(COUNT):
        at = slice(i * BLOCK, (i + 1) * BLOCK)
        tau = (
            lax.broadcasted_iota(jnp.int32, (BLOCK, LANES), 0) + i * BLOCK
        ).astype(F32) * (1.0 / LONG)
        kernel = dot_tn(second[:, at], own_filter, HIGH) * jnp.exp(-tau * own_decay)
        r.kernel[at, :] = kernel
        low = kernel.astype(BF16)
        r.spread[0:BLOCK, i * LANES : (i + 1) * LANES] = low
        if i + 1 < COUNT:
            r.spread[BLOCK:BINS, (i + 1) * LANES : (i + 2) * LANES] = low
    r.kernel_wave[...] = dot(r.waves[...], r.spread[...])

    def gather_copies(n, held):
        out = []
        for k in range(1, halves):
            out.append(
                remote(
                    held.at[mine],
                    held.at[mine],
                    r.gather_send.at[n, k],
                    r.gather_recv.at[n, k],
                    device(y, c, q, ahead(k)),
                )
            )
        out.append(
            remote(
                held.at[mine],
                held.at[mine],
                r.gather_send.at[n, 0],
                r.gather_recv.at[n, 0],
                sibling,
            )
        )
        return out

    def gather_start(n, held):
        for copy in gather_copies(n, held):
            copy.start()

    def gather_finish(n, held):
        forwards = []
        for k in range(1, halves):
            came = held.at[block_rows(c, behind(k))]
            remote(
                came,
                came,
                r.gather_send.at[n, k],
                r.gather_recv.at[n, k],
                device(y, c, q, behind(k)),
            ).wait_recv()
            forward = remote(
                came, came, r.pass_send.at[n, k], r.pass_recv.at[n, k], sibling
            )
            forward.start()
            forwards.append(forward)
        for k in range(halves):
            came = held.at[block_rows(other, behind(k))]
            recv = r.pass_recv.at[n, k] if k else r.gather_recv.at[n, 0]
            remote(came, came, r.pass_send.at[n, k], recv, sibling).wait_recv()
        for copy in gather_copies(n, held) + forwards:
            copy.wait_send()

    def chip_copy(n, k):
        return remote(
            r.chip_out.at[n, k],
            r.chip_in.at[n, k],
            r.chip_send.at[n, k],
            r.chip_recv.at[n, k],
            sibling,
        )

    def link_copy(n, k):
        return remote(
            r.link_out.at[n, k],
            r.link_in.at[n, k],
            r.link_send.at[n, k],
            r.link_recv.at[n, k],
            device(y, c, q, ahead(k)),
        )

    def chip_give(n, k, value):
        r.chip_out[n, k] = value.astype(BF16)
        chip_copy(n, k).start()

    def chip_add(n, k, value):
        chip_copy(n, k).wait_recv()
        return value + r.chip_in[n, k].astype(F32)

    def scatter(n, part):
        def give(i, carry):
            k = (i + 1) % halves
            chip_give(n, k, part(block_rows(other, ahead(k))))
            return carry

        lax.fori_loop(0, halves, give, 0)

        def send(k, carry):
            r.link_out[n, k] = chip_add(n, k, part(block_rows(c, ahead(k)))).astype(BF16)
            link_copy(n, k).start()
            return carry

        lax.fori_loop(1, halves, send, 0)
        r.own_sum[n] = chip_add(n, 0, part(mine))

    def scatter_finish(n):
        total = r.own_sum[n]
        for k in range(1, halves):
            link_copy(n, k).wait_recv()
            total = total + r.link_in[n, k].astype(F32)
        for k in range(halves):
            chip_copy(n, k).wait_send()
            if k:
                link_copy(n, k).wait_send()
        return total

    taken(0)
    unit, _ = norm_parts(r.x_in[...].astype(F32))
    r.g_one[mine, :] = (unit * r.mixer_gain[...]).astype(BF16)
    gather_start(0, r.g_one)
    taken(1, 2)
    par_wide = dot(par_in_rows(r.par_in, channels), r.order_wide[...], precision=HIGH)
    r.taps[...] = par_wide
    for i in range(3):
        at = slice(i * BLOCK, (i + 1) * BLOCK)
        r.win_apart[at, :] = dot(r.win[at, :], r.order[...]).astype(BF16)
    r.wout[channels:, :] = jnp.zeros_like(r.wout[channels:, :])
    gather_finish(0, r.g_one)

    taken(3)
    r.g_out[mine, :] = r.og_in[...]
    gather_start(1, r.g_out)

    def project(i, carry):
        at = pl.ds(pl.multiple_of(i * LANES, LANES), LANES)
        r.projected[at, :] = dot(r.g_one[at, :], r.win_apart[...]) + r.taps[0:1, :]
        return carry

    lax.fori_loop(0, LONG // LANES, project, 0)

    rows_here = lax.broadcasted_iota(jnp.int32, (BLOCK, 1), 0)

    def back_rows(i):
        now = r.projected[i * BLOCK : (i + 1) * BLOCK, :]
        one, two = pltpu.roll(now, 1, 0), pltpu.roll(now, 2, 0)
        if i:
            edge = r.projected[i * BLOCK - 8 : i * BLOCK, :] * follows[i]
            last, before = edge[7:8], edge[6:7]
        else:
            last = before = jnp.zeros((1, WIDE), F32)
        one = jnp.where(rows_here == 0, last, one)
        two = jnp.where(rows_here == 0, before, jnp.where(rows_here == 1, last, two))
        return now, one, two

    for i in range(COUNT):
        now, one, two = back_rows(i)
        short = r.taps[1:2, :] * now + r.taps[2:3, :] * one + r.taps[3:4, :] * two
        r.short[i * BLOCK : (i + 1) * BLOCK, :] = short
        signal = short[:, 2 * LANES :] * short[:, LANES : 2 * LANES] * valid[i]
        r.signal[:, i * LANES : (i + 1) * LANES] = signal.astype(BF16)

    near = r.waves[:, 0:BLOCK]
    unnear = r.unwaves[:, 0:BINS]
    r.signal_wave[...] = dot(near, r.signal[...])
    step = 16

    def load_wave(ref, at, count=COUNT):
        low, high = pl.ds(at, step), pl.ds(at + BLOCK, step)
        return [
            (ref[low, i * LANES : (i + 1) * LANES], ref[high, i * LANES : (i + 1) * LANES])
            for i in range(count)
        ]

    def store_wave(ref, base, at, i, pair):
        ref[pl.ds(base + at, step), i * LANES : (i + 1) * LANES] = pair[0].astype(BF16)
        ref[pl.ds(base + at + BLOCK, step), i * LANES : (i + 1) * LANES] = pair[1].astype(BF16)

    def weighted(terms):
        real = imag = None
        for weight, (a, b) in terms:
            real = a * weight if real is None else real + a * weight
            imag = b * weight if imag is None else imag + b * weight
        return real, imag

    def times(left, right):
        return left[0] * right[0] - left[1] * right[1], left[0] * right[1] + left[1] * right[0]

    def times_conj(left, right):
        return left[0] * right[0] + left[1] * right[1], left[0] * right[1] - left[1] * right[0]

    def forward_wave(n, carry):
        at = pl.multiple_of(n * step, step)
        kernels, signals = load_wave(r.kernel_wave, at), load_wave(r.signal_wave, at)
        for i in range(COUNT):
            store_wave(
                r.product,
                0,
                at,
                i,
                weighted([(joined[i][p], times(kernels[i - p], signals[p])) for p in range(i + 1)]),
            )
        return carry

    lax.fori_loop(0, BLOCK // step, forward_wave, 0)
    skip = r.par_in[4:5, 0:LANES]
    convolved = dot(unnear, r.product[0:BINS, :])
    for i in range(COUNT):
        at = slice(i * BLOCK, (i + 1) * BLOCK)
        lanes = slice(i * LANES, (i + 1) * LANES)
        direct = convolved[:, lanes] + skip * r.signal[:, lanes].astype(F32)
        r.direct[at, :] = direct
        r.mixed[at, :] = (direct * r.short[at, 0:LANES]).astype(BF16)

    taken(4)
    scatter(0, lambda at: dot(r.mixed[at, :], r.wout[...]))
    gather_finish(1, r.g_out)
    middle = r.x_in[...].astype(F32) + r.out_bias[...] + scatter_finish(0)
    r.middle[...] = middle
    unit, _ = norm_parts(middle)
    r.g_two[mine, :] = (unit * r.ffn_gain[...]).astype(BF16)
    gather_start(2, r.g_two)
    taken(5, 6)
    gather_finish(2, r.g_two)

    def feed(at):
        value = dot(r.g_two[at, :], r.wup[...]) + r.par_in[5:6, 0:hidden]
        square = value * value
        bend = jnp.tanh(ROOT * value * (1.0 + CUBE * square))
        half = 0.5 * (1.0 + bend)
        active = (value * half).astype(BF16)
        slope = half + 0.5 * value * (1.0 - bend * bend) * (ROOT * (1.0 + 3.0 * CUBE * square))
        grad = (slope * dot_nt(r.g_out[at, :], r.wdn[...])).astype(BF16)
        r.active[at, :] = active
        r.hidden_grad[at, :] = grad
        return dot_nt(grad, r.wup[...]), dot(active, r.wdn[...])

    def feed_give(i, carry):
        k = (i + 1) % halves
        back, forth = feed(block_rows(other, ahead(k)))
        chip_give(1, k, back)
        chip_give(2, k, forth)
        return carry

    lax.fori_loop(0, halves, feed_give, 0)

    def feed_send(k, carry):
        back, forth = feed(block_rows(c, ahead(k)))
        r.link_out[1, k] = chip_add(1, k, back).astype(BF16)
        link_copy(1, k).start()
        r.link_out[2, k] = chip_add(2, k, forth).astype(BF16)
        return carry

    lax.fori_loop(1, halves, feed_send, 0)
    back, forth = feed(mine)
    r.own_sum[1] = chip_add(1, 0, back)
    r.own_sum[2] = chip_add(2, 0, forth)

    sums = [
        (r.grad_in, r.part_in, r.y_in, r.z_in, r.gwin),
        (r.grad_out, r.part_out, r.y_out, r.z_out, r.gwout),
        (r.grad_up, r.part_up, r.y_up, r.z_up, r.gwup),
        (r.grad_dn, r.part_dn, r.y_dn, r.z_dn, r.gwdn),
    ]
    owner = jnp.logical_not(moved)

    def part_rows(ref, yy):
        size = ref.shape[0] // ranks
        return pl.ds(pl.multiple_of(yy * size, 16), size)

    def y_copy(w, dy):
        full, _, came, _, _ = sums[w]
        to = (y + dy) % ranks
        return remote(
            full.at[part_rows(full, to)],
            came.at[dy],
            r.y_send.at[w, dy],
            r.y_recv.at[w, dy],
            device(to, c, q, j),
        )

    def z_copy(w):
        _, part, _, came, _ = sums[w]
        return remote(
            part, came, r.z_send.at[w], r.z_recv.at[w], device(y, c, across, j)
        )

    def out_copy(w, dy):
        final = sums[w][4]
        at = part_rows(final, y)
        return remote(
            final.at[at],
            final.at[at],
            r.out_send.at[w, dy],
            r.out_recv.at[w, dy],
            device((y + dy) % ranks, c, q, j),
        )

    def chip_final(w, dy):
        final = sums[w][4]
        at = part_rows(final, (y + ranks - dy) % ranks)
        return remote(
            final.at[at],
            final.at[at],
            r.fin_send.at[w, dy],
            r.fin_recv.at[w, dy],
            sibling,
        )

    def sum_start(w):
        for dy in range(1, ranks):
            y_copy(w, dy).start()

    def sum_cross(w):
        full, part, came, _, _ = sums[w]
        total = full[part_rows(full, y), :].astype(F32)
        for dy in range(1, ranks):
            y_copy(w, dy).wait_recv()
            total = total + came[dy].astype(F32)
        part[...] = total.astype(BF16)

        @pl.when(moved)
        def _():
            z_copy(w).start()

    def sum_close(w):
        _, part, _, came, final = sums[w]

        @pl.when(owner)
        def _():
            z_copy(w).wait_recv()
            final[part_rows(final, y), :] = (
                part[...].astype(F32) + came[...].astype(F32)
            ).astype(BF16)
            for dy in range(1, ranks):
                out_copy(w, dy).start()
            chip_final(w, 0).start()

    def sum_finish(w):
        final = sums[w][4]

        @pl.when(owner)
        def _():
            for dy in range(1, ranks):
                at = part_rows(final, (y + ranks - dy) % ranks)
                remote(
                    final.at[at],
                    final.at[at],
                    r.out_send.at[w, dy],
                    r.out_recv.at[w, dy],
                    sibling,
                ).wait_recv()
                chip_final(w, dy).start()
            for dy in range(1, ranks):
                out_copy(w, dy).wait_send()
            for dy in range(ranks):
                chip_final(w, dy).wait_send()

        @pl.when(moved)
        def _():
            for dy in range(ranks):
                chip_final(w, dy).wait_recv()
            z_copy(w).wait_send()

        for dy in range(1, ranks):
            y_copy(w, dy).wait_send()

    def weight_grad(target, left, right, by_right=False):
        def chunk(i, carry):
            at = pl.ds(pl.multiple_of(i * BLOCK, BLOCK), BLOCK)
            if by_right:
                target[0 : left.shape[1], at] = dot_tn(left[...], right[:, at]).astype(BF16)
            else:
                target[at, :] = dot_tn(left[:, at], right[...]).astype(BF16)
            return carry

        lax.fori_loop(0, D // BLOCK, chunk, 0)

    if r.grad_dn.shape[0] > hidden:
        r.grad_dn[hidden:, :] = jnp.zeros_like(r.grad_dn[hidden:, :])
    weight_grad(r.grad_dn, r.active, r.g_out, True)
    sum_start(3)
    weight_grad(r.grad_up, r.g_two, r.hidden_grad)
    sum_start(2)

    ffn_back = scatter_finish(1)
    seed = r.og_in[...].astype(F32)
    unit, scale = norm_parts(r.middle[...])
    middle_grad = seed + norm_back(ffn_back, r.ffn_gain[...], unit, scale)
    r.middle_grad[...] = middle_grad
    branch_grad = middle_grad.astype(BF16)
    r.g_back[mine, :] = branch_grad
    gather_start(3, r.g_back)
    vectors = [
        jnp.sum(ffn_back * unit, axis=0, keepdims=True),
        jnp.sum(branch_grad.astype(F32), axis=0, keepdims=True),
        jnp.sum(seed, axis=0, keepdims=True),
    ]
    r.pay[...] = jnp.zeros_like(r.pay)
    for v, vector in enumerate(vectors):
        for k in range(D // LANES):
            at = PAY_VEC + v * (D // LANES) + k
            r.pay[at : at + 1, :] = vector[:, k * LANES : (k + 1) * LANES]
    par_grad = r.par_grad
    par_grad[...] = jnp.zeros_like(par_grad)
    par_grad[5:6, 0:hidden] = jnp.sum(r.hidden_grad[...].astype(F32), axis=0, keepdims=True)
    sum_cross(3)
    sum_cross(2)
    gather_finish(3, r.g_back)
    for k in range(1, halves):
        link_copy(2, k).start()

    skip_total = jnp.zeros((1, LANES), F32)
    for i in range(COUNT):
        at = slice(i * BLOCK, (i + 1) * BLOCK)
        lanes = slice(i * LANES, (i + 1) * LANES)
        mixed_grad = dot_nt(r.g_back[at, :], r.wout[...])
        r.short_grad[at, 0:LANES] = mixed_grad * r.direct[at, :]
        direct_grad = mixed_grad * r.short[at, 0:LANES]
        r.direct[at, :] = direct_grad
        r.direct_low[:, lanes] = direct_grad.astype(BF16)
        skip_total += jnp.sum(
            direct_grad * r.signal[:, lanes].astype(F32), axis=0, keepdims=True
        )
    par_grad[4:5, 0:LANES] = skip_total
    r.grad_wave[...] = dot(near, r.direct_low[...])
    r.back_product[...] = jnp.zeros_like(r.back_product)

    def backward_wave(n, carry):
        at = pl.multiple_of(n * step, step)
        kernels, signals = load_wave(r.kernel_wave, at), load_wave(r.signal_wave, at)
        grads = load_wave(r.grad_wave, at)
        for p in range(COUNT):
            terms = [(joined[i][p], times_conj(kernels[i - p], grads[i])) for i in range(p, COUNT)]
            store_wave(r.product, 0, at, p, weighted(terms))
        for d in range(COUNT):
            terms = [
                (joined[i][i - d], times_conj(signals[i - d], grads[i])) for i in range(d, COUNT)
            ]
            pair = weighted(terms)
            store_wave(r.back_product, 0, at, d, pair)
            if d:
                store_wave(r.back_product, BINS, at, d - 1, pair)
        return carry

    lax.fori_loop(0, BLOCK // step, backward_wave, 0)
    signal_grads = dot(unnear, r.product[0:BINS, :])
    for i in range(COUNT):
        at = slice(i * BLOCK, (i + 1) * BLOCK)
        lanes = slice(i * LANES, (i + 1) * LANES)
        signal_grad = (signal_grads[:, lanes] + skip * r.direct[at, :]) * valid[i]
        r.short_grad[at, LANES : 2 * LANES] = signal_grad * r.short[at, 2 * LANES :]
        r.short_grad[at, 2 * LANES :] = signal_grad * r.short[at, LANES : 2 * LANES]

    bias_total = jnp.zeros((1, WIDE), F32)
    tap_totals = [jnp.zeros((1, WIDE), F32) for _ in range(3)]
    for i in range(COUNT):
        at = slice(i * BLOCK, (i + 1) * BLOCK)
        now, one, two = back_rows(i)
        grad = r.short_grad[at, :]
        for t, value in enumerate((now, one, two)):
            tap_totals[t] += jnp.sum(grad * value, axis=0, keepdims=True)
        next_one = pltpu.roll(grad, BLOCK - 1, 0)
        next_two = pltpu.roll(grad, BLOCK - 2, 0)
        if i + 1 < COUNT:
            edge = r.short_grad[(i + 1) * BLOCK : (i + 1) * BLOCK + 8, :] * follows[i + 1]
            head, after = edge[0:1], edge[1:2]
        else:
            head = after = jnp.zeros((1, WIDE), F32)
        next_one = jnp.where(rows_here == BLOCK - 1, head, next_one)
        next_two = jnp.where(
            rows_here == BLOCK - 2, head, jnp.where(rows_here == BLOCK - 1, after, next_two)
        )
        low = (
            r.taps[1:2, :] * grad + r.taps[2:3, :] * next_one + r.taps[3:4, :] * next_two
        ).astype(BF16)
        bias_total += jnp.sum(low.astype(F32), axis=0, keepdims=True)
        r.projected_grad[at, :] = dot_nt(low, r.order[...]).astype(BF16)
    par_grad[0:1, :] = bias_total
    for t in range(3):
        par_grad[t + 1 : t + 2, :] = tap_totals[t]

    scatter(3, lambda at: dot_nt(r.projected_grad[at, :], r.win[...]))

    weight_grad(r.grad_in, r.g_one, r.projected_grad)
    sum_start(0)
    r.grad_out[...] = dot_tn(r.mixed[...], r.g_back[...]).astype(BF16)
    sum_start(1)
    sum_close(3)
    sum_close(2)

    kernel_grads = dot(r.unwaves[...], r.back_product[...])
    decay_total = jnp.zeros((1, LANES), F32)
    penalty = jnp.zeros((1, LANES), F32)
    own_filter = r.own_filter[...]
    own_decay = r.own_decay[0:1, :]
    lead = jnp.where(pack == 0, 1.0 / D, 0.0).astype(F32)
    for i in range(COUNT):
        at = slice(i * BLOCK, (i + 1) * BLOCK)
        tau = (
            lax.broadcasted_iota(jnp.int32, (BLOCK, LANES), 0) + i * BLOCK
        ).astype(F32) * (1.0 / LONG)
        kernel = r.kernel[at, :]
        weighed = tau * kernel
        penalty += jnp.sum(weighed * kernel, axis=0, keepdims=True) * lead
        kernel_grad = (
            kernel_grads[:, i * LANES : (i + 1) * LANES] + weighed * (2.0 * lead)
        )
        decay_total -= jnp.sum(kernel_grad * weighed, axis=0, keepdims=True)
        r.raw_grad[at, :] = kernel_grad * jnp.exp(-tau * own_decay)
    shard_sum = r.shard_sum
    slot = y * 2 + q
    shard_sum[slot] = jnp.zeros((SHARD_ROWS, LANES), F32)
    shard_sum[slot, 0:FILT, :] = dot(r.second[...], r.raw_grad[...], precision=HIGH)
    shard_sum[slot, SHARD_DECAY : SHARD_DECAY + 1, :] = decay_total
    for k in range(3):
        at = SHARD_PAR + 8 * k
        shard_sum[slot, at : at + 8, :] = par_grad[:, k * LANES : (k + 1) * LANES]
    r.pay[PAY_PEN : PAY_PEN + 1, :] = penalty
    second_grad = dot_nt(own_filter, r.raw_grad[...], HIGH)
    angle_grad = second_grad * r.second_cos[...]
    freq_grad = jnp.sum(angle_grad * r.second_sum[...], axis=1, keepdims=True)
    sum_grad = angle_grad * column(r.hidden_freq[...])
    at = slice(PAY_HID, PAY_HID + FILT)
    r.pay[at, 0:FILT] = dot_nt(r.first[...], sum_grad, HIGH)
    r.pay[at, FILT : FILT + 1] = freq_grad
    r.pay[at, FILT + 1 : FILT + 2] = jnp.sum(sum_grad, axis=1, keepdims=True)
    angle_grad = dot(r.hidden_weight[...], sum_grad, precision=HIGH) * r.first_cos[...]
    r.pay[at, FILT + 2 : FILT + 3] = jnp.sum(
        angle_grad * r.first_sum[...], axis=1, keepdims=True
    )
    sum_grad = angle_grad * column(r.embed_freq[...])
    r.pay[at, FILT + 3 : FILT + 4] = jnp.sum(sum_grad, axis=1, keepdims=True)
    r.pay[PAY_EMB : PAY_EMB + EMB, 0:FILT] = dot_nt(features, sum_grad, HIGH)

    def pay_chip(n, src, dst):
        return remote(src, dst, r.pay_send.at[n, 0], r.pay_recv.at[n, 0], sibling)

    def pay_links(n, held):
        return [
            remote(
                held.at[j],
                held.at[j],
                r.pay_send.at[n, k],
                r.pay_recv.at[n, k],
                device(y, c, q, ahead(k)),
            )
            for k in range(1, halves)
        ]

    def pay_packs(n, held):
        out = []
        for dy in range(ranks):
            for dq in range(2):
                if dy or dq:
                    out.append(
                        remote(
                            held.at[slot],
                            held.at[slot],
                            r.cross_send.at[n, dy * 2 + dq],
                            r.cross_recv.at[n, dy * 2 + dq],
                            device((y + dy) % ranks, c, (q + dq) % 2, j),
                        )
                    )
        return out

    def pay_packs_wait(n, held):
        total = None
        for dy in range(ranks):
            for dq in range(2):
                if dy or dq:
                    yy, qq = (y + ranks - dy) % ranks, (q + dq) % 2
                    came = held.at[yy * 2 + qq]
                    remote(
                        came,
                        came,
                        r.cross_send.at[n, dy * 2 + dq],
                        r.cross_recv.at[n, dy * 2 + dq],
                        device(yy, c, qq, j),
                    ).wait_recv()
        for i in range(2 * ranks):
            total = held[i] if total is None else total + held[i]
        return total

    def pay_group(n, own, chip_in, held):
        first_copy = pay_chip(n, own, chip_in)
        first_copy.wait_recv()
        held[j] = own[...] + chip_in[...]
        for copy in pay_links(n, held):
            copy.start()

    def pay_group_wait(n, held):
        for k in range(1, halves):
            came = held.at[behind(k)]
            remote(
                came,
                came,
                r.pay_send.at[n, k],
                r.pay_recv.at[n, k],
                device(y, c, q, behind(k)),
            ).wait_recv()
        total = held[0]
        for i in range(1, halves):
            total = total + held[i]
        return total

    for copy in pay_packs(2, shard_sum):
        copy.start()
    pay_chip(0, r.pay, r.pay_in).start()
    sum_cross(0)
    sum_cross(1)
    pay_group(0, r.pay, r.pay_in, r.pay_held)

    mixer_back = scatter_finish(3)
    unit, scale = norm_parts(r.x_in[...].astype(F32))
    r.input_grad[...] = r.middle_grad[...] + norm_back(
        mixer_back, r.mixer_gain[...], unit, scale
    )
    r.block_out[...] = (
        r.middle[...] + r.down_bias[...] + scatter_finish(2)
    ).astype(BF16)
    gives = [(r.input_grad, r.input_any), (r.block_out, r.block_any)]

    def give(i):
        src, dst = gives[i]
        return remote(src, dst, r.give_send.at[i], r.give_recv.at[i], partner)

    def give_local(i):
        src, dst = gives[i]
        return pltpu.make_async_copy(src, dst, r.give_local.at[i])

    @pl.when(moved)
    def _():
        for i in range(len(gives)):
            give(i).start()

    @pl.when(owner)
    def _():
        for i in range(len(gives)):
            give_local(i).start()

    gain_row = jnp.sum(mixer_back * unit, axis=0, keepdims=True)
    r.late[...] = jnp.zeros_like(r.late)
    for k in range(D // LANES):
        r.late[k : k + 1, :] = gain_row[:, k * LANES : (k + 1) * LANES]
    pay_chip(1, r.late, r.late_in).start()
    sum_close(0)
    sum_close(1)
    r.pay_cross[slot] = pay_group_wait(0, r.pay_held)
    for copy in pay_packs(0, r.pay_cross):
        copy.start()
    pay_group(1, r.late, r.late_in, r.late_held)

    r.shards[shard] = pay_packs_wait(2, shard_sum)

    def shard_copies():
        held = r.shards
        out = [
            remote(
                held.at[shard],
                held.at[shard],
                r.gather_send.at[4, k],
                r.gather_recv.at[4, k],
                device(y, c, q, ahead(k)) if k else sibling,
            )
            for k in range(halves)
        ]
        return out

    for copy in shard_copies():
        copy.start()
    r.late_cross[slot] = pay_group_wait(1, r.late_held)
    for copy in pay_packs(1, r.late_cross):
        copy.start()
    forwards = []
    for k in range(1, halves):
        came = r.shards.at[c * halves + behind(k)]
        remote(
            came,
            came,
            r.gather_send.at[4, k],
            r.gather_recv.at[4, k],
            device(y, c, q, behind(k)),
        ).wait_recv()
        forward = remote(came, came, r.pass_send.at[4, k], r.pass_recv.at[4, k], sibling)
        forward.start()
        forwards.append(forward)
    for k in range(halves):
        came = r.shards.at[other * halves + behind(k)]
        recv = r.pass_recv.at[4, k] if k else r.gather_recv.at[4, 0]
        remote(came, came, r.pass_send.at[4, k], recv, sibling).wait_recv()
    r.pay_total[...] = pay_packs_wait(0, r.pay_cross)
    home = r.shards[q * halves + j]
    wide = jnp.concatenate(
        [home[SHARD_PAR + 8 * k : SHARD_PAR + 8 * k + 8] for k in range(3)], axis=1
    )
    r.par_wide[...] = wide
    r.par_close[...] = dot_nt(wide, r.order_wide[...], HIGH)
    r.late_total[...] = pay_packs_wait(1, r.late_cross)
    for w in (3, 2, 1, 0):
        sum_finish(w)

    for copy in shard_copies() + forwards:
        copy.wait_send()
    for n, own, chip_in, held, cross in (
        (0, r.pay, r.pay_in, r.pay_held, r.pay_cross),
        (1, r.late, r.late_in, r.late_held, r.late_cross),
    ):
        pay_chip(n, own, chip_in).wait_send()
        for copy in pay_links(n, held) + pay_packs(n, cross):
            copy.wait_send()
    for copy in pay_packs(2, shard_sum):
        copy.wait_send()

    @pl.when(moved)
    def _():
        for i in range(len(takes)):
            take(i).wait_send()
        for i in range(len(gives)):
            give(i).wait()

    @pl.when(owner)
    def _():
        for i in range(len(gives)):
            give_local(i).wait()


def par_in_rows(ref, channels):
    return ref[:, 0 : 3 * channels]


def round_up(value, unit):
    return (value + unit - 1) // unit * unit


def solution(mesh):
    n_dp, n_mp = mesh.shape["dp"], mesh.shape["mp"]

    def per_device(
        block_input,
        mixer_gain,
        in_weight,
        in_bias,
        short_taps,
        skip_gain,
        out_weight,
        out_bias,
        ffn_gain,
        up_weight,
        up_bias,
        down_weight,
        down_bias,
        embed_weight,
        embed_bias,
        embed_freq,
        hidden_weight,
        hidden_bias,
        hidden_freq,
        filter_weight,
        decay_rate,
        out_grad,
        sequence_lengths,
        sequence_rank,
        sequence_offset,
    ):
        ranks, halves = n_dp // 2, n_mp // 2
        rows = block_input.shape[0]
        channels, hidden = skip_gain.shape[0], up_weight.shape[1]
        sizes = types.SimpleNamespace(
            ranks=ranks,
            halves=halves,
            inner=n_mp // 4,
            rows=rows,
            channels=channels,
            hidden=hidden,
            sequences=sequence_lengths.shape[0],
        )
        down_rows = round_up(hidden, 16 * ranks)
        group = 2 * halves
        anywhere = pl.BlockSpec(memory_space=pl.ANY)
        vector = pl.BlockSpec(memory_space=pltpu.VMEM)
        scalar = pl.BlockSpec(memory_space=pltpu.SMEM)
        row = lambda value: value.reshape(1, -1)
        inputs = [
            ("x_any", block_input, anywhere),
            ("og_any", out_grad, anywhere),
            ("win_any", in_weight, anywhere),
            ("wout_any", out_weight, anywhere),
            ("wup_any", up_weight, anywhere),
            ("wdn_any", down_weight, anywhere),
            ("mixer_gain", row(mixer_gain), vector),
            ("ffn_gain", row(ffn_gain), vector),
            ("out_bias", row(out_bias), vector),
            ("down_bias", row(down_bias), vector),
            ("in_bias", row(in_bias), vector),
            ("short_taps", short_taps, vector),
            ("skip_gain", row(skip_gain), vector),
            ("up_bias", row(up_bias), vector),
            ("embed_weight", embed_weight, vector),
            ("embed_bias", row(embed_bias), vector),
            ("embed_freq", row(embed_freq), vector),
            ("hidden_weight", hidden_weight, vector),
            ("hidden_bias", row(hidden_bias), vector),
            ("hidden_freq", row(hidden_freq), vector),
            ("filter_weight", filter_weight, vector),
            ("decay_rate", row(decay_rate), vector),
            ("waves", jnp.asarray(WAVES, BF16), vector),
            ("unwaves", jnp.asarray(UNWAVES, BF16), vector),
            ("features", jnp.asarray(position_features(), F32), vector),
            ("lengths", sequence_lengths, scalar),
            ("owners", sequence_rank, scalar),
            ("offsets", sequence_offset, scalar),
        ]
        outputs = [
            ("block_any", (rows, D), BF16, anywhere),
            ("input_any", (rows, D), F32, anywhere),
            ("gwin", (D, 3 * channels), BF16, vector),
            ("gwout", (LANES, D), BF16, vector),
            ("gwup", (D, hidden), BF16, vector),
            ("gwdn", (down_rows, D), BF16, vector),
            ("pay_total", (PAY_ROWS, LANES), F32, vector),
            ("late_total", (8, LANES), F32, vector),
            ("shards", (group, SHARD_ROWS, LANES), F32, vector),
            ("par_wide", (8, WIDE), F32, vector),
            ("par_close", (8, 3 * channels), F32, vector),
        ]
        dma = pltpu.SemaphoreType.DMA
        scratch = {}

        def hold(name, shape, dtype=F32):
            scratch[name] = pltpu.VMEM(shape, dtype)

        hold("x_in", (rows, D), BF16)
        hold("og_in", (rows, D), BF16)
        hold("par_own", (8, WIDE))
        hold("par_in", (8, WIDE))
        hold("par_grad", (8, WIDE))
        hold("taps", (8, WIDE))
        hold("win", (D, 3 * channels), BF16)
        hold("win_apart", (D, WIDE), BF16)
        hold("wout", (LANES, D), BF16)
        hold("wup", (D, hidden), BF16)
        hold("wdn", (hidden, D), BF16)
        hold("order", (3 * channels, WIDE), BF16)
        hold("order_wide", (3 * channels, WIDE))
        for name in ("first", "first_sum", "first_cos", "second", "second_sum", "second_cos"):
            hold(name, (FILT, LONG))
        hold("own_filter", (FILT, LANES))
        hold("own_decay", (8, LANES))
        hold("kernel", (LONG, LANES))
        hold("raw_grad", (LONG, LANES))
        hold("spread", (BINS, COUNT * LANES), BF16)
        for name in ("kernel_wave", "signal_wave", "grad_wave"):
            hold(name, (BINS, COUNT * LANES))
        hold("product", (BINS, COUNT * LANES), BF16)
        hold("back_product", (2 * BINS, COUNT * LANES), BF16)
        for name in ("g_one", "g_out", "g_two", "g_back"):
            hold(name, (LONG, D), BF16)
        for name in ("projected", "short", "short_grad"):
            hold(name, (LONG, WIDE))
        hold("signal", (BLOCK, COUNT * LANES), BF16)
        hold("direct_low", (BLOCK, COUNT * LANES), BF16)
        hold("direct", (LONG, LANES))
        hold("mixed", (LONG, LANES), BF16)
        hold("middle", (rows, D))
        hold("middle_grad", (rows, D))
        hold("input_grad", (rows, D))
        hold("block_out", (rows, D), BF16)
        hold("active", (LONG, hidden), BF16)
        hold("hidden_grad", (LONG, hidden), BF16)
        hold("projected_grad", (LONG, 3 * channels), BF16)
        for name in ("chip_out", "chip_in", "link_out", "link_in"):
            hold(name, (4, halves, rows, D), BF16)
        hold("own_sum", (4, rows, D))
        for name, full in (
            ("in", (D, 3 * channels)),
            ("out", (LANES, D)),
            ("up", (D, hidden)),
            ("dn", (down_rows, D)),
        ):
            part = (full[0] // ranks, full[1])
            hold("grad_" + name, full, BF16)
            hold("part_" + name, part, BF16)
            hold("y_" + name, (ranks,) + part, BF16)
            hold("z_" + name, part, BF16)
        hold("pay", (PAY_ROWS, LANES))
        hold("pay_in", (PAY_ROWS, LANES))
        hold("pay_held", (halves, PAY_ROWS, LANES))
        hold("pay_cross", (2 * ranks, PAY_ROWS, LANES))
        hold("late", (8, LANES))
        hold("late_in", (8, LANES))
        hold("late_held", (halves, 8, LANES))
        hold("late_cross", (2 * ranks, 8, LANES))
        hold("shard_sum", (2 * ranks, SHARD_ROWS, LANES))
        for name, shape in (
            ("take", (7,)),
            ("give", (2,)),
            ("gather", (5, halves)),
            ("pass", (5, halves)),
            ("chip", (4, halves)),
            ("link", (4, halves)),
            ("y", (4, ranks)),
            ("z", (4,)),
            ("out", (4, ranks)),
            ("fin", (4, ranks)),
            ("pay", (2, halves)),
            ("cross", (3, 2 * ranks)),
        ):
            scratch[name + "_send"] = dma(shape)
            scratch[name + "_recv"] = dma(shape)
        scratch["take_local"] = dma((7,))
        scratch["give_local"] = dma((2,))
        names = [i[0] for i in inputs] + [o[0] for o in outputs] + list(scratch)
        results = pl.pallas_call(
            functools.partial(fused, sizes, names),
            out_shape=[jax.ShapeDtypeStruct(o[1], o[2]) for o in outputs],
            in_specs=[i[2] for i in inputs],
            out_specs=[o[3] for o in outputs],
            scratch_shapes=list(scratch.values()),
            compiler_params=pltpu.CompilerParams(
                collective_id=0,
                has_side_effects=True,
                vmem_limit_bytes=60 * 2**20,
            ),
            name="block",
        )(*[i[1] for i in inputs])
        out = dict(zip([o[0] for o in outputs], results))
        pay, shards = out["pay_total"], out["shards"]
        lines = D // LANES

        def shared(at):
            return pay[at : at + lines].reshape(D)

        def vector_of(k):
            return pay[PAY_HID : PAY_HID + FILT, FILT + k]

        return (
            out["block_any"],
            out["input_any"],
            jnp.sum(pay[PAY_PEN]),
            out["late_total"][0:lines].reshape(D),
            out["gwin"].astype(F32),
            out["par_close"][0],
            out["par_close"][1:4],
            out["par_wide"][4, 0:channels],
            out["gwout"][0:channels].astype(F32),
            shared(PAY_VEC + lines),
            shared(PAY_VEC),
            out["gwup"].astype(F32),
            out["par_wide"][5, 0:hidden],
            out["gwdn"][0:hidden].astype(F32),
            shared(PAY_VEC + 2 * lines),
            pay[PAY_EMB : PAY_EMB + EMB, 0:FILT],
            vector_of(3),
            vector_of(2),
            pay[PAY_HID : PAY_HID + FILT, 0:FILT],
            vector_of(1),
            vector_of(0),
            shards[:, 0:FILT, 0:channels].transpose(1, 0, 2).reshape(FILT, D),
            shards[:, SHARD_DECAY, 0:channels].reshape(D),
        )

    placed = (
        P(("dp", "mp"), None),
        P(),
        P(None, "mp"),
        P("mp"),
        P(None, "mp"),
        P("mp"),
        P("mp", None),
        P(),
        P(),
        P(None, "mp"),
        P("mp"),
        P("mp", None),
        P(),
        P(),
        P(),
        P(),
        P(),
        P(),
        P(),
        P(),
        P(),
        P(("dp", "mp"), None),
        P(),
        P(),
        P(),
    )
    return jax.shard_map(
        per_device,
        mesh=mesh,
        in_specs=placed,
        out_specs=(
            P(("dp", "mp"), None),
            P(("dp", "mp"), None),
            P(),
            P(),
            P(None, "mp"),
            P("mp"),
            P(None, "mp"),
            P("mp"),
            P("mp", None),
            P(),
            P(),
            P(None, "mp"),
            P("mp"),
            P("mp", None),
            P(),
            P(),
            P(),
            P(),
            P(),
            P(),
            P(),
            P(),
            P(),
        ),
        check_vma=False,
    )
```

```python
import functools
import math
import types

import jax
import jax.numpy as jnp
import numpy as np
from jax import lax
from jax.experimental import pallas as pl
from jax.experimental.pallas import tpu as pltpu
from jax.sharding import PartitionSpec as P

D = 768
BANDS = 16
EMB = 2 * BANDS + 1
FILT = 64
LONG = 1024
BLOCK = 256
BINS = 2 * BLOCK
COUNT = LONG // BLOCK
LANES = 128
WIDE = 3 * LANES
MESH = pl.DeviceIdType.MESH
BF16 = jnp.bfloat16
F32 = jnp.float32
EPS = 1e-05
ROOT = math.sqrt(2.0 / math.pi)
CUBE = 0.044715

PAY_VEC, PAY_PEN, PAY_HID, PAY_EMB, PAY_ROWS = 0, 18, 24, 88, 128
SHARD_DECAY, SHARD_PAR, SHARD_ROWS = 64, 72, 96


def wave_table(shift):
    bins = np.arange(BLOCK)[:, None]
    angle = np.pi * (2 * bins + 1) * (np.arange(BLOCK)[None, :] + shift) / BINS
    return np.concatenate([np.cos(angle), -np.sin(angle)], 0)


NEAR, FAR = wave_table(0), wave_table(-BLOCK)
WAVES = np.concatenate([NEAR, FAR], 1)
UNWAVES = np.concatenate([NEAR.T, FAR.T], 1) / BLOCK


def position_features():
    tau = np.arange(LONG) / LONG
    angles = 2.0 * np.pi * np.arange(1, BANDS + 1)[:, None] * tau[None, :]
    return np.concatenate([tau[None, :], np.cos(angles), np.sin(angles)], 0)


def dot(left, right, dims=((1,), (0,)), precision=None):
    return lax.dot_general(
        left, right, (dims, ((), ())), precision=precision, preferred_element_type=F32
    )


def dot_nt(left, right, precision=None):
    return dot(left, right, ((1,), (1,)), precision)


def dot_tn(left, right, precision=None):
    return dot(left, right, ((0,), (0,)), precision)


HIGH = lax.Precision.HIGHEST


def sin_cos(angle):
    turns = jnp.floor(angle * (2.0 / math.pi) + 0.5)
    rest = angle - turns * 1.5703125
    rest = rest - turns * 4.837512969970703125e-4
    rest = rest - turns * 7.54978995489188e-8
    square = rest * rest
    sine = rest + rest * square * (
        -1.6666654611e-1 + square * (8.3321608736e-3 + square * -1.9515295891e-4)
    )
    cosine = (
        1.0
        - 0.5 * square
        + square
        * square
        * (4.166664568298827e-2 + square * (-1.388731625493765e-3 + square * 2.443315711809948e-5))
    )
    half = jnp.floor(turns * 0.5)
    odd = turns - 2.0 * half
    sign = 1.0 - 2.0 * (half - 2.0 * jnp.floor(half * 0.5))
    swapped = odd > 0.5
    return (
        jnp.where(swapped, cosine, sine) * sign,
        jnp.where(swapped, -sine, cosine) * sign,
    )


def norm_parts(values):
    center = values - jnp.mean(values, axis=-1, keepdims=True)
    scale = lax.rsqrt(jnp.mean(center * center, axis=-1, keepdims=True) + EPS)
    return center * scale, scale


def norm_back(grad, gain, unit, scale):
    inner = grad * gain
    return scale * (
        inner
        - jnp.mean(inner, axis=-1, keepdims=True)
        - unit * jnp.mean(inner * unit, axis=-1, keepdims=True)
    )


def column(row):
    size = row.shape[1]
    same = lax.broadcasted_iota(jnp.int32, (size, size), 0) == lax.broadcasted_iota(
        jnp.int32, (size, size), 1
    )
    return jnp.sum(jnp.where(same, row, 0.0), axis=1, keepdims=True)


def fused(s, names, *refs):
    r = types.SimpleNamespace(**dict(zip(names, refs)))
    ranks, halves, inner, rows = s.ranks, s.halves, s.inner, s.rows
    channels, hidden = s.channels, s.hidden
    dp, mp = lax.axis_index("dp"), lax.axis_index("mp")
    y, c = dp // 2, dp % 2
    q, j = mp // halves, mp % halves
    other, across = 1 - c, 1 - q
    outer = halves // inner

    def device(yy, cc, qq, jj):
        return (yy * 2 + cc, qq * halves + jj)

    def ahead(k):
        return ((j // inner + k // inner) % outer) * inner + (j % inner + k % inner) % inner

    def behind(k):
        return ((j // inner + outer - k // inner) % outer) * inner + (
            j % inner + inner - k % inner
        ) % inner

    sibling = device(y, other, q, j)
    partner = device(y, other, across, j)
    moved = c != q

    def remote(src, dst, send, recv, target):
        return pltpu.make_async_remote_copy(
            src_ref=src,
            dst_ref=dst,
            send_sem=send,
            recv_sem=recv,
            device_id=target,
            device_id_type=MESH,
        )

    def block_rows(cc, jj):
        return pl.ds(pl.multiple_of((cc * halves + jj) * rows, rows), rows)

    mine = block_rows(c, j)

    barrier = pltpu.get_barrier_semaphore()
    greeted = [sibling, partner]
    for k in range(1, halves):
        greeted += [device(y, c, q, ahead(k)), device(y, other, q, ahead(k))]
    for dy in range(ranks):
        for dq in range(2):
            if dy or dq:
                greeted.append(device((y + dy) % ranks, c, (q + dq) % 2, j))
    for target in greeted:
        pl.semaphore_signal(barrier, inc=1, device_id=target, device_id_type=MESH)

    def load(name):
        i = s.loads.index(name)
        return pltpu.make_async_copy(
            getattr(r, name + "_any"), getattr(r, name), r.load_sem.at[i]
        )

    pl.semaphore_wait(barrier, len(greeted))

    par = r.par_own
    theirs = block_rows(other, j)
    x, own_par, w_in, grads, w_out, w_up, w_down = range(7)
    takes = [
        (r.x_any, r.x_in, r.x_in),
        (par, r.par_in, r.par_in),
        (r.win_any, r.win, r.win),
        (r.og_any, r.g_out.at[theirs], r.g_out.at[mine]),
        (r.wout_any, r.wout.at[pl.ds(0, channels)], r.wout.at[pl.ds(0, channels)]),
        (r.wup_any, r.wup, r.wup),
        (r.wdn_any, r.wdn, r.wdn),
    ]
    owner = jnp.logical_not(moved)

    def cut_rows(i, yy):
        size = takes[i][0].shape[0] // ranks
        return pl.ds(pl.multiple_of(yy * size, 16), size)

    def in_parts(i):
        return i in (w_in, w_up, w_down) and takes[i][0].shape[0] % (16 * ranks) == 0

    def take(i, arriving=False):
        src, dst, here = takes[i]
        dst = here if arriving else dst
        if in_parts(i):
            src, dst = src.at[cut_rows(i, y)], dst.at[cut_rows(i, y)]
        return remote(src, dst, r.take_send.at[i], r.take_recv.at[i], partner)

    def take_local(i):
        return pltpu.make_async_copy(takes[i][0], takes[i][2], r.take_local.at[i])

    def pass_copy(i, dy):
        at = takes[i][2].at[cut_rows(i, y)]
        return remote(
            at,
            at,
            r.cut_send.at[i, dy],
            r.cut_recv.at[i, dy],
            device((y + dy) % ranks, c, q, j),
        )

    def take_start(*which, after=()):
        @pl.when(moved)
        def _():
            for i in after:
                take(i).wait_send()
            for i in which:
                take(i).start()

    def take_pass(*which):
        @pl.when(moved)
        def _():
            for i in which:
                take(i, True).wait_recv()
                if in_parts(i):
                    for dy in range(1, ranks):
                        pass_copy(i, dy).start()

    def taken(*which):
        @pl.when(moved)
        def _():
            for i in which:
                if i not in (w_in, w_up, w_down):
                    take(i, True).wait_recv()
                elif in_parts(i):
                    for dy in range(1, ranks):
                        at = takes[i][2].at[cut_rows(i, (y + ranks - dy) % ranks)]
                        remote(
                            at,
                            at,
                            r.cut_send.at[i, dy],
                            r.cut_recv.at[i, dy],
                            device((y + ranks - dy) % ranks, c, q, j),
                        ).wait_recv()
                        pass_copy(i, dy).wait_send()

        @pl.when(owner)
        def _():
            for i in which:
                take_local(i).wait()

    take_start(x)
    @pl.when(owner)
    def _():
        for i in range(len(takes)):
            if i != own_par:
                take_local(i).start()

    for name in s.loads:
        load(name).start()
    for name in s.loads:
        if name not in s.late_loads:
            load(name).wait()

    def line(ref):
        return jnp.reshape(ref[...], (1, ref.shape[0]))

    par[...] = jnp.zeros_like(par)
    par[0:1, 0 : 3 * channels] = line(r.in_bias)
    par[1:4, 0 : 3 * channels] = r.short_taps[...]
    par[4:5, 0:channels] = line(r.skip_gain)
    par[5:6, 0:hidden] = line(r.up_bias).astype(F32)

    @pl.when(owner)
    def _():
        take_local(own_par).start()

    def seat(n, cc, jj):
        size = PAY_ROWS // (2 * halves) if n == 5 else SHARD_ROWS if n == 4 else rows
        return pl.ds(pl.multiple_of((cc * halves + jj) * size, size), size)

    def gather_copies(n, held):
        mine = seat(n, c, j)
        out = []
        for k in range(1, halves):
            out.append(
                remote(
                    held.at[mine],
                    held.at[mine],
                    r.gather_send.at[n, k],
                    r.gather_recv.at[n, k],
                    device(y, c, q, ahead(k)),
                )
            )
        out.append(
            remote(
                held.at[mine],
                held.at[mine],
                r.gather_send.at[n, 0],
                r.gather_recv.at[n, 0],
                sibling,
            )
        )
        return out

    def gather_start(n, held):
        for copy in gather_copies(n, held):
            copy.start()

    def gather_finish(n, held):
        forwards = []
        for k in range(1, halves):
            came = held.at[seat(n, c, behind(k))]
            remote(
                came,
                came,
                r.gather_send.at[n, k],
                r.gather_recv.at[n, k],
                device(y, c, q, behind(k)),
            ).wait_recv()
            forward = remote(
                came, came, r.hop_send.at[n, k], r.hop_recv.at[n, k], sibling
            )
            forward.start()
            forwards.append(forward)
        for k in range(halves):
            came = held.at[seat(n, other, behind(k))]
            recv = r.hop_recv.at[n, k] if k else r.gather_recv.at[n, 0]
            remote(came, came, r.hop_send.at[n, k], recv, sibling).wait_recv()
        for copy in gather_copies(n, held) + forwards:
            copy.wait_send()

    def first_norm():
        unit, _ = norm_parts(r.x_in[...].astype(F32))
        r.g_one[mine, :] = (unit * line(r.mixer_gain)).astype(BF16)
        gather_start(0, r.g_one)

    @pl.when(owner)
    def _():
        take_local(x).wait()
        first_norm()
        take_local(grads).wait()
        gather_start(1, r.g_out)

    pack = y * 2 + q
    segments = []
    for i in range(COUNT):
        found = jnp.int32(-1)
        for k in range(s.sequences):
            start = r.offsets[k]
            hit = (
                (r.owners[k] == pack)
                & (start <= i * BLOCK)
                & (start + r.lengths[k] > i * BLOCK)
            )
            found = jnp.where(hit, jnp.int32(k), found)
        segments.append(found)
    valid = [jnp.where(seg >= 0, jnp.float32(1), jnp.float32(0)) for seg in segments]
    joined = [
        [valid[i] * jnp.where(segments[i] == segments[p], jnp.float32(1), jnp.float32(0)) for p in range(i + 1)]
        for i in range(COUNT)
    ]
    follows = [jnp.float32(0)] + [joined[i][i - 1] for i in range(1, COUNT)]

    row_index = lax.broadcasted_iota(jnp.int32, (3 * channels, WIDE), 0)
    lane_index = lax.broadcasted_iota(jnp.int32, (3 * channels, WIDE), 1)
    within = lane_index % LANES
    order = jnp.where(
        (row_index == 3 * within + lane_index // LANES) & (within < channels), 1.0, 0.0
    )
    r.order[...] = order.astype(BF16)
    r.order_wide[...] = order

    load("features").wait()
    features = r.features[...]
    embed_freq, embed_bias = column(line(r.embed_freq)), column(line(r.embed_bias))
    hidden_freq, hidden_bias = column(line(r.hidden_freq)), column(line(r.hidden_bias))
    first_sum = dot_tn(r.embed_weight[...], features, HIGH) + embed_bias
    first, first_cos = sin_cos(embed_freq * first_sum)
    r.first_sum[...] = first_sum
    r.first[...] = first
    r.first_cos[...] = first_cos
    take_start(w_in, own_par, after=(x,))
    second_sum = dot_tn(r.hidden_weight[...], first, HIGH) + hidden_bias
    second, second_cos = sin_cos(hidden_freq * second_sum)
    r.second_sum[...] = second_sum
    r.second[...] = second
    r.second_cos[...] = second_cos
    half_rows = LONG // 2
    chunks = half_rows // BLOCK
    per_chunk = BLOCK // rows

    def half_chunk(cc, t):
        return pl.ds(pl.multiple_of(cc * half_rows + t * BLOCK, BLOCK), BLOCK)

    def chunk_rows(t):
        return pl.ds(pl.multiple_of(t * BLOCK, BLOCK), BLOCK)

    def place(jj):
        return pl.ds(pl.multiple_of(jj * rows, rows), rows)

    def chip_copy(n, t):
        return remote(
            r.chip_out.at[n, chunk_rows(t)],
            r.chip_in.at[n, chunk_rows(t)],
            r.chip_send.at[n, t],
            r.chip_recv.at[n, t],
            sibling,
        )

    def link_copy(n, jj):
        return remote(
            r.link_out.at[n, place(jj)],
            r.link_in.at[n, place(j)],
            r.link_send.at[n, jj],
            r.link_recv.at[n, j],
            device(y, c, q, jj),
        )

    def chip_give(n, t, value):
        r.chip_out[n, chunk_rows(t), :] = value.astype(BF16)
        chip_copy(n, t).start()

    def chip_add(n, t, value):
        chip_copy(n, t).wait_recv()
        r.link_out[n, chunk_rows(t), :] = (
            value + r.chip_in[n, chunk_rows(t), :].astype(F32)
        ).astype(BF16)

    def link_start(n, t):
        for i in range(per_chunk):
            jj = t * per_chunk + i

            @pl.when(jj != j)
            def _():
                link_copy(n, jj).start()

    def scatter(n, part):
        def give(t, carry):
            chip_give(n, t, part(half_chunk(other, t)))
            return carry

        lax.fori_loop(0, chunks, give, 0)

        def send(t, carry):
            chip_add(n, t, part(half_chunk(c, t)))
            link_start(n, t)
            return carry

        lax.fori_loop(0, chunks, send, 0)

    def scatter_finish(n):
        total = r.link_out[n, place(j), :].astype(F32)
        for k in range(1, halves):
            jj = behind(k)
            came = r.link_in.at[n, place(jj)]
            remote(
                came, came, r.link_send.at[n, jj], r.link_recv.at[n, jj], device(y, c, q, jj)
            ).wait_recv()
            total = total + r.link_in[n, place(jj), :].astype(F32)
        for t in range(chunks):
            chip_copy(n, t).wait_send()
        for k in range(1, halves):
            link_copy(n, ahead(k)).wait_send()
        return total

    @pl.when(moved)
    def _():
        take(x, True).wait_recv()
        first_norm()

    shard = c * halves + j
    pick_row = lax.broadcasted_iota(jnp.int32, (D, LANES), 0)
    pick_lane = lax.broadcasted_iota(jnp.int32, (D, LANES), 1)
    pick = jnp.where((pick_row == shard * channels + pick_lane) & (pick_lane < channels), 1.0, 0.0)
    own_filter = dot(r.filter_weight[...], pick, precision=HIGH)
    own_decay = dot(jnp.broadcast_to(line(r.decay_rate), (8, D)), pick, precision=HIGH)[0:1]
    r.own_filter[...] = own_filter
    r.own_decay[...] = jnp.broadcast_to(own_decay, (8, LANES))
    r.spread[...] = jnp.zeros_like(r.spread)
    for i in range(COUNT):
        at = slice(i * BLOCK, (i + 1) * BLOCK)
        tau = (
            lax.broadcasted_iota(jnp.int32, (BLOCK, LANES), 0) + i * BLOCK
        ).astype(F32) * (1.0 / LONG)
        kernel = dot_tn(second[:, at], own_filter, HIGH) * jnp.exp(-tau * own_decay)
        r.kernel[at, :] = kernel
        low = kernel.astype(BF16)
        r.spread[0:BLOCK, i * LANES : (i + 1) * LANES] = low
        if i + 1 < COUNT:
            r.spread[BLOCK:BINS, (i + 1) * LANES : (i + 2) * LANES] = low
    take_start(grads, w_out, after=(w_in, own_par))
    take_pass(w_in)
    load("waves").wait()
    load("unwaves").wait()
    r.kernel_wave[...] = dot(r.waves[...], r.spread[...])
    gather_finish(0, r.g_one)

    @pl.when(moved)
    def _():
        take(grads, True).wait_recv()
        gather_start(1, r.g_out)

    take_start(w_up, w_down, after=(grads,))
    taken(own_par, w_in)
    par_wide = dot(r.par_in[:, 0 : 3 * channels], r.order_wide[...], precision=HIGH)
    r.taps[...] = par_wide
    r.win_apart[...] = dot_tn(r.order[...], r.win[...]).astype(BF16)
    r.wout[channels:, :] = jnp.zeros_like(r.wout[channels:, :])

    def project(i, carry):
        at = pl.ds(pl.multiple_of(i * BINS, BINS), BINS)
        r.projected[at, :] = dot_nt(r.g_one[at, :], r.win_apart[...]) + r.taps[0:1, :]
        return carry

    lax.fori_loop(0, LONG // BINS, project, 0)

    rows_here = lax.broadcasted_iota(jnp.int32, (BLOCK, 1), 0)

    def back_rows(i):
        now = r.projected[i * BLOCK : (i + 1) * BLOCK, :]
        one, two = pltpu.roll(now, 1, 0), pltpu.roll(now, 2, 0)
        if i:
            edge = r.projected[i * BLOCK - 8 : i * BLOCK, :] * follows[i]
            last, before = edge[7:8], edge[6:7]
        else:
            last = before = jnp.zeros((1, WIDE), F32)
        one = jnp.where(rows_here == 0, last, one)
        two = jnp.where(rows_here == 0, before, jnp.where(rows_here == 1, last, two))
        return now, one, two

    for i in range(COUNT):
        now, one, two = back_rows(i)
        short = r.taps[1:2, :] * now + r.taps[2:3, :] * one + r.taps[3:4, :] * two
        r.short[i * BLOCK : (i + 1) * BLOCK, :] = short
        signal = short[:, 2 * LANES :] * short[:, LANES : 2 * LANES] * valid[i]
        r.signal[:, i * LANES : (i + 1) * LANES] = signal.astype(BF16)

    near = r.waves[:, 0:BLOCK]
    unnear = r.unwaves[:, 0:BINS]
    r.signal_wave[...] = dot(near, r.signal[...])
    step = 16

    def load_wave(ref, at, count=COUNT):
        low, high = pl.ds(at, step), pl.ds(at + BLOCK, step)
        return [
            (ref[low, i * LANES : (i + 1) * LANES], ref[high, i * LANES : (i + 1) * LANES])
            for i in range(count)
        ]

    def store_wave(ref, base, at, i, pair):
        ref[pl.ds(base + at, step), i * LANES : (i + 1) * LANES] = pair[0].astype(BF16)
        ref[pl.ds(base + at + BLOCK, step), i * LANES : (i + 1) * LANES] = pair[1].astype(BF16)

    def weighted(terms):
        real = imag = None
        for weight, (a, b) in terms:
            real = a * weight if real is None else real + a * weight
            imag = b * weight if imag is None else imag + b * weight
        return real, imag

    def times(left, right):
        return left[0] * right[0] - left[1] * right[1], left[0] * right[1] + left[1] * right[0]

    def times_conj(left, right):
        return left[0] * right[0] + left[1] * right[1], left[0] * right[1] - left[1] * right[0]

    def forward_wave(n, carry):
        at = pl.multiple_of(n * step, step)
        kernels, signals = load_wave(r.kernel_wave, at), load_wave(r.signal_wave, at)
        for i in range(COUNT):
            store_wave(
                r.product,
                0,
                at,
                i,
                weighted([(joined[i][p], times(kernels[i - p], signals[p])) for p in range(i + 1)]),
            )
        return carry

    lax.fori_loop(0, BLOCK // step, forward_wave, 0)
    skip = r.par_in[4:5, 0:LANES]
    convolved = dot(unnear, r.product[0:BINS, :])
    for i in range(COUNT):
        at = slice(i * BLOCK, (i + 1) * BLOCK)
        lanes = slice(i * LANES, (i + 1) * LANES)
        direct = convolved[:, lanes] + skip * r.signal[:, lanes].astype(F32)
        r.direct[at, :] = direct
        r.mixed[at, :] = (direct * r.short[at, 0:LANES]).astype(BF16)

    taken(w_out)
    scatter(0, lambda at: dot(r.mixed[at, :], r.wout[...]))
    take_pass(w_up)
    middle = r.x_in[...].astype(F32) + line(r.out_bias) + scatter_finish(0)
    unit, scale = norm_parts(middle)
    r.g_two[mine, :] = (unit * line(r.ffn_gain)).astype(BF16)
    gather_start(2, r.g_two)
    r.middle[...] = middle
    r.unit[...] = unit
    r.scale[...] = jnp.broadcast_to(scale, r.scale.shape)
    take_pass(w_down)
    gather_finish(1, r.g_out)
    gather_finish(2, r.g_two)
    taken(w_up, w_down)

    def feed(at):
        value = dot(r.g_two[at, :], r.wup[...]) + r.par_in[5:6, 0:hidden]
        square = value * value
        bend = jnp.tanh(ROOT * value * (1.0 + CUBE * square))
        half = 0.5 * (1.0 + bend)
        active = (value * half).astype(BF16)
        slope = half + 0.5 * value * (1.0 - bend * bend) * (ROOT * (1.0 + 3.0 * CUBE * square))
        grad = (slope * dot_nt(r.g_out[at, :], r.wdn[...])).astype(BF16)
        r.active[at, :] = active
        r.hidden_grad[at, :] = grad
        return dot_nt(grad, r.wup[...]), dot(active, r.wdn[...])

    def feed_step(i, carry):
        t, own = i // 2, i % 2
        back, forth = feed(half_chunk(own * c + (1 - own) * other, t))

        @pl.when(own == 0)
        def _():
            chip_give(1, t, back)
            chip_give(2, t, forth)

        @pl.when(own == 1)
        def _():
            chip_add(1, t, back)
            link_start(1, t)
            chip_add(2, t, forth)

        return carry

    lax.fori_loop(0, 2 * chunks, feed_step, 0)

    sums = [
        (r.grad_in, r.part_in, r.y_in, r.z_in, r.gwin),
        (r.grad_out, r.part_out, r.y_out, r.z_out, r.gwout),
        (r.grad_up, r.part_up, r.y_up, r.z_up, r.gwup),
        (r.grad_dn, r.part_dn, r.y_dn, r.z_dn, r.gwdn),
    ]
    def part_rows(ref, yy):
        size = ref.shape[0] // ranks
        return pl.ds(pl.multiple_of(yy * size, 16), size)

    def y_copy(w, dy):
        full, _, came, _, _ = sums[w]
        to = (y + dy) % ranks
        return remote(
            full.at[part_rows(full, to)],
            came.at[dy],
            r.y_send.at[w, dy],
            r.y_recv.at[w, dy],
            device(to, c, q, j),
        )

    def z_copy(w):
        _, part, _, came, _ = sums[w]
        return remote(
            part, came, r.z_send.at[w], r.z_recv.at[w], device(y, c, across, j)
        )

    def out_copy(w, dy):
        final = sums[w][4]
        at = part_rows(final, y)
        return remote(
            final.at[at],
            final.at[at],
            r.out_send.at[w, dy],
            r.out_recv.at[w, dy],
            device((y + dy) % ranks, c, q, j),
        )

    def chip_final(w, dy):
        final = sums[w][4]
        at = part_rows(final, (y + ranks - dy) % ranks)
        return remote(
            final.at[at],
            final.at[at],
            r.fin_send.at[w, dy],
            r.fin_recv.at[w, dy],
            sibling,
        )

    def sum_start(w):
        for dy in range(1, ranks):
            y_copy(w, dy).start()

    def sum_cross(w):
        full, part, came, _, _ = sums[w]
        total = full[part_rows(full, y), :].astype(F32)
        for dy in range(1, ranks):
            y_copy(w, dy).wait_recv()
            total = total + came[dy].astype(F32)
        part[...] = total.astype(BF16)

        @pl.when(moved)
        def _():
            z_copy(w).start()

    def sum_close(w):
        _, part, _, came, final = sums[w]

        @pl.when(owner)
        def _():
            z_copy(w).wait_recv()
            final[part_rows(final, y), :] = (
                part[...].astype(F32) + came[...].astype(F32)
            ).astype(BF16)
            for dy in range(1, ranks):
                out_copy(w, dy).start()
            chip_final(w, 0).start()

    def sum_finish(w):
        final = sums[w][4]

        @pl.when(owner)
        def _():
            for dy in range(1, ranks):
                at = part_rows(final, (y + ranks - dy) % ranks)
                remote(
                    final.at[at],
                    final.at[at],
                    r.out_send.at[w, dy],
                    r.out_recv.at[w, dy],
                    sibling,
                ).wait_recv()
                chip_final(w, dy).start()
            for dy in range(1, ranks):
                out_copy(w, dy).wait_send()
            for dy in range(ranks):
                chip_final(w, dy).wait_send()

        @pl.when(moved)
        def _():
            for dy in range(ranks):
                chip_final(w, dy).wait_recv()
            z_copy(w).wait_send()

        for dy in range(1, ranks):
            y_copy(w, dy).wait_send()

    def weight_grad(target, left, right, by_right=False):
        def chunk(i, carry):
            at = pl.ds(pl.multiple_of(i * BLOCK, BLOCK), BLOCK)
            if by_right:
                target[0 : left.shape[1], at] = dot_tn(left[...], right[:, at]).astype(BF16)
            else:
                target[at, :] = dot_tn(left[:, at], right[...]).astype(BF16)
            return carry

        lax.fori_loop(0, D // BLOCK, chunk, 0)

    for grad, size in ((r.grad_dn, hidden), (r.grad_in, 3 * channels)):
        if grad.shape[0] > size:
            grad[size:, :] = jnp.zeros_like(grad[size:, :])
    weight_grad(r.grad_dn, r.active, r.g_out, True)
    sum_start(3)
    weight_grad(r.grad_up, r.g_two, r.hidden_grad)
    sum_start(2)

    seed = r.g_out[mine, :].astype(F32)
    ffn_back = scatter_finish(1)
    unit, scale = r.unit[...], jnp.concatenate([r.scale[...]] * (D // LANES), axis=1)
    middle_grad = seed + norm_back(ffn_back, line(r.ffn_gain), unit, scale)
    r.middle_grad[...] = middle_grad
    branch_grad = middle_grad.astype(BF16)
    r.g_back[mine, :] = branch_grad
    gather_start(3, r.g_back)
    vectors = [
        jnp.sum(ffn_back * unit, axis=0, keepdims=True),
        jnp.sum(branch_grad.astype(F32), axis=0, keepdims=True),
        jnp.sum(seed, axis=0, keepdims=True),
    ]
    r.pay[...] = jnp.zeros_like(r.pay)
    for v, vector in enumerate(vectors):
        for k in range(D // LANES):
            at = PAY_VEC + v * (D // LANES) + k
            r.pay[at : at + 1, :] = vector[:, k * LANES : (k + 1) * LANES]
    par_grad = r.par_grad
    par_grad[...] = jnp.zeros_like(par_grad)
    par_grad[5:6, 0:hidden] = jnp.sum(r.hidden_grad[...].astype(F32), axis=0, keepdims=True)
    sum_cross(3)
    sum_cross(2)
    gather_finish(3, r.g_back)
    for t in range(chunks):
        link_start(2, t)
    r.grad_out[...] = dot_tn(r.mixed[...], r.g_back[...]).astype(BF16)
    sum_start(1)

    skip_total = jnp.zeros((1, LANES), F32)
    for i in range(COUNT):
        at = slice(i * BLOCK, (i + 1) * BLOCK)
        lanes = slice(i * LANES, (i + 1) * LANES)
        mixed_grad = dot_nt(r.g_back[at, :], r.wout[...])
        r.short_grad[at, 0:LANES] = mixed_grad * r.direct[at, :]
        direct_grad = mixed_grad * r.short[at, 0:LANES]
        r.direct[at, :] = direct_grad
        r.direct_low[:, lanes] = direct_grad.astype(BF16)
        skip_total += jnp.sum(
            direct_grad * r.signal[:, lanes].astype(F32), axis=0, keepdims=True
        )
    par_grad[4:5, 0:LANES] = skip_total
    r.grad_wave[...] = dot(near, r.direct_low[...])
    r.back_product[...] = jnp.zeros_like(r.back_product)

    def backward_wave(n, carry):
        at = pl.multiple_of(n * step, step)
        kernels, signals = load_wave(r.kernel_wave, at), load_wave(r.signal_wave, at)
        grads = load_wave(r.grad_wave, at)
        for p in range(COUNT):
            terms = [(joined[i][p], times_conj(kernels[i - p], grads[i])) for i in range(p, COUNT)]
            store_wave(r.product, 0, at, p, weighted(terms))
        for d in range(COUNT):
            terms = [
                (joined[i][i - d], times_conj(signals[i - d], grads[i])) for i in range(d, COUNT)
            ]
            pair = weighted(terms)
            store_wave(r.back_product, 0, at, d, pair)
            if d:
                store_wave(r.back_product, BINS, at, d - 1, pair)
        return carry

    lax.fori_loop(0, BLOCK // step, backward_wave, 0)
    signal_grads = dot(unnear, r.product[0:BINS, :])
    for i in range(COUNT):
        at = slice(i * BLOCK, (i + 1) * BLOCK)
        lanes = slice(i * LANES, (i + 1) * LANES)
        signal_grad = (signal_grads[:, lanes] + skip * r.direct[at, :]) * valid[i]
        r.short_grad[at, LANES : 2 * LANES] = signal_grad * r.short[at, 2 * LANES :]
        r.short_grad[at, 2 * LANES :] = signal_grad * r.short[at, LANES : 2 * LANES]

    bias_total = jnp.zeros((1, WIDE), F32)
    tap_totals = [jnp.zeros((1, WIDE), F32) for _ in range(3)]
    for i in range(COUNT):
        at = slice(i * BLOCK, (i + 1) * BLOCK)
        now, one, two = back_rows(i)
        grad = r.short_grad[at, :]
        for t, value in enumerate((now, one, two)):
            tap_totals[t] += jnp.sum(grad * value, axis=0, keepdims=True)
        next_one = pltpu.roll(grad, BLOCK - 1, 0)
        next_two = pltpu.roll(grad, BLOCK - 2, 0)
        if i + 1 < COUNT:
            edge = r.short_grad[(i + 1) * BLOCK : (i + 1) * BLOCK + 8, :] * follows[i + 1]
            head, after = edge[0:1], edge[1:2]
        else:
            head = after = jnp.zeros((1, WIDE), F32)
        next_one = jnp.where(rows_here == BLOCK - 1, head, next_one)
        next_two = jnp.where(
            rows_here == BLOCK - 2, head, jnp.where(rows_here == BLOCK - 1, after, next_two)
        )
        low = (
            r.taps[1:2, :] * grad + r.taps[2:3, :] * next_one + r.taps[3:4, :] * next_two
        ).astype(BF16)
        bias_total += jnp.sum(low.astype(F32), axis=0, keepdims=True)
        r.projected_grad[at, :] = dot_nt(low, r.order[...]).astype(BF16)
    par_grad[0:1, :] = bias_total
    for t in range(3):
        par_grad[t + 1 : t + 2, :] = tap_totals[t]

    sum_cross(1)
    scatter(3, lambda at: dot(r.projected_grad[at, :], r.win[...]))

    weight_grad(r.grad_in, r.projected_grad, r.g_one, True)
    sum_start(0)

    kernel_grads = dot(r.unwaves[...], r.back_product[...])
    decay_total = jnp.zeros((1, LANES), F32)
    penalty = jnp.zeros((1, LANES), F32)
    own_filter = r.own_filter[...]
    own_decay = r.own_decay[0:1, :]
    lead = jnp.where(pack == 0, 1.0 / D, 0.0).astype(F32)
    for i in range(COUNT):
        at = slice(i * BLOCK, (i + 1) * BLOCK)
        tau = (
            lax.broadcasted_iota(jnp.int32, (BLOCK, LANES), 0) + i * BLOCK
        ).astype(F32) * (1.0 / LONG)
        kernel = r.kernel[at, :]
        weighed = tau * kernel
        penalty += jnp.sum(weighed * kernel, axis=0, keepdims=True) * lead
        kernel_grad = (
            kernel_grads[:, i * LANES : (i + 1) * LANES] + weighed * (2.0 * lead)
        )
        decay_total -= jnp.sum(kernel_grad * weighed, axis=0, keepdims=True)
        r.raw_grad[at, :] = kernel_grad * jnp.exp(-tau * own_decay)
    sums_y, sums_q = r.shard_y, r.shard_q
    sums_y[y] = jnp.zeros((SHARD_ROWS, LANES), F32)
    sums_y[y, 0:FILT, :] = dot(r.second[...], r.raw_grad[...], precision=HIGH)
    sums_y[y, SHARD_DECAY : SHARD_DECAY + 1, :] = decay_total
    for k in range(3):
        at = SHARD_PAR + 8 * k
        sums_y[y, at : at + 8, :] = par_grad[:, k * LANES : (k + 1) * LANES]

    def shard_y(dy, back=False):
        at = sums_y.at[(y + ranks - dy) % ranks if back else y]
        return remote(
            at, at, r.sy_send.at[dy], r.sy_recv.at[dy], device((y + dy) % ranks, c, q, j)
        )

    def shard_q(back=False):
        at = sums_q.at[across if back else q]
        return remote(at, at, r.sq_send.at[0], r.sq_recv.at[0], device(y, c, across, j))

    for dy in range(1, ranks):
        shard_y(dy).start()
    r.pay[PAY_PEN : PAY_PEN + 1, :] = penalty
    second_grad = dot_nt(own_filter, r.raw_grad[...], HIGH)
    angle_grad = second_grad * r.second_cos[...]
    freq_grad = jnp.sum(angle_grad * r.second_sum[...], axis=1, keepdims=True)
    sum_grad = angle_grad * column(line(r.hidden_freq))
    at = slice(PAY_HID, PAY_HID + FILT)
    r.pay[at, 0:FILT] = dot_nt(r.first[...], sum_grad, HIGH)
    r.pay[at, FILT : FILT + 1] = freq_grad
    r.pay[at, FILT + 1 : FILT + 2] = jnp.sum(sum_grad, axis=1, keepdims=True)
    angle_grad = dot(r.hidden_weight[...], sum_grad, precision=HIGH) * r.first_cos[...]
    r.pay[at, FILT + 2 : FILT + 3] = jnp.sum(
        angle_grad * r.first_sum[...], axis=1, keepdims=True
    )
    sum_grad = angle_grad * column(line(r.embed_freq))
    r.pay[at, FILT + 3 : FILT + 4] = jnp.sum(sum_grad, axis=1, keepdims=True)
    r.pay[PAY_EMB : PAY_EMB + EMB, 0:FILT] = dot_nt(features, sum_grad, HIGH)

    half_pay = PAY_ROWS // 2
    part_pay = half_pay // halves
    slot = y * 2 + q

    def pay_half(cc):
        return pl.ds(pl.multiple_of(cc * half_pay, half_pay), half_pay)

    def pay_chip():
        return remote(
            r.pay.at[pay_half(other)], r.pay_in, r.pay_send.at[0], r.pay_recv.at[0], sibling
        )

    def pay_link(jj):
        at = pl.ds(pl.multiple_of(jj * part_pay, part_pay), part_pay)
        return remote(
            r.pay_sum.at[at],
            r.pay_held.at[j],
            r.paylink_send.at[jj],
            r.paylink_recv.at[j],
            device(y, c, q, jj),
        )

    def slots_copies(n, held):
        out = []
        for dy in range(ranks):
            for dq in range(2):
                if dy or dq:
                    out.append(
                        remote(
                            held.at[slot],
                            held.at[slot],
                            r.cross_send.at[n, dy * 2 + dq],
                            r.cross_recv.at[n, dy * 2 + dq],
                            device((y + dy) % ranks, c, (q + dq) % 2, j),
                        )
                    )
        return out

    def slots_sum(n, held):
        for dy in range(ranks):
            for dq in range(2):
                if dy or dq:
                    yy, qq = (y + ranks - dy) % ranks, (q + dq) % 2
                    came = held.at[yy * 2 + qq]
                    remote(
                        came,
                        came,
                        r.cross_send.at[n, dy * 2 + dq],
                        r.cross_recv.at[n, dy * 2 + dq],
                        device(yy, c, qq, j),
                    ).wait_recv()
        return added(held, 2 * ranks)

    def added(held, count):
        total = held[0]
        for i in range(1, count):
            total = total + held[i]
        return total

    pay_chip().start()
    for w in (3, 2, 1):
        sum_close(w)

    pay_chip().wait_recv()
    r.pay_sum[...] = r.pay[pay_half(c), :] + r.pay_in[...]
    for k in range(1, halves):
        pay_link(ahead(k)).start()
    r.pay_held[j] = r.pay_sum[pl.ds(pl.multiple_of(j * part_pay, part_pay), part_pay), :]
    for dy in range(1, ranks):
        shard_y(dy, True).wait_recv()
    sums_q[q] = added(sums_y, ranks)
    shard_q().start()
    sum_cross(0)

    r.block_out[...] = (r.middle[...] + line(r.down_bias) + scatter_finish(2)).astype(BF16)
    gives = [(r.input_grad, r.input_any), (r.block_out, r.block_any)]

    def give(i):
        src, dst = gives[i]
        return remote(src, dst, r.give_send.at[i], r.give_recv.at[i], partner)

    def give_local(i):
        src, dst = gives[i]
        return pltpu.make_async_copy(src, dst, r.give_local.at[i])

    def give_start(i):
        @pl.when(moved)
        def _():
            give(i).start()

        @pl.when(owner)
        def _():
            give_local(i).start()

    give_start(1)

    for k in range(1, halves):
        jj = behind(k)
        remote(
            r.pay_held.at[jj],
            r.pay_held.at[jj],
            r.paylink_send.at[jj],
            r.paylink_recv.at[jj],
            device(y, c, q, jj),
        ).wait_recv()
    r.pay_cross[slot] = added(r.pay_held, halves)
    for copy in slots_copies(0, r.pay_cross):
        copy.start()
    shard_q(True).wait_recv()
    r.shards[pl.ds(pl.multiple_of(shard * SHARD_ROWS, SHARD_ROWS), SHARD_ROWS), :] = added(
        sums_q, 2
    )
    gather_start(4, r.shards)

    unit, scale = norm_parts(r.x_in[...].astype(F32))
    mixer_back = scatter_finish(3)
    r.input_grad[...] = (
        r.middle_grad[...] + norm_back(mixer_back, line(r.mixer_gain), unit, scale)
    ).astype(BF16)
    give_start(0)
    gain_row = jnp.sum(mixer_back * unit, axis=0, keepdims=True)
    r.late[...] = jnp.zeros_like(r.late)
    for k in range(D // LANES):
        r.late[k : k + 1, :] = gain_row[:, k * LANES : (k + 1) * LANES]

    def late_chip():
        return remote(r.late, r.late_in, r.late_send.at[0], r.late_recv.at[0], sibling)

    def late_links():
        return [
            remote(
                r.late_held.at[j],
                r.late_held.at[j],
                r.late_send.at[k],
                r.late_recv.at[k],
                device(y, c, q, ahead(k)),
            )
            for k in range(1, halves)
        ]

    late_chip().start()

    def store(name):
        i = s.stores.index(name)
        return pltpu.make_async_copy(
            getattr(r, name), getattr(r, name + "_out"), r.store_sem.at[i]
        )

    r.pay_total[seat(5, c, j), :] = slots_sum(0, r.pay_cross)
    gather_start(5, r.pay_total)
    late_chip().wait_recv()
    r.late_held[j] = r.late[...] + r.late_in[...]
    for copy in late_links():
        copy.start()
    sum_close(0)
    for k in range(1, halves):
        came = r.late_held.at[behind(k)]
        remote(
            came, came, r.late_send.at[k], r.late_recv.at[k], device(y, c, q, behind(k))
        ).wait_recv()
    r.late_cross[slot] = added(r.late_held, halves)
    for copy in slots_copies(1, r.late_cross):
        copy.start()

    gather_finish(4, r.shards)
    store("shards").start()
    home = pl.multiple_of((q * halves + j) * SHARD_ROWS, SHARD_ROWS)
    wide = jnp.concatenate(
        [r.shards[pl.ds(home + SHARD_PAR + 8 * k, 8), :] for k in range(3)], axis=1
    )
    r.par_wide[...] = wide
    r.par_close[...] = dot_nt(wide, r.order_wide[...], HIGH)
    store("par_wide").start()
    store("par_close").start()
    for w, name in ((3, "gwdn"), (2, "gwup"), (1, "gwout")):
        sum_finish(w)
        store(name).start()
    gather_finish(5, r.pay_total)
    store("pay_total").start()
    r.late_total[...] = slots_sum(1, r.late_cross)
    store("late_total").start()
    sum_finish(0)
    store("gwin").start()
    for name in s.stores:
        store(name).wait()

    pay_chip().wait_send()
    for k in range(1, halves):
        pay_link(ahead(k)).wait_send()
    for dy in range(1, ranks):
        shard_y(dy).wait_send()
    shard_q().wait_send()
    late_chip().wait_send()
    for copy in late_links() + slots_copies(0, r.pay_cross) + slots_copies(1, r.late_cross):
        copy.wait_send()

    @pl.when(moved)
    def _():
        for i in (w_out, w_up, w_down):
            take(i).wait_send()
        for i in range(len(gives)):
            give(i).wait()

    @pl.when(owner)
    def _():
        for i in range(len(gives)):
            give_local(i).wait()


def close(s, names, *refs):
    r = types.SimpleNamespace(**dict(zip(names, refs)))
    lines = D // LANES

    def load(name):
        i = s.loads.index(name)
        return pltpu.make_async_copy(
            getattr(r, name + "_any"), getattr(r, name), r.load_sem.at[i]
        )

    def store(name):
        i = s.stores.index(name)
        return pltpu.make_async_copy(getattr(r, name), getattr(r, name + "_out"), r.store_sem.at[i])

    def put(**values):
        for name, value in values.items():
            held = getattr(r, name)
            held[...] = value if value.shape == held.shape else jnp.reshape(value, held.shape)
            store(name).start()

    for name in s.loads:
        load(name).start()
    load("block").wait()
    through = pltpu.make_async_copy(r.block, r.block_out, r.block_sem)
    through.start()
    for name in ("gwin", "gwup", "gwdn", "gwout", "input"):
        load(name).wait()
        held = getattr(r, name)
        size = getattr(r, name + "_wide").shape[0]
        put(**{name + "_wide": held[0:size, :].astype(F32)})
    load("pay_total").wait()
    pay = r.pay_total

    def long_row(ref, at):
        return jnp.concatenate([ref[at + k : at + k + 1, :] for k in range(lines)], axis=1)

    same = lax.broadcasted_iota(jnp.int32, (FILT, FILT), 0) == lax.broadcasted_iota(
        jnp.int32, (FILT, FILT), 1
    )

    def vector_of(k):
        col = pay[PAY_HID : PAY_HID + FILT, FILT + k : FILT + k + 1]
        return jnp.sum(jnp.where(same, col, 0.0), axis=0, keepdims=True)

    put(ffn_gain=long_row(pay, PAY_VEC))
    put(out_bias=long_row(pay, PAY_VEC + lines))
    put(down_bias=long_row(pay, PAY_VEC + 2 * lines))
    put(embed_weight=pay[PAY_EMB : PAY_EMB + EMB, 0:FILT])
    put(embed_bias=vector_of(3))
    put(embed_freq=vector_of(2))
    put(hidden_weight=pay[PAY_HID : PAY_HID + FILT, 0:FILT])
    put(hidden_bias=vector_of(1))
    put(hidden_freq=vector_of(0))
    r.penalty_out[0] = jnp.sum(pay[PAY_PEN : PAY_PEN + 1, :])
    load("late_total").wait()
    put(mixer_gain=long_row(r.late_total, 0))
    load("par_wide").wait()
    load("par_close").wait()
    put(in_bias=r.par_close[0:1, :])
    put(short_taps=r.par_close[1:4, :])
    put(skip_gain=r.par_wide[4:5, 0 : s.channels])
    put(up_bias=r.par_wide[5:6, 0 : s.hidden])
    load("shards").wait()
    for i in range(2 * s.halves):
        at = slice(i * s.channels, (i + 1) * s.channels)
        base = i * SHARD_ROWS
        r.filter_weight[:, at] = r.shards[base : base + FILT, 0 : s.channels]
        r.decay_row[0:1, at] = r.shards[
            base + SHARD_DECAY : base + SHARD_DECAY + 1, 0 : s.channels
        ]
    store("filter_weight").start()
    put(decay_rate=r.decay_row[0:1, :])
    for name in s.stores:
        store(name).wait()
    through.wait()


def round_up(value, unit):
    return (value + unit - 1) // unit * unit


def solution(mesh):
    n_dp, n_mp = mesh.shape["dp"], mesh.shape["mp"]

    def per_device(
        block_input,
        mixer_gain,
        in_weight,
        in_bias,
        short_taps,
        skip_gain,
        out_weight,
        out_bias,
        ffn_gain,
        up_weight,
        up_bias,
        down_weight,
        down_bias,
        embed_weight,
        embed_bias,
        embed_freq,
        hidden_weight,
        hidden_bias,
        hidden_freq,
        filter_weight,
        decay_rate,
        out_grad,
        sequence_lengths,
        sequence_rank,
        sequence_offset,
    ):
        ranks, halves = n_dp // 2, n_mp // 2
        rows = block_input.shape[0]
        channels, hidden = skip_gain.shape[0], up_weight.shape[1]
        down_rows = round_up(hidden, 16 * ranks)
        in_rows = round_up(3 * channels, 16 * ranks)
        group = 2 * halves
        anywhere = pl.BlockSpec(memory_space=pl.ANY)
        scalar = pl.BlockSpec(memory_space=pltpu.SMEM)
        small = dict(
            mixer_gain=mixer_gain,
            ffn_gain=ffn_gain,
            out_bias=out_bias,
            down_bias=down_bias,
            in_bias=in_bias,
            short_taps=short_taps,
            skip_gain=skip_gain,
            embed_weight=embed_weight,
            embed_bias=embed_bias,
            embed_freq=embed_freq,
            hidden_weight=hidden_weight,
            hidden_bias=hidden_bias,
            hidden_freq=hidden_freq,
            filter_weight=filter_weight,
            decay_rate=decay_rate,
            features=jnp.asarray(position_features(), F32),
            waves=jnp.asarray(WAVES, BF16),
            unwaves=jnp.asarray(UNWAVES, BF16),
        )
        inputs = dict(
            x_any=(block_input, anywhere),
            og_any=(out_grad, anywhere),
            win_any=(in_weight.T, anywhere),
            wout_any=(out_weight, anywhere),
            wup_any=(up_weight, anywhere),
            wdn_any=(down_weight, anywhere),
            up_bias=(up_bias, pl.BlockSpec(memory_space=pltpu.VMEM)),
            lengths=(sequence_lengths, scalar),
            owners=(sequence_rank, scalar),
            offsets=(sequence_offset, scalar),
        )
        for name, value in small.items():
            inputs[name + "_any"] = (value, anywhere)
        kept = dict(
            gwin=((in_rows, D), BF16),
            gwout=((LANES, D), BF16),
            gwup=((D, hidden), BF16),
            gwdn=((down_rows, D), BF16),
            pay_total=((PAY_ROWS, LANES), F32),
            late_total=((8, LANES), F32),
            shards=((group * SHARD_ROWS, LANES), F32),
            par_wide=((8, WIDE), F32),
            par_close=((8, 3 * channels), F32),
        )
        outputs = dict(block_any=((rows, D), BF16), input_any=((rows, D), BF16))
        for name, kind in kept.items():
            outputs[name + "_out"] = kind
        sizes = types.SimpleNamespace(
            ranks=ranks,
            halves=halves,
            inner=n_mp // 4,
            rows=rows,
            channels=channels,
            hidden=hidden,
            sequences=sequence_lengths.shape[0],
            loads=list(small),
            late_loads=("features", "waves", "unwaves"),
            stores=list(kept),
        )
        dma = pltpu.SemaphoreType.DMA
        scratch = {}

        def hold(**held):
            for name, kind in held.items():
                scratch[name] = pltpu.VMEM(*kind)

        for name, value in small.items():
            scratch[name] = pltpu.VMEM(value.shape, value.dtype)
        for name, kind in kept.items():
            scratch[name] = pltpu.VMEM(*kind)
        hold(x_in=((rows, D), BF16))
        hold(unit=((rows, D), F32))
        hold(scale=((rows, LANES), F32))
        hold(par_own=((8, WIDE), F32))
        hold(par_in=((8, WIDE), F32))
        hold(par_grad=((8, WIDE), F32))
        hold(taps=((8, WIDE), F32))
        hold(win=((3 * channels, D), BF16))
        hold(win_apart=((WIDE, D), BF16))
        hold(wout=((LANES, D), BF16))
        hold(wup=((D, hidden), BF16))
        hold(wdn=((hidden, D), BF16))
        hold(order=((3 * channels, WIDE), BF16))
        hold(order_wide=((3 * channels, WIDE), F32))
        hold(first=((FILT, LONG), F32))
        hold(first_sum=((FILT, LONG), F32))
        hold(first_cos=((FILT, LONG), F32))
        hold(second=((FILT, LONG), F32))
        hold(second_sum=((FILT, LONG), F32))
        hold(second_cos=((FILT, LONG), F32))
        hold(own_filter=((FILT, LANES), F32))
        hold(own_decay=((8, LANES), F32))
        hold(kernel=((LONG, LANES), F32))
        hold(raw_grad=((LONG, LANES), F32))
        hold(spread=((BINS, COUNT * LANES), BF16))
        hold(kernel_wave=((BINS, COUNT * LANES), F32))
        hold(signal_wave=((BINS, COUNT * LANES), F32))
        hold(grad_wave=((BINS, COUNT * LANES), F32))
        hold(product=((BINS, COUNT * LANES), BF16))
        hold(back_product=((2 * BINS, COUNT * LANES), BF16))
        hold(g_one=((LONG, D), BF16))
        hold(g_out=((LONG, D), BF16))
        hold(g_two=((LONG, D), BF16))
        hold(g_back=((LONG, D), BF16))
        hold(projected=((LONG, WIDE), F32))
        hold(short=((LONG, WIDE), F32))
        hold(short_grad=((LONG, WIDE), F32))
        hold(signal=((BLOCK, COUNT * LANES), BF16))
        hold(direct_low=((BLOCK, COUNT * LANES), BF16))
        hold(direct=((LONG, LANES), F32))
        hold(mixed=((LONG, LANES), BF16))
        hold(middle=((rows, D), F32))
        hold(middle_grad=((rows, D), F32))
        hold(input_grad=((rows, D), BF16))
        hold(block_out=((rows, D), BF16))
        hold(active=((LONG, hidden), BF16))
        hold(hidden_grad=((LONG, hidden), BF16))
        hold(projected_grad=((LONG, 3 * channels), BF16))
        hold(chip_out=((4, LONG // 2, D), BF16))
        hold(chip_in=((4, LONG // 2, D), BF16))
        hold(link_out=((4, LONG // 2, D), BF16))
        hold(link_in=((4, LONG // 2, D), BF16))
        for name, full in dict(
            _in=(in_rows, D), _out=(LANES, D), _up=(D, hidden), _dn=(down_rows, D)
        ).items():
            part = (full[0] // ranks, full[1])
            for kind, shape in dict(grad=full, part=part, y=(ranks,) + part, z=part).items():
                scratch[kind + name] = pltpu.VMEM(shape, BF16)
        hold(pay=((PAY_ROWS, LANES), F32))
        hold(pay_in=((PAY_ROWS // 2, LANES), F32))
        hold(pay_sum=((PAY_ROWS // 2, LANES), F32))
        hold(pay_held=((halves, PAY_ROWS // group, LANES), F32))
        hold(pay_cross=((2 * ranks, PAY_ROWS // group, LANES), F32))
        hold(late=((8, LANES), F32))
        hold(late_in=((8, LANES), F32))
        hold(late_held=((halves, 8, LANES), F32))
        hold(late_cross=((2 * ranks, 8, LANES), F32))
        hold(shard_y=((ranks, SHARD_ROWS, LANES), F32))
        hold(shard_q=((2, SHARD_ROWS, LANES), F32))
        for name, shape in dict(
            take=(7,),
            give=(2,),
            cut=(7, ranks),
            gather=(6, halves),
            hop=(6, halves),
            chip=(4, LONG // 2 // BLOCK),
            link=(4, halves),
            y=(4, ranks),
            z=(4,),
            out=(4, ranks),
            fin=(4, ranks),
            pay=(1,),
            paylink=(halves,),
            late=(halves,),
            sy=(ranks,),
            sq=(1,),
            cross=(2, 2 * ranks),
        ).items():
            scratch[name + "_send"] = dma(shape)
            scratch[name + "_recv"] = dma(shape)
        scratch["take_local"] = dma((7,))
        scratch["give_local"] = dma((2,))
        scratch["load_sem"] = dma((len(small),))
        scratch["store_sem"] = dma((len(kept),))
        names = list(inputs) + list(outputs) + list(scratch)
        results = pl.pallas_call(
            functools.partial(fused, sizes, names),
            out_shape=[jax.ShapeDtypeStruct(*kind) for kind in outputs.values()],
            in_specs=[i[1] for i in inputs.values()],
            out_specs=[anywhere for _ in outputs],
            scratch_shapes=list(scratch.values()),
            compiler_params=pltpu.CompilerParams(
                collective_id=0,
                has_side_effects=True,
                vmem_limit_bytes=60 * 2**20,
            ),
            name="block",
        )(*[i[0] for i in inputs.values()])
        finals = dict(
            gwin_wide=(3 * channels, D),
            gwout_wide=(channels, D),
            gwup_wide=(D, hidden),
            gwdn_wide=(hidden, D),
            input_wide=(rows, D),
            mixer_gain=(D,),
            in_bias=(3 * channels,),
            short_taps=(3, 3 * channels),
            skip_gain=(channels,),
            out_bias=(D,),
            ffn_gain=(D,),
            up_bias=(hidden,),
            down_bias=(D,),
            embed_weight=(EMB, FILT),
            embed_bias=(FILT,),
            embed_freq=(FILT,),
            hidden_weight=(FILT, FILT),
            hidden_bias=(FILT,),
            hidden_freq=(FILT,),
            filter_weight=(FILT, D),
            decay_rate=(D,),
        )
        loads = ["block", "input"] + list(kept)
        closing = types.SimpleNamespace(
            halves=halves, channels=channels, hidden=hidden, loads=loads, stores=list(finals)
        )
        scratch = dict(
            block=pltpu.VMEM((rows, D), BF16),
            input=pltpu.VMEM((rows, D), BF16),
            decay_row=pltpu.VMEM((8, D), F32),
        )
        for name, kind in kept.items():
            scratch[name] = pltpu.VMEM(*kind)
        for name, shape in finals.items():
            scratch[name] = pltpu.VMEM(shape, F32)
        scratch["load_sem"] = dma((len(loads),))
        scratch["store_sem"] = dma((len(finals),))
        scratch["block_sem"] = dma
        names = [name + "_any" for name in loads] + ["block_out"]
        names += [name + "_out" for name in finals] + ["penalty_out"] + list(scratch)
        done = pl.pallas_call(
            functools.partial(close, closing, names),
            out_shape=[jax.ShapeDtypeStruct((rows, D), BF16)]
            + [jax.ShapeDtypeStruct(shape, F32) for shape in finals.values()]
            + [jax.ShapeDtypeStruct((1,), F32)],
            in_specs=[anywhere] * len(loads),
            out_specs=[anywhere] * (1 + len(finals)) + [scalar],
            scratch_shapes=list(scratch.values()),
            compiler_params=pltpu.CompilerParams(vmem_limit_bytes=60 * 2**20),
            name="close",
        )(*results)
        out = types.SimpleNamespace(**dict(zip(finals, done[1:-1])))
        return (
            done[0],
            out.input_wide,
            done[-1].reshape(()),
            out.mixer_gain,
            out.gwin_wide.T,
            out.in_bias,
            out.short_taps,
            out.skip_gain,
            out.gwout_wide,
            out.out_bias,
            out.ffn_gain,
            out.gwup_wide,
            out.up_bias,
            out.gwdn_wide,
            out.down_bias,
            out.embed_weight,
            out.embed_bias,
            out.embed_freq,
            out.hidden_weight,
            out.hidden_bias,
            out.hidden_freq,
            out.filter_weight,
            out.decay_rate,
        )

    placed = (
        P(("dp", "mp"), None),
        P(),
        P(None, "mp"),
        P("mp"),
        P(None, "mp"),
        P("mp"),
        P("mp", None),
        P(),
        P(),
        P(None, "mp"),
        P("mp"),
        P("mp", None),
        P(),
        P(),
        P(),
        P(),
        P(),
        P(),
        P(),
        P(),
        P(),
        P(("dp", "mp"), None),
        P(),
        P(),
        P(),
    )
    return jax.shard_map(
        per_device,
        mesh=mesh,
        in_specs=placed,
        out_specs=(
            P(("dp", "mp"), None),
            P(("dp", "mp"), None),
            P(),
            P(),
            P(None, "mp"),
            P("mp"),
            P(None, "mp"),
            P("mp"),
            P("mp", None),
            P(),
            P(),
            P(None, "mp"),
            P("mp"),
            P("mp", None),
            P(),
            P(),
            P(),
            P(),
            P(),
            P(),
            P(),
            P(),
            P(),
        ),
        check_vma=False,
    )
```

```python
import functools
import math
import types

import jax
import jax.numpy as jnp
import numpy as np
from jax import lax
from jax.experimental import pallas as pl
from jax.experimental.pallas import tpu as pltpu
from jax.sharding import PartitionSpec as P

D = 768
BANDS = 16
EMB = 2 * BANDS + 1
FILT = 64
LONG = 1024
BLOCK = 256
BINS = 2 * BLOCK
COUNT = LONG // BLOCK
LANES = 128
WIDE = 3 * LANES
MESH = pl.DeviceIdType.MESH
BF16 = jnp.bfloat16
F32 = jnp.float32
EPS = 1e-05
ROOT = math.sqrt(2.0 / math.pi)
CUBE = 0.044715

PAY_VEC, PAY_HID, PAY_EMB, PAY_PEN, PAY_ROWS = 0, 24, 88, 121, 128
SHARD_DECAY, SHARD_PAR, SHARD_ROWS = 64, 72, 96


def wave_table(shift):
    bins = np.arange(BLOCK)[:, None]
    angle = np.pi * (2 * bins + 1) * (np.arange(BLOCK)[None, :] + shift) / BINS
    return np.concatenate([np.cos(angle), -np.sin(angle)], 0)


NEAR, FAR = wave_table(0), wave_table(-BLOCK)
WAVES = np.concatenate([NEAR, FAR], 1)
UNWAVES = np.concatenate([NEAR.T, FAR.T], 1) / BLOCK


def position_features():
    tau = np.arange(LONG) / LONG
    angles = 2.0 * np.pi * np.arange(1, BANDS + 1)[:, None] * tau[None, :]
    return np.concatenate([tau[None, :], np.cos(angles), np.sin(angles)], 0)


def dot(left, right, dims=((1,), (0,)), precision=None):
    return lax.dot_general(
        left, right, (dims, ((), ())), precision=precision, preferred_element_type=F32
    )


def dot_nt(left, right, precision=None):
    return dot(left, right, ((1,), (1,)), precision)


def dot_tn(left, right, precision=None):
    return dot(left, right, ((0,), (0,)), precision)


HIGH = lax.Precision.HIGHEST


def sin_cos(angle):
    turns = jnp.floor(angle * (2.0 / math.pi) + 0.5)
    rest = angle - turns * 1.5703125
    rest = rest - turns * 4.837512969970703125e-4
    rest = rest - turns * 7.54978995489188e-8
    square = rest * rest
    sine = rest + rest * square * (
        -1.6666654611e-1 + square * (8.3321608736e-3 + square * -1.9515295891e-4)
    )
    cosine = (
        1.0
        - 0.5 * square
        + square
        * square
        * (4.166664568298827e-2 + square * (-1.388731625493765e-3 + square * 2.443315711809948e-5))
    )
    half = jnp.floor(turns * 0.5)
    odd = turns - 2.0 * half
    sign = 1.0 - 2.0 * (half - 2.0 * jnp.floor(half * 0.5))
    swapped = odd > 0.5
    return (
        jnp.where(swapped, cosine, sine) * sign,
        jnp.where(swapped, -sine, cosine) * sign,
    )


def norm_parts(values):
    center = values - jnp.mean(values, axis=-1, keepdims=True)
    scale = lax.rsqrt(jnp.mean(center * center, axis=-1, keepdims=True) + EPS)
    return center * scale, scale


def norm_back(grad, gain, unit, scale):
    inner = grad * gain
    return scale * (
        inner
        - jnp.mean(inner, axis=-1, keepdims=True)
        - unit * jnp.mean(inner * unit, axis=-1, keepdims=True)
    )


def column(row):
    size = row.shape[1]
    same = lax.broadcasted_iota(jnp.int32, (size, size), 0) == lax.broadcasted_iota(
        jnp.int32, (size, size), 1
    )
    return jnp.sum(jnp.where(same, row, 0.0), axis=1, keepdims=True)


def fused(s, names, *refs):
    r = types.SimpleNamespace(**dict(zip(names, refs)))
    ranks, halves, inner, rows = s.ranks, s.halves, s.inner, s.rows
    channels, hidden = s.channels, s.hidden
    dp, mp = lax.axis_index("dp"), lax.axis_index("mp")
    y, c = dp // 2, dp % 2
    q, j = mp // halves, mp % halves
    other, across = 1 - c, 1 - q
    outer = halves // inner

    def device(yy, cc, qq, jj):
        return (yy * 2 + cc, qq * halves + jj)

    def ahead(k):
        return ((j // inner + k // inner) % outer) * inner + (j % inner + k % inner) % inner

    def behind(k):
        return ((j // inner + outer - k // inner) % outer) * inner + (
            j % inner + inner - k % inner
        ) % inner

    sibling = device(y, other, q, j)
    partner = device(y, other, across, j)
    moved = c != q

    def remote(src, dst, send, recv, target):
        return pltpu.make_async_remote_copy(
            src_ref=src,
            dst_ref=dst,
            send_sem=send,
            recv_sem=recv,
            device_id=target,
            device_id_type=MESH,
        )

    def block_rows(cc, jj):
        return pl.ds(pl.multiple_of((cc * halves + jj) * rows, rows), rows)

    mine = block_rows(c, j)

    barrier = pltpu.get_barrier_semaphore()
    greeted = [sibling, partner]
    for k in range(1, halves):
        greeted += [device(y, c, q, ahead(k)), device(y, other, q, ahead(k))]
    for dy in range(ranks):
        for dq in range(2):
            if dy or dq:
                greeted.append(device((y + dy) % ranks, c, (q + dq) % 2, j))
    for target in greeted:
        pl.semaphore_signal(barrier, inc=1, device_id=target, device_id_type=MESH)

    def load(name):
        i = s.loads.index(name)
        return pltpu.make_async_copy(
            getattr(r, name + "_any"), getattr(r, name), r.load_sem.at[i]
        )

    pl.semaphore_wait(barrier, len(greeted))

    par = r.par_own
    theirs = block_rows(other, j)
    x, own_par, w_in, grads, w_out, w_up, w_down = range(7)
    takes = [
        (r.x_any, r.x_in, r.x_in),
        (par, r.par_in, r.par_in),
        (r.win_any, r.win, r.win),
        (r.og_any, r.g_out.at[theirs], r.g_out.at[mine]),
        (r.wout_any, r.wout.at[pl.ds(0, channels)], r.wout.at[pl.ds(0, channels)]),
        (r.wup_any, r.wup, r.wup),
        (r.wdn_any, r.wdn, r.wdn),
    ]
    owner = jnp.logical_not(moved)

    def cut_rows(i, yy):
        size = takes[i][0].shape[0] // ranks
        return pl.ds(pl.multiple_of(yy * size, 16), size)

    def in_parts(i):
        return i in (w_in, w_up, w_down) and takes[i][0].shape[0] % (16 * ranks) == 0

    def take(i, arriving=False):
        src, dst, here = takes[i]
        dst = here if arriving else dst
        if in_parts(i):
            src, dst = src.at[cut_rows(i, y)], dst.at[cut_rows(i, y)]
        return remote(src, dst, r.take_send.at[i], r.take_recv.at[i], partner)

    def take_local(i):
        return pltpu.make_async_copy(takes[i][0], takes[i][2], r.take_local.at[i])

    def pass_copy(i, dy):
        at = takes[i][2].at[cut_rows(i, y)]
        return remote(
            at,
            at,
            r.cut_send.at[i, dy],
            r.cut_recv.at[i, dy],
            device((y + dy) % ranks, c, q, j),
        )

    def take_start(*which, after=()):
        @pl.when(moved)
        def _():
            for i in after:
                take(i).wait_send()
            for i in which:
                take(i).start()

    def take_pass(*which):
        @pl.when(moved)
        def _():
            for i in which:
                take(i, True).wait_recv()
                if in_parts(i):
                    for dy in range(1, ranks):
                        pass_copy(i, dy).start()

    def taken(*which):
        @pl.when(moved)
        def _():
            for i in which:
                if i not in (w_in, w_up, w_down):
                    take(i, True).wait_recv()
                elif in_parts(i):
                    for dy in range(1, ranks):
                        at = takes[i][2].at[cut_rows(i, (y + ranks - dy) % ranks)]
                        remote(
                            at,
                            at,
                            r.cut_send.at[i, dy],
                            r.cut_recv.at[i, dy],
                            device((y + ranks - dy) % ranks, c, q, j),
                        ).wait_recv()
                        pass_copy(i, dy).wait_send()

        @pl.when(owner)
        def _():
            for i in which:
                take_local(i).wait()

    take_start(x)
    @pl.when(owner)
    def _():
        for i in range(len(takes)):
            if i != own_par:
                take_local(i).start()

    for name in s.loads:
        load(name).start()
    for name in s.loads:
        if name not in s.late_loads:
            load(name).wait()

    def line(ref):
        return jnp.reshape(ref[...], (1, ref.shape[0]))

    par[...] = jnp.zeros_like(par)
    par[0:1, 0 : 3 * channels] = line(r.in_bias)
    par[1:4, 0 : 3 * channels] = r.short_taps[...]
    par[4:5, 0:channels] = line(r.skip_gain)
    par[5:6, 0:hidden] = line(r.up_bias).astype(F32)

    @pl.when(owner)
    def _():
        take_local(own_par).start()

    def seat(n, cc, jj):
        size = PAY_ROWS // (2 * halves) if n == 5 else SHARD_ROWS if n == 4 else rows
        return pl.ds(pl.multiple_of((cc * halves + jj) * size, size), size)

    def gather_copies(n, held):
        mine = seat(n, c, j)
        out = []
        for k in range(1, halves):
            out.append(
                remote(
                    held.at[mine],
                    held.at[mine],
                    r.gather_send.at[n, k],
                    r.gather_recv.at[n, k],
                    device(y, c, q, ahead(k)),
                )
            )
        out.append(
            remote(
                held.at[mine],
                held.at[mine],
                r.gather_send.at[n, 0],
                r.gather_recv.at[n, 0],
                sibling,
            )
        )
        return out

    def gather_start(n, held):
        for copy in gather_copies(n, held):
            copy.start()

    def gather_finish(n, held):
        forwards = []
        for k in range(1, halves):
            came = held.at[seat(n, c, behind(k))]
            remote(
                came,
                came,
                r.gather_send.at[n, k],
                r.gather_recv.at[n, k],
                device(y, c, q, behind(k)),
            ).wait_recv()
            forward = remote(
                came, came, r.hop_send.at[n, k], r.hop_recv.at[n, k], sibling
            )
            forward.start()
            forwards.append(forward)
        for k in range(halves):
            came = held.at[seat(n, other, behind(k))]
            recv = r.hop_recv.at[n, k] if k else r.gather_recv.at[n, 0]
            remote(came, came, r.hop_send.at[n, k], recv, sibling).wait_recv()
        for copy in gather_copies(n, held) + forwards:
            copy.wait_send()

    def first_norm():
        unit, _ = norm_parts(r.x_in[...].astype(F32))
        r.g_one[mine, :] = (unit * line(r.mixer_gain)).astype(BF16)
        gather_start(0, r.g_one)

    @pl.when(owner)
    def _():
        take_local(x).wait()
        first_norm()
        take_local(grads).wait()
        gather_start(1, r.g_out)

    pack = y * 2 + q
    segments = []
    for i in range(COUNT):
        found = jnp.int32(-1)
        for k in range(s.sequences):
            start = r.offsets[k]
            hit = (
                (r.owners[k] == pack)
                & (start <= i * BLOCK)
                & (start + r.lengths[k] > i * BLOCK)
            )
            found = jnp.where(hit, jnp.int32(k), found)
        segments.append(found)
    valid = [jnp.where(seg >= 0, jnp.float32(1), jnp.float32(0)) for seg in segments]
    joined = [
        [valid[i] * jnp.where(segments[i] == segments[p], jnp.float32(1), jnp.float32(0)) for p in range(i + 1)]
        for i in range(COUNT)
    ]
    follows = [jnp.float32(0)] + [joined[i][i - 1] for i in range(1, COUNT)]

    row_index = lax.broadcasted_iota(jnp.int32, (3 * channels, WIDE), 0)
    lane_index = lax.broadcasted_iota(jnp.int32, (3 * channels, WIDE), 1)
    within = lane_index % LANES
    order = jnp.where(
        (row_index == 3 * within + lane_index // LANES) & (within < channels), 1.0, 0.0
    )
    r.order[...] = order.astype(BF16)
    r.order_wide[...] = order

    load("features").wait()
    features = r.features[...]
    embed_freq, embed_bias = column(line(r.embed_freq)), column(line(r.embed_bias))
    hidden_freq, hidden_bias = column(line(r.hidden_freq)), column(line(r.hidden_bias))
    first_sum = dot_tn(r.embed_weight[...], features, HIGH) + embed_bias
    first, first_cos = sin_cos(embed_freq * first_sum)
    r.first_sum[...] = first_sum
    r.first[...] = first
    r.first_cos[...] = first_cos
    take_start(w_in, own_par, after=(x,))
    second_sum = dot_tn(r.hidden_weight[...], first, HIGH) + hidden_bias
    second, second_cos = sin_cos(hidden_freq * second_sum)
    r.second_sum[...] = second_sum
    r.second[...] = second
    r.second_cos[...] = second_cos
    half_rows = LONG // 2
    chunks = half_rows // BLOCK
    per_chunk = BLOCK // rows

    def half_chunk(cc, t):
        return pl.ds(pl.multiple_of(cc * half_rows + t * BLOCK, BLOCK), BLOCK)

    def chunk_rows(t):
        return pl.ds(pl.multiple_of(t * BLOCK, BLOCK), BLOCK)

    def place(jj):
        return pl.ds(pl.multiple_of(jj * rows, rows), rows)

    def chip_copy(n, t):
        return remote(
            r.chip_out.at[n, chunk_rows(t)],
            r.chip_in.at[n, chunk_rows(t)],
            r.chip_send.at[n, t],
            r.chip_recv.at[n, t],
            sibling,
        )

    def link_copy(n, jj):
        return remote(
            r.link_out.at[n, place(jj)],
            r.link_in.at[n, place(j)],
            r.link_send.at[n, jj],
            r.link_recv.at[n, j],
            device(y, c, q, jj),
        )

    def chip_give(n, t, value):
        r.chip_out[n, chunk_rows(t), :] = value.astype(BF16)
        chip_copy(n, t).start()

    def chip_add(n, t, value):
        chip_copy(n, t).wait_recv()
        r.link_out[n, chunk_rows(t), :] = (
            value + r.chip_in[n, chunk_rows(t), :].astype(F32)
        ).astype(BF16)

    def link_start(n, t):
        for i in range(per_chunk):
            jj = t * per_chunk + i

            @pl.when(jj != j)
            def _():
                link_copy(n, jj).start()

    def scatter(n, part):
        def give(t, carry):
            chip_give(n, t, part(half_chunk(other, t)))
            return carry

        lax.fori_loop(0, chunks, give, 0)

        def send(t, carry):
            chip_add(n, t, part(half_chunk(c, t)))
            link_start(n, t)
            return carry

        lax.fori_loop(0, chunks, send, 0)

    def scatter_finish(n):
        total = r.link_out[n, place(j), :].astype(F32)
        for k in range(1, halves):
            jj = behind(k)
            came = r.link_in.at[n, place(jj)]
            remote(
                came, came, r.link_send.at[n, jj], r.link_recv.at[n, jj], device(y, c, q, jj)
            ).wait_recv()
            total = total + r.link_in[n, place(jj), :].astype(F32)
        for t in range(chunks):
            chip_copy(n, t).wait_send()
        for k in range(1, halves):
            link_copy(n, ahead(k)).wait_send()
        return total

    @pl.when(moved)
    def _():
        take(x, True).wait_recv()
        first_norm()

    shard = c * halves + j
    pick_row = lax.broadcasted_iota(jnp.int32, (D, LANES), 0)
    pick_lane = lax.broadcasted_iota(jnp.int32, (D, LANES), 1)
    pick = jnp.where((pick_row == shard * channels + pick_lane) & (pick_lane < channels), 1.0, 0.0)
    own_filter = dot(r.filter_weight[...], pick, precision=HIGH)
    own_decay = dot(jnp.broadcast_to(line(r.decay_rate), (8, D)), pick, precision=HIGH)[0:1]
    r.own_filter[...] = own_filter
    r.own_decay[...] = jnp.broadcast_to(own_decay, (8, LANES))
    r.spread[...] = jnp.zeros_like(r.spread)
    for i in range(COUNT):
        at = slice(i * BLOCK, (i + 1) * BLOCK)
        tau = (
            lax.broadcasted_iota(jnp.int32, (BLOCK, LANES), 0) + i * BLOCK
        ).astype(F32) * (1.0 / LONG)
        kernel = dot_tn(second[:, at], own_filter, HIGH) * jnp.exp(-tau * own_decay)
        r.kernel[at, :] = kernel
        low = kernel.astype(BF16)
        r.spread[0:BLOCK, i * LANES : (i + 1) * LANES] = low
        if i + 1 < COUNT:
            r.spread[BLOCK:BINS, (i + 1) * LANES : (i + 2) * LANES] = low
    take_start(grads, w_out, after=(w_in, own_par))
    take_pass(w_in)
    load("waves").wait()
    load("unwaves").wait()
    r.kernel_wave[...] = dot(r.waves[...], r.spread[...])
    gather_finish(0, r.g_one)

    @pl.when(moved)
    def _():
        take(grads, True).wait_recv()
        gather_start(1, r.g_out)

    take_start(w_up, w_down, after=(grads,))
    taken(own_par, w_in)
    par_wide = dot(r.par_in[:, 0 : 3 * channels], r.order_wide[...], precision=HIGH)
    r.taps[...] = par_wide
    r.win_apart[...] = dot_tn(r.order[...], r.win[...]).astype(BF16)
    r.wout[channels:, :] = jnp.zeros_like(r.wout[channels:, :])

    def project(i, carry):
        at = pl.ds(pl.multiple_of(i * BINS, BINS), BINS)
        r.projected[at, :] = dot_nt(r.g_one[at, :], r.win_apart[...]) + r.taps[0:1, :]
        return carry

    lax.fori_loop(0, LONG // BINS, project, 0)

    rows_here = lax.broadcasted_iota(jnp.int32, (BLOCK, 1), 0)

    def back_rows(i):
        now = r.projected[i * BLOCK : (i + 1) * BLOCK, :]
        one, two = pltpu.roll(now, 1, 0), pltpu.roll(now, 2, 0)
        if i:
            edge = r.projected[i * BLOCK - 8 : i * BLOCK, :] * follows[i]
            last, before = edge[7:8], edge[6:7]
        else:
            last = before = jnp.zeros((1, WIDE), F32)
        one = jnp.where(rows_here == 0, last, one)
        two = jnp.where(rows_here == 0, before, jnp.where(rows_here == 1, last, two))
        return now, one, two

    for i in range(COUNT):
        now, one, two = back_rows(i)
        short = r.taps[1:2, :] * now + r.taps[2:3, :] * one + r.taps[3:4, :] * two
        r.short[i * BLOCK : (i + 1) * BLOCK, :] = short
        signal = short[:, 2 * LANES :] * short[:, LANES : 2 * LANES] * valid[i]
        r.signal[:, i * LANES : (i + 1) * LANES] = signal.astype(BF16)

    near = r.waves[:, 0:BLOCK]
    unnear = r.unwaves[:, 0:BINS]
    r.signal_wave[...] = dot(near, r.signal[...])
    step = 16

    def load_wave(ref, at, count=COUNT):
        low, high = pl.ds(at, step), pl.ds(at + BLOCK, step)
        return [
            (ref[low, i * LANES : (i + 1) * LANES], ref[high, i * LANES : (i + 1) * LANES])
            for i in range(count)
        ]

    def store_wave(ref, base, at, i, pair):
        ref[pl.ds(base + at, step), i * LANES : (i + 1) * LANES] = pair[0].astype(BF16)
        ref[pl.ds(base + at + BLOCK, step), i * LANES : (i + 1) * LANES] = pair[1].astype(BF16)

    def weighted(terms):
        real = imag = None
        for weight, (a, b) in terms:
            real = a * weight if real is None else real + a * weight
            imag = b * weight if imag is None else imag + b * weight
        return real, imag

    def times(left, right):
        return left[0] * right[0] - left[1] * right[1], left[0] * right[1] + left[1] * right[0]

    def times_conj(left, right):
        return left[0] * right[0] + left[1] * right[1], left[0] * right[1] - left[1] * right[0]

    def forward_wave(n, carry):
        at = pl.multiple_of(n * step, step)
        kernels, signals = load_wave(r.kernel_wave, at), load_wave(r.signal_wave, at)
        for i in range(COUNT):
            store_wave(
                r.product,
                0,
                at,
                i,
                weighted([(joined[i][p], times(kernels[i - p], signals[p])) for p in range(i + 1)]),
            )
        return carry

    lax.fori_loop(0, BLOCK // step, forward_wave, 0)
    skip = r.par_in[4:5, 0:LANES]
    convolved = dot(unnear, r.product[0:BINS, :])
    for i in range(COUNT):
        at = slice(i * BLOCK, (i + 1) * BLOCK)
        lanes = slice(i * LANES, (i + 1) * LANES)
        direct = convolved[:, lanes] + skip * r.signal[:, lanes].astype(F32)
        r.direct[at, :] = direct
        r.mixed[at, :] = (direct * r.short[at, 0:LANES]).astype(BF16)

    taken(w_out)
    scatter(0, lambda at: dot(r.mixed[at, :], r.wout[...]))
    take_pass(w_up)
    middle = r.x_in[...].astype(F32) + line(r.out_bias) + scatter_finish(0)
    unit, scale = norm_parts(middle)
    r.g_two[mine, :] = (unit * line(r.ffn_gain)).astype(BF16)
    gather_start(2, r.g_two)
    r.middle[...] = middle
    r.unit[...] = unit
    r.scale[...] = jnp.broadcast_to(scale, r.scale.shape)
    take_pass(w_down)
    gather_finish(1, r.g_out)
    gather_finish(2, r.g_two)
    taken(w_up, w_down)

    def feed(at):
        value = dot(r.g_two[at, :], r.wup[...]) + r.par_in[5:6, 0:hidden]
        square = value * value
        bend = jnp.tanh(ROOT * value * (1.0 + CUBE * square))
        half = 0.5 * (1.0 + bend)
        active = (value * half).astype(BF16)
        slope = half + 0.5 * value * (1.0 - bend * bend) * (ROOT * (1.0 + 3.0 * CUBE * square))
        grad = (slope * dot_nt(r.g_out[at, :], r.wdn[...])).astype(BF16)
        r.active[at, :] = active
        r.hidden_grad[at, :] = grad
        return dot_nt(grad, r.wup[...])

    def feed_step(i, carry):
        t, own = i // 2, i % 2
        back = feed(half_chunk(own * c + (1 - own) * other, t))

        @pl.when(own == 0)
        def _():
            chip_give(1, t, back)

        @pl.when(own == 1)
        def _():
            chip_add(1, t, back)
            link_start(1, t)

        return carry

    lax.fori_loop(0, 2 * chunks, feed_step, 0)

    def down(at):
        return dot(r.active[at, :], r.wdn[...])

    def down_give(t, carry):
        chip_give(2, t, down(half_chunk(other, t)))
        return carry

    def down_add(t, carry):
        chip_add(2, t, down(half_chunk(c, t)))
        return carry

    lax.fori_loop(0, chunks, down_give, 0)

    sums = [
        (r.grad_in, r.part_in, r.y_in, r.z_in, r.gwin),
        (r.grad_out, r.part_out, r.y_out, r.z_out, r.gwout),
        (r.grad_up, r.part_up, r.y_up, r.z_up, r.gwup),
        (r.grad_dn, r.part_dn, r.y_dn, r.z_dn, r.gwdn),
    ]
    def part_rows(ref, yy):
        size = ref.shape[0] // ranks
        return pl.ds(pl.multiple_of(yy * size, 16), size)

    def y_copy(w, dy):
        full, _, came, _, _ = sums[w]
        to = (y + dy) % ranks
        return remote(
            full.at[part_rows(full, to)],
            came.at[dy],
            r.y_send.at[w, dy],
            r.y_recv.at[w, dy],
            device(to, c, q, j),
        )

    def z_copy(w):
        _, part, _, came, _ = sums[w]
        return remote(
            part, came, r.z_send.at[w], r.z_recv.at[w], device(y, c, across, j)
        )

    def out_copy(w, dy):
        final = sums[w][4]
        at = part_rows(final, y)
        return remote(
            final.at[at],
            final.at[at],
            r.out_send.at[w, dy],
            r.out_recv.at[w, dy],
            device((y + dy) % ranks, c, q, j),
        )

    def chip_final(w, dy):
        final = sums[w][4]
        at = part_rows(final, (y + ranks - dy) % ranks)
        return remote(
            final.at[at],
            final.at[at],
            r.fin_send.at[w, dy],
            r.fin_recv.at[w, dy],
            sibling,
        )

    def sum_start(w):
        for dy in range(1, ranks):
            y_copy(w, dy).start()

    def sum_cross(w):
        full, part, came, _, _ = sums[w]
        total = full[part_rows(full, y), :].astype(F32)
        for dy in range(1, ranks):
            y_copy(w, dy).wait_recv()
            total = total + came[dy].astype(F32)
        part[...] = total.astype(BF16)

        @pl.when(moved)
        def _():
            z_copy(w).start()

    def sum_close(w):
        _, part, _, came, final = sums[w]

        @pl.when(owner)
        def _():
            z_copy(w).wait_recv()
            final[part_rows(final, y), :] = (
                part[...].astype(F32) + came[...].astype(F32)
            ).astype(BF16)
            for dy in range(1, ranks):
                out_copy(w, dy).start()
            chip_final(w, 0).start()

    def sum_finish(w):
        final = sums[w][4]

        @pl.when(owner)
        def _():
            for dy in range(1, ranks):
                at = part_rows(final, (y + ranks - dy) % ranks)
                remote(
                    final.at[at],
                    final.at[at],
                    r.out_send.at[w, dy],
                    r.out_recv.at[w, dy],
                    sibling,
                ).wait_recv()
                chip_final(w, dy).start()
            for dy in range(1, ranks):
                out_copy(w, dy).wait_send()
            for dy in range(ranks):
                chip_final(w, dy).wait_send()

        @pl.when(moved)
        def _():
            for dy in range(ranks):
                chip_final(w, dy).wait_recv()
            z_copy(w).wait_send()

        for dy in range(1, ranks):
            y_copy(w, dy).wait_send()

    def weight_grad(target, left, right, by_right=False):
        def chunk(i, carry):
            at = pl.ds(pl.multiple_of(i * BLOCK, BLOCK), BLOCK)
            if by_right:
                target[0 : left.shape[1], at] = dot_tn(left[...], right[:, at]).astype(BF16)
            else:
                target[at, :] = dot_tn(left[:, at], right[...]).astype(BF16)
            return carry

        lax.fori_loop(0, D // BLOCK, chunk, 0)

    for grad, size in ((r.grad_dn, hidden), (r.grad_in, 3 * channels)):
        if grad.shape[0] > size:
            grad[size:, :] = jnp.zeros_like(grad[size:, :])
    weight_grad(r.grad_dn, r.active, r.g_out, True)
    sum_start(3)
    weight_grad(r.grad_up, r.g_two, r.hidden_grad)
    sum_start(2)
    lax.fori_loop(0, chunks, down_add, 0)

    seed = r.g_out[mine, :].astype(F32)
    ffn_back = scatter_finish(1)
    unit, scale = r.unit[...], jnp.concatenate([r.scale[...]] * (D // LANES), axis=1)
    middle_grad = seed + norm_back(ffn_back, line(r.ffn_gain), unit, scale)
    r.middle_grad[...] = middle_grad
    branch_grad = middle_grad.astype(BF16)
    r.g_back[mine, :] = branch_grad
    gather_start(3, r.g_back)
    vectors = [
        jnp.sum(ffn_back * unit, axis=0, keepdims=True),
        jnp.sum(branch_grad.astype(F32), axis=0, keepdims=True),
        jnp.sum(seed, axis=0, keepdims=True),
    ]
    r.pay[...] = jnp.zeros_like(r.pay)
    for v, vector in enumerate(vectors):
        for k in range(D // LANES):
            at = PAY_VEC + v * (D // LANES) + k
            r.pay[at : at + 1, :] = vector[:, k * LANES : (k + 1) * LANES]
    par_grad = r.par_grad
    par_grad[...] = jnp.zeros_like(par_grad)
    par_grad[5:6, 0:hidden] = jnp.sum(r.hidden_grad[...].astype(F32), axis=0, keepdims=True)
    sum_cross(3)
    sum_cross(2)
    gather_finish(3, r.g_back)
    for t in range(chunks):
        link_start(2, t)
    r.grad_out[...] = dot_tn(r.mixed[...], r.g_back[...]).astype(BF16)
    sum_start(1)

    skip_total = jnp.zeros((1, LANES), F32)
    for i in range(COUNT):
        at = slice(i * BLOCK, (i + 1) * BLOCK)
        lanes = slice(i * LANES, (i + 1) * LANES)
        mixed_grad = dot_nt(r.g_back[at, :], r.wout[...])
        r.short_grad[at, 0:LANES] = mixed_grad * r.direct[at, :]
        direct_grad = mixed_grad * r.short[at, 0:LANES]
        r.direct[at, :] = direct_grad
        r.direct_low[:, lanes] = direct_grad.astype(BF16)
        skip_total += jnp.sum(
            direct_grad * r.signal[:, lanes].astype(F32), axis=0, keepdims=True
        )
    par_grad[4:5, 0:LANES] = skip_total
    r.grad_wave[...] = dot(near, r.direct_low[...])
    r.back_product[...] = jnp.zeros_like(r.back_product)

    def backward_wave(n, carry):
        at = pl.multiple_of(n * step, step)
        kernels, signals = load_wave(r.kernel_wave, at), load_wave(r.signal_wave, at)
        grads = load_wave(r.grad_wave, at)
        for p in range(COUNT):
            terms = [(joined[i][p], times_conj(kernels[i - p], grads[i])) for i in range(p, COUNT)]
            store_wave(r.product, 0, at, p, weighted(terms))
        for d in range(COUNT):
            terms = [
                (joined[i][i - d], times_conj(signals[i - d], grads[i])) for i in range(d, COUNT)
            ]
            pair = weighted(terms)
            store_wave(r.back_product, 0, at, d, pair)
            if d:
                store_wave(r.back_product, BINS, at, d - 1, pair)
        return carry

    lax.fori_loop(0, BLOCK // step, backward_wave, 0)
    signal_grads = dot(unnear, r.product[0:BINS, :])
    for i in range(COUNT):
        at = slice(i * BLOCK, (i + 1) * BLOCK)
        lanes = slice(i * LANES, (i + 1) * LANES)
        signal_grad = (signal_grads[:, lanes] + skip * r.direct[at, :]) * valid[i]
        r.short_grad[at, LANES : 2 * LANES] = signal_grad * r.short[at, 2 * LANES :]
        r.short_grad[at, 2 * LANES :] = signal_grad * r.short[at, LANES : 2 * LANES]

    bias_total = jnp.zeros((1, WIDE), F32)
    tap_totals = [jnp.zeros((1, WIDE), F32) for _ in range(3)]
    for i in range(COUNT):
        at = slice(i * BLOCK, (i + 1) * BLOCK)
        now, one, two = back_rows(i)
        grad = r.short_grad[at, :]
        for t, value in enumerate((now, one, two)):
            tap_totals[t] += jnp.sum(grad * value, axis=0, keepdims=True)
        next_one = pltpu.roll(grad, BLOCK - 1, 0)
        next_two = pltpu.roll(grad, BLOCK - 2, 0)
        if i + 1 < COUNT:
            edge = r.short_grad[(i + 1) * BLOCK : (i + 1) * BLOCK + 8, :] * follows[i + 1]
            head, after = edge[0:1], edge[1:2]
        else:
            head = after = jnp.zeros((1, WIDE), F32)
        next_one = jnp.where(rows_here == BLOCK - 1, head, next_one)
        next_two = jnp.where(
            rows_here == BLOCK - 2, head, jnp.where(rows_here == BLOCK - 1, after, next_two)
        )
        low = (
            r.taps[1:2, :] * grad + r.taps[2:3, :] * next_one + r.taps[3:4, :] * next_two
        ).astype(BF16)
        bias_total += jnp.sum(low.astype(F32), axis=0, keepdims=True)
        r.projected_grad[at, :] = dot_nt(low, r.order[...]).astype(BF16)
    par_grad[0:1, :] = bias_total
    for t in range(3):
        par_grad[t + 1 : t + 2, :] = tap_totals[t]

    sum_cross(1)

    r.gain_sum[...] = jnp.zeros_like(r.gain_sum)

    def normed_back(at):
        value = dot(r.projected_grad[at, :], r.win[...])
        weighed = value * r.g_one[at, :].astype(F32)
        r.gain_sum[...] += jnp.sum(jnp.reshape(weighed, (BLOCK // 8, 8, D)), axis=0)
        return value

    scatter(3, normed_back)

    weight_grad(r.grad_in, r.projected_grad, r.g_one, True)
    sum_start(0)

    kernel_grads = dot(r.unwaves[...], r.back_product[...])
    decay_total = jnp.zeros((1, LANES), F32)
    penalty = jnp.zeros((1, LANES), F32)
    own_filter = r.own_filter[...]
    own_decay = r.own_decay[0:1, :]
    lead = jnp.where(pack == 0, 1.0 / D, 0.0).astype(F32)
    for i in range(COUNT):
        at = slice(i * BLOCK, (i + 1) * BLOCK)
        tau = (
            lax.broadcasted_iota(jnp.int32, (BLOCK, LANES), 0) + i * BLOCK
        ).astype(F32) * (1.0 / LONG)
        kernel = r.kernel[at, :]
        weighed = tau * kernel
        penalty += jnp.sum(weighed * kernel, axis=0, keepdims=True) * lead
        kernel_grad = (
            kernel_grads[:, i * LANES : (i + 1) * LANES] + weighed * (2.0 * lead)
        )
        decay_total -= jnp.sum(kernel_grad * weighed, axis=0, keepdims=True)
        r.raw_grad[at, :] = kernel_grad * jnp.exp(-tau * own_decay)
    sums_y, sums_q = r.shard_y, r.shard_q
    sums_y[y] = jnp.zeros((SHARD_ROWS, LANES), F32)
    sums_y[y, 0:FILT, :] = dot(r.second[...], r.raw_grad[...], precision=HIGH)
    sums_y[y, SHARD_DECAY : SHARD_DECAY + 1, :] = decay_total
    for k in range(3):
        at = SHARD_PAR + 8 * k
        sums_y[y, at : at + 8, :] = par_grad[:, k * LANES : (k + 1) * LANES]

    def shard_y(dy, back=False):
        at = sums_y.at[(y + ranks - dy) % ranks if back else y]
        return remote(
            at, at, r.sy_send.at[dy], r.sy_recv.at[dy], device((y + dy) % ranks, c, q, j)
        )

    def shard_q(back=False):
        at = sums_q.at[across if back else q]
        return remote(at, at, r.sq_send.at[0], r.sq_recv.at[0], device(y, c, across, j))

    for dy in range(1, ranks):
        shard_y(dy).start()
    r.pay[PAY_PEN : PAY_PEN + 1, :] = penalty
    gain_row = jnp.sum(r.gain_sum[...], axis=0, keepdims=True) / line(r.mixer_gain)
    for k in range(D // LANES):
        at = PAY_VEC + 3 * (D // LANES) + k
        r.pay[at : at + 1, :] = gain_row[:, k * LANES : (k + 1) * LANES]
    second_grad = dot_nt(own_filter, r.raw_grad[...], HIGH)
    angle_grad = second_grad * r.second_cos[...]
    freq_grad = jnp.sum(angle_grad * r.second_sum[...], axis=1, keepdims=True)
    sum_grad = angle_grad * column(line(r.hidden_freq))
    at = slice(PAY_HID, PAY_HID + FILT)
    r.pay[at, 0:FILT] = dot_nt(r.first[...], sum_grad, HIGH)
    r.pay[at, FILT : FILT + 1] = freq_grad
    r.pay[at, FILT + 1 : FILT + 2] = jnp.sum(sum_grad, axis=1, keepdims=True)
    angle_grad = dot(r.hidden_weight[...], sum_grad, precision=HIGH) * r.first_cos[...]
    r.pay[at, FILT + 2 : FILT + 3] = jnp.sum(
        angle_grad * r.first_sum[...], axis=1, keepdims=True
    )
    sum_grad = angle_grad * column(line(r.embed_freq))
    r.pay[at, FILT + 3 : FILT + 4] = jnp.sum(sum_grad, axis=1, keepdims=True)
    r.pay[PAY_EMB : PAY_EMB + EMB, 0:FILT] = dot_nt(features, sum_grad, HIGH)

    half_pay = PAY_ROWS // 2
    part_pay = half_pay // halves
    slot = y * 2 + q

    def pay_half(cc):
        return pl.ds(pl.multiple_of(cc * half_pay, half_pay), half_pay)

    def pay_chip():
        return remote(
            r.pay.at[pay_half(other)], r.pay_in, r.pay_send.at[0], r.pay_recv.at[0], sibling
        )

    def pay_link(jj):
        at = pl.ds(pl.multiple_of(jj * part_pay, part_pay), part_pay)
        return remote(
            r.pay_sum.at[at],
            r.pay_held.at[j],
            r.paylink_send.at[jj],
            r.paylink_recv.at[j],
            device(y, c, q, jj),
        )

    def slots_copies(n, held):
        out = []
        for dy in range(ranks):
            for dq in range(2):
                if dy or dq:
                    out.append(
                        remote(
                            held.at[slot],
                            held.at[slot],
                            r.cross_send.at[n, dy * 2 + dq],
                            r.cross_recv.at[n, dy * 2 + dq],
                            device((y + dy) % ranks, c, (q + dq) % 2, j),
                        )
                    )
        return out

    def slots_sum(n, held):
        for dy in range(ranks):
            for dq in range(2):
                if dy or dq:
                    yy, qq = (y + ranks - dy) % ranks, (q + dq) % 2
                    came = held.at[yy * 2 + qq]
                    remote(
                        came,
                        came,
                        r.cross_send.at[n, dy * 2 + dq],
                        r.cross_recv.at[n, dy * 2 + dq],
                        device(yy, c, qq, j),
                    ).wait_recv()
        return added(held, 2 * ranks)

    def added(held, count):
        total = held[0]
        for i in range(1, count):
            total = total + held[i]
        return total

    pay_chip().start()
    for w in (3, 2, 1):
        sum_close(w)

    pay_chip().wait_recv()
    r.pay_sum[...] = r.pay[pay_half(c), :] + r.pay_in[...]
    for k in range(1, halves):
        pay_link(ahead(k)).start()
    r.pay_held[j] = r.pay_sum[pl.ds(pl.multiple_of(j * part_pay, part_pay), part_pay), :]
    for dy in range(1, ranks):
        shard_y(dy, True).wait_recv()
    sums_q[q] = added(sums_y, ranks)
    shard_q().start()
    sum_cross(0)

    r.block_out[...] = (r.middle[...] + line(r.down_bias) + scatter_finish(2)).astype(BF16)
    gives = [(r.input_grad, r.input_any), (r.block_out, r.block_any)]

    def give(i):
        src, dst = gives[i]
        return remote(src, dst, r.give_send.at[i], r.give_recv.at[i], partner)

    def give_local(i):
        src, dst = gives[i]
        return pltpu.make_async_copy(src, dst, r.give_local.at[i])

    def give_start(i):
        @pl.when(moved)
        def _():
            give(i).start()

        @pl.when(owner)
        def _():
            give_local(i).start()

    give_start(1)

    for k in range(1, halves):
        jj = behind(k)
        remote(
            r.pay_held.at[jj],
            r.pay_held.at[jj],
            r.paylink_send.at[jj],
            r.paylink_recv.at[jj],
            device(y, c, q, jj),
        ).wait_recv()
    r.pay_cross[slot] = added(r.pay_held, halves)
    for copy in slots_copies(0, r.pay_cross):
        copy.start()
    shard_q(True).wait_recv()
    r.shards[pl.ds(pl.multiple_of(shard * SHARD_ROWS, SHARD_ROWS), SHARD_ROWS), :] = added(
        sums_q, 2
    )
    gather_start(4, r.shards)

    unit, scale = norm_parts(r.x_in[...].astype(F32))
    mixer_back = scatter_finish(3)
    r.input_grad[...] = (
        r.middle_grad[...] + norm_back(mixer_back, line(r.mixer_gain), unit, scale)
    ).astype(BF16)
    give_start(0)
    def store(name):
        i = s.stores.index(name)
        return pltpu.make_async_copy(
            getattr(r, name), getattr(r, name + "_out"), r.store_sem.at[i]
        )

    r.pay_total[seat(5, c, j), :] = slots_sum(0, r.pay_cross)
    gather_start(5, r.pay_total)
    sum_close(0)
    gather_finish(4, r.shards)
    store("shards").start()
    home = pl.multiple_of((q * halves + j) * SHARD_ROWS, SHARD_ROWS)
    wide = jnp.concatenate(
        [r.shards[pl.ds(home + SHARD_PAR + 8 * k, 8), :] for k in range(3)], axis=1
    )
    r.par_wide[...] = wide
    r.par_close[...] = dot_nt(wide, r.order_wide[...], HIGH)
    store("par_wide").start()
    store("par_close").start()
    for w, name in ((3, "gwdn"), (2, "gwup"), (1, "gwout")):
        sum_finish(w)
        store(name).start()
    gather_finish(5, r.pay_total)
    store("pay_total").start()
    sum_finish(0)
    store("gwin").start()
    for name in s.stores:
        store(name).wait()

    pay_chip().wait_send()
    for k in range(1, halves):
        pay_link(ahead(k)).wait_send()
    for dy in range(1, ranks):
        shard_y(dy).wait_send()
    shard_q().wait_send()
    for copy in slots_copies(0, r.pay_cross):
        copy.wait_send()

    @pl.when(moved)
    def _():
        for i in (w_out, w_up, w_down):
            take(i).wait_send()
        for i in range(len(gives)):
            give(i).wait()

    @pl.when(owner)
    def _():
        for i in range(len(gives)):
            give_local(i).wait()


def close(s, names, *refs):
    r = types.SimpleNamespace(**dict(zip(names, refs)))
    lines = D // LANES

    def load(name):
        i = s.loads.index(name)
        return pltpu.make_async_copy(
            getattr(r, name + "_any"), getattr(r, name), r.load_sem.at[i]
        )

    def store(name):
        i = s.stores.index(name)
        return pltpu.make_async_copy(getattr(r, name), getattr(r, name + "_out"), r.store_sem.at[i])

    def put(**values):
        for name, value in values.items():
            held = getattr(r, name)
            held[...] = value if value.shape == held.shape else jnp.reshape(value, held.shape)
            store(name).start()

    for name in s.loads:
        load(name).start()
    load("block").wait()
    through = pltpu.make_async_copy(r.block, r.block_out, r.block_sem)
    through.start()
    for name in ("gwin", "gwup", "gwdn", "gwout", "input"):
        load(name).wait()
        held = getattr(r, name)
        size = getattr(r, name + "_wide").shape[0]
        put(**{name + "_wide": held[0:size, :].astype(F32)})
    load("pay_total").wait()
    pay = r.pay_total

    def long_row(ref, at):
        return jnp.concatenate([ref[at + k : at + k + 1, :] for k in range(lines)], axis=1)

    same = lax.broadcasted_iota(jnp.int32, (FILT, FILT), 0) == lax.broadcasted_iota(
        jnp.int32, (FILT, FILT), 1
    )

    def vector_of(k):
        col = pay[PAY_HID : PAY_HID + FILT, FILT + k : FILT + k + 1]
        return jnp.sum(jnp.where(same, col, 0.0), axis=0, keepdims=True)

    put(ffn_gain=long_row(pay, PAY_VEC))
    put(out_bias=long_row(pay, PAY_VEC + lines))
    put(down_bias=long_row(pay, PAY_VEC + 2 * lines))
    put(embed_weight=pay[PAY_EMB : PAY_EMB + EMB, 0:FILT])
    put(embed_bias=vector_of(3))
    put(embed_freq=vector_of(2))
    put(hidden_weight=pay[PAY_HID : PAY_HID + FILT, 0:FILT])
    put(hidden_bias=vector_of(1))
    put(hidden_freq=vector_of(0))
    r.penalty_out[0] = jnp.sum(pay[PAY_PEN : PAY_PEN + 1, :])
    put(mixer_gain=long_row(pay, PAY_VEC + 3 * lines))
    load("par_wide").wait()
    load("par_close").wait()
    put(in_bias=r.par_close[0:1, :])
    put(short_taps=r.par_close[1:4, :])
    put(skip_gain=r.par_wide[4:5, 0 : s.channels])
    put(up_bias=r.par_wide[5:6, 0 : s.hidden])
    load("shards").wait()
    for i in range(2 * s.halves):
        at = slice(i * s.channels, (i + 1) * s.channels)
        base = i * SHARD_ROWS
        r.filter_weight[:, at] = r.shards[base : base + FILT, 0 : s.channels]
        r.decay_row[0:1, at] = r.shards[
            base + SHARD_DECAY : base + SHARD_DECAY + 1, 0 : s.channels
        ]
    store("filter_weight").start()
    put(decay_rate=r.decay_row[0:1, :])
    for name in s.stores:
        store(name).wait()
    through.wait()


def round_up(value, unit):
    return (value + unit - 1) // unit * unit


def solution(mesh):
    n_dp, n_mp = mesh.shape["dp"], mesh.shape["mp"]

    def per_device(
        block_input,
        mixer_gain,
        in_weight,
        in_bias,
        short_taps,
        skip_gain,
        out_weight,
        out_bias,
        ffn_gain,
        up_weight,
        up_bias,
        down_weight,
        down_bias,
        embed_weight,
        embed_bias,
        embed_freq,
        hidden_weight,
        hidden_bias,
        hidden_freq,
        filter_weight,
        decay_rate,
        out_grad,
        sequence_lengths,
        sequence_rank,
        sequence_offset,
    ):
        ranks, halves = n_dp // 2, n_mp // 2
        rows = block_input.shape[0]
        channels, hidden = skip_gain.shape[0], up_weight.shape[1]
        down_rows = round_up(hidden, 16 * ranks)
        in_rows = round_up(3 * channels, 16 * ranks)
        group = 2 * halves
        anywhere = pl.BlockSpec(memory_space=pl.ANY)
        scalar = pl.BlockSpec(memory_space=pltpu.SMEM)
        small = dict(
            mixer_gain=mixer_gain,
            ffn_gain=ffn_gain,
            out_bias=out_bias,
            down_bias=down_bias,
            in_bias=in_bias,
            short_taps=short_taps,
            skip_gain=skip_gain,
            embed_weight=embed_weight,
            embed_bias=embed_bias,
            embed_freq=embed_freq,
            hidden_weight=hidden_weight,
            hidden_bias=hidden_bias,
            hidden_freq=hidden_freq,
            filter_weight=filter_weight,
            decay_rate=decay_rate,
            features=jnp.asarray(position_features(), F32),
            waves=jnp.asarray(WAVES, BF16),
            unwaves=jnp.asarray(UNWAVES, BF16),
        )
        inputs = dict(
            x_any=(block_input, anywhere),
            og_any=(out_grad, anywhere),
            win_any=(in_weight.T, anywhere),
            wout_any=(out_weight, anywhere),
            wup_any=(up_weight, anywhere),
            wdn_any=(down_weight, anywhere),
            up_bias=(up_bias, pl.BlockSpec(memory_space=pltpu.VMEM)),
            lengths=(sequence_lengths, scalar),
            owners=(sequence_rank, scalar),
            offsets=(sequence_offset, scalar),
        )
        for name, value in small.items():
            inputs[name + "_any"] = (value, anywhere)
        kept = dict(
            gwin=((in_rows, D), BF16),
            gwout=((LANES, D), BF16),
            gwup=((D, hidden), BF16),
            gwdn=((down_rows, D), BF16),
            pay_total=((PAY_ROWS, LANES), F32),
            shards=((group * SHARD_ROWS, LANES), F32),
            par_wide=((8, WIDE), F32),
            par_close=((8, 3 * channels), F32),
        )
        outputs = dict(block_any=((rows, D), BF16), input_any=((rows, D), BF16))
        for name, kind in kept.items():
            outputs[name + "_out"] = kind
        sizes = types.SimpleNamespace(
            ranks=ranks,
            halves=halves,
            inner=n_mp // 4,
            rows=rows,
            channels=channels,
            hidden=hidden,
            sequences=sequence_lengths.shape[0],
            loads=list(small),
            late_loads=("features", "waves", "unwaves"),
            stores=list(kept),
        )
        dma = pltpu.SemaphoreType.DMA
        scratch = {}

        def hold(**held):
            for name, kind in held.items():
                scratch[name] = pltpu.VMEM(*kind)

        for name, value in small.items():
            scratch[name] = pltpu.VMEM(value.shape, value.dtype)
        for name, kind in kept.items():
            scratch[name] = pltpu.VMEM(*kind)
        hold(x_in=((rows, D), BF16))
        hold(unit=((rows, D), F32))
        hold(scale=((rows, LANES), F32))
        hold(par_own=((8, WIDE), F32))
        hold(par_in=((8, WIDE), F32))
        hold(par_grad=((8, WIDE), F32))
        hold(taps=((8, WIDE), F32))
        hold(win=((3 * channels, D), BF16))
        hold(win_apart=((WIDE, D), BF16))
        hold(wout=((LANES, D), BF16))
        hold(wup=((D, hidden), BF16))
        hold(wdn=((hidden, D), BF16))
        hold(order=((3 * channels, WIDE), BF16))
        hold(order_wide=((3 * channels, WIDE), F32))
        hold(first=((FILT, LONG), F32))
        hold(first_sum=((FILT, LONG), F32))
        hold(first_cos=((FILT, LONG), F32))
        hold(second=((FILT, LONG), F32))
        hold(second_sum=((FILT, LONG), F32))
        hold(second_cos=((FILT, LONG), F32))
        hold(own_filter=((FILT, LANES), F32))
        hold(own_decay=((8, LANES), F32))
        hold(kernel=((LONG, LANES), F32))
        hold(raw_grad=((LONG, LANES), F32))
        hold(spread=((BINS, COUNT * LANES), BF16))
        hold(kernel_wave=((BINS, COUNT * LANES), F32))
        hold(signal_wave=((BINS, COUNT * LANES), F32))
        hold(grad_wave=((BINS, COUNT * LANES), F32))
        hold(product=((BINS, COUNT * LANES), BF16))
        hold(back_product=((2 * BINS, COUNT * LANES), BF16))
        hold(g_one=((LONG, D), BF16))
        hold(g_out=((LONG, D), BF16))
        hold(g_two=((LONG, D), BF16))
        hold(g_back=((LONG, D), BF16))
        hold(projected=((LONG, WIDE), F32))
        hold(short=((LONG, WIDE), F32))
        hold(short_grad=((LONG, WIDE), F32))
        hold(signal=((BLOCK, COUNT * LANES), BF16))
        hold(direct_low=((BLOCK, COUNT * LANES), BF16))
        hold(direct=((LONG, LANES), F32))
        hold(mixed=((LONG, LANES), BF16))
        hold(middle=((rows, D), F32))
        hold(middle_grad=((rows, D), F32))
        hold(input_grad=((rows, D), BF16))
        hold(block_out=((rows, D), BF16))
        hold(active=((LONG, hidden), BF16))
        hold(hidden_grad=((LONG, hidden), BF16))
        hold(projected_grad=((LONG, 3 * channels), BF16))
        hold(chip_out=((4, LONG // 2, D), BF16))
        hold(chip_in=((4, LONG // 2, D), BF16))
        hold(link_out=((4, LONG // 2, D), BF16))
        hold(link_in=((4, LONG // 2, D), BF16))
        for name, full in dict(
            _in=(in_rows, D), _out=(LANES, D), _up=(D, hidden), _dn=(down_rows, D)
        ).items():
            part = (full[0] // ranks, full[1])
            for kind, shape in dict(grad=full, part=part, y=(ranks,) + part, z=part).items():
                scratch[kind + name] = pltpu.VMEM(shape, BF16)
        hold(gain_sum=((8, D), F32))
        hold(pay=((PAY_ROWS, LANES), F32))
        hold(pay_in=((PAY_ROWS // 2, LANES), F32))
        hold(pay_sum=((PAY_ROWS // 2, LANES), F32))
        hold(pay_held=((halves, PAY_ROWS // group, LANES), F32))
        hold(pay_cross=((2 * ranks, PAY_ROWS // group, LANES), F32))
        hold(shard_y=((ranks, SHARD_ROWS, LANES), F32))
        hold(shard_q=((2, SHARD_ROWS, LANES), F32))
        for name, shape in dict(
            take=(7,),
            give=(2,),
            cut=(7, ranks),
            gather=(6, halves),
            hop=(6, halves),
            chip=(4, LONG // 2 // BLOCK),
            link=(4, halves),
            y=(4, ranks),
            z=(4,),
            out=(4, ranks),
            fin=(4, ranks),
            pay=(1,),
            paylink=(halves,),
            sy=(ranks,),
            sq=(1,),
            cross=(2, 2 * ranks),
        ).items():
            scratch[name + "_send"] = dma(shape)
            scratch[name + "_recv"] = dma(shape)
        scratch["take_local"] = dma((7,))
        scratch["give_local"] = dma((2,))
        scratch["load_sem"] = dma((len(small),))
        scratch["store_sem"] = dma((len(kept),))
        names = list(inputs) + list(outputs) + list(scratch)
        results = pl.pallas_call(
            functools.partial(fused, sizes, names),
            out_shape=[jax.ShapeDtypeStruct(*kind) for kind in outputs.values()],
            in_specs=[i[1] for i in inputs.values()],
            out_specs=[anywhere for _ in outputs],
            scratch_shapes=list(scratch.values()),
            compiler_params=pltpu.CompilerParams(
                collective_id=0,
                has_side_effects=True,
                vmem_limit_bytes=60 * 2**20,
            ),
            name="block",
        )(*[i[0] for i in inputs.values()])
        finals = dict(
            gwin_wide=(3 * channels, D),
            gwout_wide=(channels, D),
            gwup_wide=(D, hidden),
            gwdn_wide=(hidden, D),
            input_wide=(rows, D),
            mixer_gain=(D,),
            in_bias=(3 * channels,),
            short_taps=(3, 3 * channels),
            skip_gain=(channels,),
            out_bias=(D,),
            ffn_gain=(D,),
            up_bias=(hidden,),
            down_bias=(D,),
            embed_weight=(EMB, FILT),
            embed_bias=(FILT,),
            embed_freq=(FILT,),
            hidden_weight=(FILT, FILT),
            hidden_bias=(FILT,),
            hidden_freq=(FILT,),
            filter_weight=(FILT, D),
            decay_rate=(D,),
        )
        loads = ["block", "input"] + list(kept)
        closing = types.SimpleNamespace(
            halves=halves, channels=channels, hidden=hidden, loads=loads, stores=list(finals)
        )
        scratch = dict(
            block=pltpu.VMEM((rows, D), BF16),
            input=pltpu.VMEM((rows, D), BF16),
            decay_row=pltpu.VMEM((8, D), F32),
        )
        for name, kind in kept.items():
            scratch[name] = pltpu.VMEM(*kind)
        for name, shape in finals.items():
            scratch[name] = pltpu.VMEM(shape, F32)
        scratch["load_sem"] = dma((len(loads),))
        scratch["store_sem"] = dma((len(finals),))
        scratch["block_sem"] = dma
        names = [name + "_any" for name in loads] + ["block_out"]
        names += [name + "_out" for name in finals] + ["penalty_out"] + list(scratch)
        done = pl.pallas_call(
            functools.partial(close, closing, names),
            out_shape=[jax.ShapeDtypeStruct((rows, D), BF16)]
            + [jax.ShapeDtypeStruct(shape, F32) for shape in finals.values()]
            + [jax.ShapeDtypeStruct((1,), F32)],
            in_specs=[anywhere] * len(loads),
            out_specs=[anywhere] * (1 + len(finals)) + [scalar],
            scratch_shapes=list(scratch.values()),
            compiler_params=pltpu.CompilerParams(vmem_limit_bytes=60 * 2**20),
            name="close",
        )(*results)
        out = types.SimpleNamespace(**dict(zip(finals, done[1:-1])))
        return (
            done[0],
            out.input_wide,
            done[-1].reshape(()),
            out.mixer_gain,
            out.gwin_wide.T,
            out.in_bias,
            out.short_taps,
            out.skip_gain,
            out.gwout_wide,
            out.out_bias,
            out.ffn_gain,
            out.gwup_wide,
            out.up_bias,
            out.gwdn_wide,
            out.down_bias,
            out.embed_weight,
            out.embed_bias,
            out.embed_freq,
            out.hidden_weight,
            out.hidden_bias,
            out.hidden_freq,
            out.filter_weight,
            out.decay_rate,
        )

    placed = (
        P(("dp", "mp"), None),
        P(),
        P(None, "mp"),
        P("mp"),
        P(None, "mp"),
        P("mp"),
        P("mp", None),
        P(),
        P(),
        P(None, "mp"),
        P("mp"),
        P("mp", None),
        P(),
        P(),
        P(),
        P(),
        P(),
        P(),
        P(),
        P(),
        P(),
        P(("dp", "mp"), None),
        P(),
        P(),
        P(),
    )
    return jax.shard_map(
        per_device,
        mesh=mesh,
        in_specs=placed,
        out_specs=(
            P(("dp", "mp"), None),
            P(("dp", "mp"), None),
            P(),
            P(),
            P(None, "mp"),
            P("mp"),
            P(None, "mp"),
            P("mp"),
            P("mp", None),
            P(),
            P(),
            P(None, "mp"),
            P("mp"),
            P("mp", None),
            P(),
            P(),
            P(),
            P(),
            P(),
            P(),
            P(),
            P(),
            P(),
        ),
        check_vma=False,
    )
```

```python
import functools
import math
import types

import jax
import jax.numpy as jnp
import numpy as np
from jax import lax
from jax.experimental import pallas as pl
from jax.experimental.pallas import tpu as pltpu
from jax.sharding import PartitionSpec as P

D = 768
BANDS = 16
EMB = 2 * BANDS + 1
FILT = 64
LONG = 1024
BLOCK = 256
BINS = 2 * BLOCK
COUNT = LONG // BLOCK
LANES = 128
WIDE = 3 * LANES
MESH = pl.DeviceIdType.MESH
BF16 = jnp.bfloat16
F32 = jnp.float32
EPS = 1e-05
ROOT = math.sqrt(2.0 / math.pi)
CUBE = 0.044715

PAY_VEC, PAY_HID, PAY_EMB, PAY_PEN, PAY_ROWS = 0, 24, 88, 121, 128
SHARD_DECAY, SHARD_PAR, SHARD_ROWS = 64, 72, 96


def wave_table(shift):
    bins = np.arange(BLOCK)[:, None]
    angle = np.pi * (2 * bins + 1) * (np.arange(BLOCK)[None, :] + shift) / BINS
    return np.concatenate([np.cos(angle), -np.sin(angle)], 0)


NEAR, FAR = wave_table(0), wave_table(-BLOCK)
WAVES = np.concatenate([NEAR, FAR], 1)
UNWAVES = np.concatenate([NEAR.T, FAR.T], 1) / BLOCK


def position_features():
    tau = np.arange(LONG) / LONG
    angles = 2.0 * np.pi * np.arange(1, BANDS + 1)[:, None] * tau[None, :]
    return np.concatenate([tau[None, :], np.cos(angles), np.sin(angles)], 0)


def dot(left, right, dims=((1,), (0,)), precision=None):
    return lax.dot_general(
        left, right, (dims, ((), ())), precision=precision, preferred_element_type=F32
    )


def dot_nt(left, right, precision=None):
    return dot(left, right, ((1,), (1,)), precision)


def dot_tn(left, right, precision=None):
    return dot(left, right, ((0,), (0,)), precision)


HIGH = lax.Precision.HIGHEST


def sin_cos(angle):
    turns = jnp.floor(angle * (2.0 / math.pi) + 0.5)
    rest = angle - turns * 1.5703125
    rest = rest - turns * 4.837512969970703125e-4
    rest = rest - turns * 7.54978995489188e-8
    square = rest * rest
    sine = rest + rest * square * (
        -1.6666654611e-1 + square * (8.3321608736e-3 + square * -1.9515295891e-4)
    )
    cosine = (
        1.0
        - 0.5 * square
        + square
        * square
        * (4.166664568298827e-2 + square * (-1.388731625493765e-3 + square * 2.443315711809948e-5))
    )
    half = jnp.floor(turns * 0.5)
    odd = turns - 2.0 * half
    sign = 1.0 - 2.0 * (half - 2.0 * jnp.floor(half * 0.5))
    swapped = odd > 0.5
    return (
        jnp.where(swapped, cosine, sine) * sign,
        jnp.where(swapped, -sine, cosine) * sign,
    )


def norm_parts(values):
    center = values - jnp.mean(values, axis=-1, keepdims=True)
    scale = lax.rsqrt(jnp.mean(center * center, axis=-1, keepdims=True) + EPS)
    return center * scale, scale


def norm_back(grad, gain, unit, scale):
    inner = grad * gain
    return scale * (
        inner
        - jnp.mean(inner, axis=-1, keepdims=True)
        - unit * jnp.mean(inner * unit, axis=-1, keepdims=True)
    )


def column(row):
    size = row.shape[1]
    same = lax.broadcasted_iota(jnp.int32, (size, size), 0) == lax.broadcasted_iota(
        jnp.int32, (size, size), 1
    )
    return jnp.sum(jnp.where(same, row, 0.0), axis=1, keepdims=True)


def fused(s, names, *refs):
    r = types.SimpleNamespace(**dict(zip(names, refs)))
    ranks, halves, inner, rows = s.ranks, s.halves, s.inner, s.rows
    channels, hidden = s.channels, s.hidden
    dp, mp = lax.axis_index("dp"), lax.axis_index("mp")
    y, c = dp // 2, dp % 2
    q, j = mp // halves, mp % halves
    other, across = 1 - c, 1 - q
    outer = halves // inner

    def device(yy, cc, qq, jj):
        return (yy * 2 + cc, qq * halves + jj)

    def ahead(k):
        return ((j // inner + k // inner) % outer) * inner + (j % inner + k % inner) % inner

    def behind(k):
        return ((j // inner + outer - k // inner) % outer) * inner + (
            j % inner + inner - k % inner
        ) % inner

    sibling = device(y, other, q, j)
    partner = device(y, other, across, j)
    moved = c != q

    def remote(src, dst, send, recv, target):
        return pltpu.make_async_remote_copy(
            src_ref=src,
            dst_ref=dst,
            send_sem=send,
            recv_sem=recv,
            device_id=target,
            device_id_type=MESH,
        )

    def block_rows(cc, jj):
        return pl.ds(pl.multiple_of((cc * halves + jj) * rows, rows), rows)

    mine = block_rows(c, j)

    barrier = pltpu.get_barrier_semaphore()
    greeted = [sibling, partner]
    for k in range(1, halves):
        greeted += [device(y, c, q, ahead(k)), device(y, other, q, ahead(k))]
    for dy in range(ranks):
        for dq in range(2):
            if dy or dq:
                greeted.append(device((y + dy) % ranks, c, (q + dq) % 2, j))
    for target in greeted:
        pl.semaphore_signal(barrier, inc=1, device_id=target, device_id_type=MESH)

    def load(name):
        i = s.loads.index(name)
        return pltpu.make_async_copy(
            getattr(r, name + "_any"), getattr(r, name), r.load_sem.at[i]
        )

    pl.semaphore_wait(barrier, len(greeted))

    par = r.par_own
    theirs = block_rows(other, j)
    x, own_par, w_in, grads, w_out, w_up, w_down = range(7)
    takes = [
        (r.x_any, r.x_in, r.x_in),
        (par, r.par_in, r.par_in),
        (r.win_any, r.win, r.win),
        (r.og_any, r.g_out.at[theirs], r.g_out.at[mine]),
        (r.wout_any, r.wout.at[pl.ds(0, channels)], r.wout.at[pl.ds(0, channels)]),
        (r.wup_any, r.wup, r.wup),
        (r.wdn_any, r.wdn, r.wdn),
    ]
    owner = jnp.logical_not(moved)

    def cut_rows(i, yy):
        size = takes[i][0].shape[0] // ranks
        return pl.ds(pl.multiple_of(yy * size, 16), size)

    def in_parts(i):
        return i in (w_in, w_up, w_down) and takes[i][0].shape[0] % (16 * ranks) == 0

    def take(i, arriving=False):
        src, dst, here = takes[i]
        dst = here if arriving else dst
        if in_parts(i):
            src, dst = src.at[cut_rows(i, y)], dst.at[cut_rows(i, y)]
        return remote(src, dst, r.take_send.at[i], r.take_recv.at[i], partner)

    def take_local(i):
        return pltpu.make_async_copy(takes[i][0], takes[i][2], r.take_local.at[i])

    def pass_copy(i, dy):
        at = takes[i][2].at[cut_rows(i, y)]
        return remote(
            at,
            at,
            r.cut_send.at[i, dy],
            r.cut_recv.at[i, dy],
            device((y + dy) % ranks, c, q, j),
        )

    def take_start(*which, after=()):
        @pl.when(moved)
        def _():
            for i in after:
                take(i).wait_send()
            for i in which:
                take(i).start()

    def take_pass(*which):
        @pl.when(moved)
        def _():
            for i in which:
                take(i, True).wait_recv()
                if in_parts(i):
                    for dy in range(1, ranks):
                        pass_copy(i, dy).start()

    def taken(*which):
        @pl.when(moved)
        def _():
            for i in which:
                if i not in (w_in, w_up, w_down):
                    take(i, True).wait_recv()
                elif in_parts(i):
                    for dy in range(1, ranks):
                        at = takes[i][2].at[cut_rows(i, (y + ranks - dy) % ranks)]
                        remote(
                            at,
                            at,
                            r.cut_send.at[i, dy],
                            r.cut_recv.at[i, dy],
                            device((y + ranks - dy) % ranks, c, q, j),
                        ).wait_recv()
                        pass_copy(i, dy).wait_send()

        @pl.when(owner)
        def _():
            for i in which:
                take_local(i).wait()

    take_start(x)
    @pl.when(owner)
    def _():
        for i in range(len(takes)):
            if i != own_par:
                take_local(i).start()

    for name in s.loads:
        load(name).start()
    for name in s.loads:
        if name not in s.late_loads:
            load(name).wait()

    def line(ref):
        return jnp.reshape(ref[...], (1, ref.shape[0]))

    par[...] = jnp.zeros_like(par)
    par[0:1, 0 : 3 * channels] = line(r.in_bias)
    par[1:4, 0 : 3 * channels] = r.short_taps[...]
    par[4:5, 0:channels] = line(r.skip_gain)
    par[5:6, 0:hidden] = line(r.up_bias).astype(F32)

    @pl.when(owner)
    def _():
        take_local(own_par).start()

    def seat(n, cc, jj):
        size = PAY_ROWS // (2 * halves) if n == 5 else SHARD_ROWS if n == 4 else rows
        return pl.ds(pl.multiple_of((cc * halves + jj) * size, size), size)

    def gather_copies(n, held):
        mine = seat(n, c, j)
        out = []
        for k in range(1, halves):
            out.append(
                remote(
                    held.at[mine],
                    held.at[mine],
                    r.gather_send.at[n, k],
                    r.gather_recv.at[n, k],
                    device(y, c, q, ahead(k)),
                )
            )
        out.append(
            remote(
                held.at[mine],
                held.at[mine],
                r.gather_send.at[n, 0],
                r.gather_recv.at[n, 0],
                sibling,
            )
        )
        return out

    def gather_start(n, held):
        for copy in gather_copies(n, held):
            copy.start()

    def gather_finish(n, held):
        forwards = []
        for k in range(1, halves):
            came = held.at[seat(n, c, behind(k))]
            remote(
                came,
                came,
                r.gather_send.at[n, k],
                r.gather_recv.at[n, k],
                device(y, c, q, behind(k)),
            ).wait_recv()
            forward = remote(
                came, came, r.hop_send.at[n, k], r.hop_recv.at[n, k], sibling
            )
            forward.start()
            forwards.append(forward)
        for k in range(halves):
            came = held.at[seat(n, other, behind(k))]
            recv = r.hop_recv.at[n, k] if k else r.gather_recv.at[n, 0]
            remote(came, came, r.hop_send.at[n, k], recv, sibling).wait_recv()
        for copy in gather_copies(n, held) + forwards:
            copy.wait_send()

    def first_norm():
        unit, _ = norm_parts(r.x_in[...].astype(F32))
        r.g_one[mine, :] = (unit * line(r.mixer_gain)).astype(BF16)
        gather_start(0, r.g_one)

    @pl.when(owner)
    def _():
        take_local(x).wait()
        first_norm()
        take_local(grads).wait()
        gather_start(1, r.g_out)

    pack = y * 2 + q
    segments = []
    for i in range(COUNT):
        found = jnp.int32(-1)
        for k in range(s.sequences):
            start = r.offsets[k]
            hit = (
                (r.owners[k] == pack)
                & (start <= i * BLOCK)
                & (start + r.lengths[k] > i * BLOCK)
            )
            found = jnp.where(hit, jnp.int32(k), found)
        segments.append(found)
    valid = [jnp.where(seg >= 0, jnp.float32(1), jnp.float32(0)) for seg in segments]
    joined = [
        [valid[i] * jnp.where(segments[i] == segments[p], jnp.float32(1), jnp.float32(0)) for p in range(i + 1)]
        for i in range(COUNT)
    ]
    follows = [jnp.float32(0)] + [joined[i][i - 1] for i in range(1, COUNT)]

    row_index = lax.broadcasted_iota(jnp.int32, (3 * channels, WIDE), 0)
    lane_index = lax.broadcasted_iota(jnp.int32, (3 * channels, WIDE), 1)
    within = lane_index % LANES
    order = jnp.where(
        (row_index == 3 * within + lane_index // LANES) & (within < channels), 1.0, 0.0
    )
    r.order[...] = order.astype(BF16)
    r.order_wide[...] = order

    load("features").wait()
    features = r.features[...]
    embed_freq, embed_bias = column(line(r.embed_freq)), column(line(r.embed_bias))
    hidden_freq, hidden_bias = column(line(r.hidden_freq)), column(line(r.hidden_bias))
    first_sum = dot_tn(r.embed_weight[...], features, HIGH) + embed_bias
    first, first_cos = sin_cos(embed_freq * first_sum)
    r.first_sum[...] = first_sum
    r.first[...] = first
    r.first_cos[...] = first_cos
    take_start(w_in, own_par, after=(x,))
    second_sum = dot_tn(r.hidden_weight[...], first, HIGH) + hidden_bias
    second, second_cos = sin_cos(hidden_freq * second_sum)
    r.second_sum[...] = second_sum
    r.second[...] = second
    r.second_cos[...] = second_cos
    half_rows = LONG // 2
    chunks = half_rows // BLOCK
    per_chunk = BLOCK // rows

    def half_chunk(cc, t):
        return pl.ds(pl.multiple_of(cc * half_rows + t * BLOCK, BLOCK), BLOCK)

    def chunk_rows(t):
        return pl.ds(pl.multiple_of(t * BLOCK, BLOCK), BLOCK)

    def place(jj):
        return pl.ds(pl.multiple_of(jj * rows, rows), rows)

    def chip_copy(n, t):
        return remote(
            r.chip_out.at[n, chunk_rows(t)],
            r.chip_in.at[n, chunk_rows(t)],
            r.chip_send.at[n, t],
            r.chip_recv.at[n, t],
            sibling,
        )

    def link_copy(n, jj):
        return remote(
            r.link_out.at[n, place(jj)],
            r.link_in.at[n, place(j)],
            r.link_send.at[n, jj],
            r.link_recv.at[n, j],
            device(y, c, q, jj),
        )

    def chip_give(n, t, value):
        r.chip_out[n, chunk_rows(t), :] = value.astype(BF16)
        chip_copy(n, t).start()

    def chip_add(n, t, value):
        chip_copy(n, t).wait_recv()
        r.link_out[n, chunk_rows(t), :] = (
            value + r.chip_in[n, chunk_rows(t), :].astype(F32)
        ).astype(BF16)

    def link_start(n, t):
        for i in range(per_chunk):
            jj = t * per_chunk + i

            @pl.when(jj != j)
            def _():
                link_copy(n, jj).start()

    def scatter(n, part):
        def give(t, carry):
            chip_give(n, t, part(half_chunk(other, t)))
            return carry

        lax.fori_loop(0, chunks, give, 0)

        def send(t, carry):
            chip_add(n, t, part(half_chunk(c, t)))
            link_start(n, t)
            return carry

        lax.fori_loop(0, chunks, send, 0)

    def scatter_finish(n):
        total = r.link_out[n, place(j), :].astype(F32)
        for k in range(1, halves):
            jj = behind(k)
            came = r.link_in.at[n, place(jj)]
            remote(
                came, came, r.link_send.at[n, jj], r.link_recv.at[n, jj], device(y, c, q, jj)
            ).wait_recv()
            total = total + r.link_in[n, place(jj), :].astype(F32)
        for t in range(chunks):
            chip_copy(n, t).wait_send()
        for k in range(1, halves):
            link_copy(n, ahead(k)).wait_send()
        return total

    @pl.when(moved)
    def _():
        take(x, True).wait_recv()
        first_norm()

    shard = c * halves + j
    pick_row = lax.broadcasted_iota(jnp.int32, (D, LANES), 0)
    pick_lane = lax.broadcasted_iota(jnp.int32, (D, LANES), 1)
    pick = jnp.where((pick_row == shard * channels + pick_lane) & (pick_lane < channels), 1.0, 0.0)
    own_filter = dot(r.filter_weight[...], pick, precision=HIGH)
    own_decay = dot(jnp.broadcast_to(line(r.decay_rate), (8, D)), pick, precision=HIGH)[0:1]
    r.own_filter[...] = own_filter
    r.own_decay[...] = jnp.broadcast_to(own_decay, (8, LANES))
    r.spread[...] = jnp.zeros_like(r.spread)
    for i in range(COUNT):
        at = slice(i * BLOCK, (i + 1) * BLOCK)
        tau = (
            lax.broadcasted_iota(jnp.int32, (BLOCK, LANES), 0) + i * BLOCK
        ).astype(F32) * (1.0 / LONG)
        kernel = dot_tn(second[:, at], own_filter, HIGH) * jnp.exp(-tau * own_decay)
        r.kernel[at, :] = kernel
        low = kernel.astype(BF16)
        r.spread[0:BLOCK, i * LANES : (i + 1) * LANES] = low
        if i + 1 < COUNT:
            r.spread[BLOCK:BINS, (i + 1) * LANES : (i + 2) * LANES] = low
    take_start(grads, w_out, after=(w_in, own_par))
    take_pass(w_in)
    load("waves").wait()
    load("unwaves").wait()
    r.kernel_wave[...] = dot(r.waves[...], r.spread[...])
    gather_finish(0, r.g_one)

    @pl.when(moved)
    def _():
        take(grads, True).wait_recv()
        gather_start(1, r.g_out)

    take_start(w_up, w_down, after=(grads,))
    taken(own_par, w_in)
    par_wide = dot(r.par_in[:, 0 : 3 * channels], r.order_wide[...], precision=HIGH)
    r.taps[...] = par_wide
    r.win_apart[...] = dot_tn(r.order[...], r.win[...]).astype(BF16)
    r.wout[channels:, :] = jnp.zeros_like(r.wout[channels:, :])

    def project(i, carry):
        at = pl.ds(pl.multiple_of(i * BINS, BINS), BINS)
        r.projected[at, :] = dot_nt(r.g_one[at, :], r.win_apart[...]) + r.taps[0:1, :]
        return carry

    lax.fori_loop(0, LONG // BINS, project, 0)

    rows_here = lax.broadcasted_iota(jnp.int32, (BLOCK, 1), 0)

    def back_rows(i):
        now = r.projected[i * BLOCK : (i + 1) * BLOCK, :]
        one, two = pltpu.roll(now, 1, 0), pltpu.roll(now, 2, 0)
        if i:
            edge = r.projected[i * BLOCK - 8 : i * BLOCK, :] * follows[i]
            last, before = edge[7:8], edge[6:7]
        else:
            last = before = jnp.zeros((1, WIDE), F32)
        one = jnp.where(rows_here == 0, last, one)
        two = jnp.where(rows_here == 0, before, jnp.where(rows_here == 1, last, two))
        return now, one, two

    for i in range(COUNT):
        now, one, two = back_rows(i)
        short = r.taps[1:2, :] * now + r.taps[2:3, :] * one + r.taps[3:4, :] * two
        r.short[i * BLOCK : (i + 1) * BLOCK, :] = short
        signal = short[:, 2 * LANES :] * short[:, LANES : 2 * LANES] * valid[i]
        r.signal[:, i * LANES : (i + 1) * LANES] = signal.astype(BF16)

    near = r.waves[:, 0:BLOCK]
    unnear = r.unwaves[:, 0:BINS]
    r.signal_wave[...] = dot(near, r.signal[...])
    step = 16

    def load_wave(ref, at, count=COUNT):
        low, high = pl.ds(at, step), pl.ds(at + BLOCK, step)
        return [
            (ref[low, i * LANES : (i + 1) * LANES], ref[high, i * LANES : (i + 1) * LANES])
            for i in range(count)
        ]

    def store_wave(ref, base, at, i, pair):
        ref[pl.ds(base + at, step), i * LANES : (i + 1) * LANES] = pair[0].astype(BF16)
        ref[pl.ds(base + at + BLOCK, step), i * LANES : (i + 1) * LANES] = pair[1].astype(BF16)

    def weighted(terms):
        real = imag = None
        for weight, (a, b) in terms:
            real = a * weight if real is None else real + a * weight
            imag = b * weight if imag is None else imag + b * weight
        return real, imag

    def times(left, right):
        return left[0] * right[0] - left[1] * right[1], left[0] * right[1] + left[1] * right[0]

    def times_conj(left, right):
        return left[0] * right[0] + left[1] * right[1], left[0] * right[1] - left[1] * right[0]

    def forward_wave(n, carry):
        at = pl.multiple_of(n * step, step)
        kernels, signals = load_wave(r.kernel_wave, at), load_wave(r.signal_wave, at)
        for i in range(COUNT):
            store_wave(
                r.product,
                0,
                at,
                i,
                weighted([(joined[i][p], times(kernels[i - p], signals[p])) for p in range(i + 1)]),
            )
        return carry

    lax.fori_loop(0, BLOCK // step, forward_wave, 0)
    skip = r.par_in[4:5, 0:LANES]
    convolved = dot(unnear, r.product[0:BINS, :])
    for i in range(COUNT):
        at = slice(i * BLOCK, (i + 1) * BLOCK)
        lanes = slice(i * LANES, (i + 1) * LANES)
        direct = convolved[:, lanes] + skip * r.signal[:, lanes].astype(F32)
        r.direct[at, :] = direct
        r.mixed[at, :] = (direct * r.short[at, 0:LANES]).astype(BF16)

    taken(w_out)
    scatter(0, lambda at: dot(r.mixed[at, :], r.wout[...]))
    take_pass(w_up)
    middle = r.x_in[...].astype(F32) + line(r.out_bias) + scatter_finish(0)
    unit, scale = norm_parts(middle)
    r.g_two[mine, :] = (unit * line(r.ffn_gain)).astype(BF16)
    gather_start(2, r.g_two)
    r.middle[...] = middle
    r.unit[...] = unit
    r.scale[...] = jnp.broadcast_to(scale, r.scale.shape)
    take_pass(w_down)
    gather_finish(1, r.g_out)
    gather_finish(2, r.g_two)
    taken(w_up, w_down)

    def feed(at):
        value = dot(r.g_two[at, :], r.wup[...]) + r.par_in[5:6, 0:hidden]
        square = value * value
        bend = jnp.tanh(ROOT * value * (1.0 + CUBE * square))
        half = 0.5 * (1.0 + bend)
        active = (value * half).astype(BF16)
        slope = half + 0.5 * value * (1.0 - bend * bend) * (ROOT * (1.0 + 3.0 * CUBE * square))
        grad = (slope * dot_nt(r.g_out[at, :], r.wdn[...])).astype(BF16)
        r.active[at, :] = active
        r.hidden_grad[at, :] = grad
        return dot_nt(grad, r.wup[...])

    def feed_step(i, carry):
        t, own = i // 2, i % 2
        back = feed(half_chunk(own * c + (1 - own) * other, t))

        @pl.when(own == 0)
        def _():
            chip_give(1, t, back)

        @pl.when(own == 1)
        def _():
            chip_add(1, t, back)
            link_start(1, t)

        return carry

    lax.fori_loop(0, 2 * chunks, feed_step, 0)

    def down(at):
        return dot(r.active[at, :], r.wdn[...])

    def down_give(t, carry):
        chip_give(2, t, down(half_chunk(other, t)))
        return carry

    def down_add(t, carry):
        chip_add(2, t, down(half_chunk(c, t)))
        return carry

    lax.fori_loop(0, chunks, down_give, 0)

    sums = [
        (r.grad_in, r.part_in, r.y_in, r.z_in, r.gwin),
        (r.grad_out, r.part_out, r.y_out, r.z_out, r.gwout),
        (r.grad_up, r.part_up, r.y_up, r.z_up, r.gwup),
        (r.grad_dn, r.part_dn, r.y_dn, r.z_dn, r.gwdn),
    ]
    def part_rows(ref, yy):
        size = ref.shape[0] // ranks
        return pl.ds(pl.multiple_of(yy * size, 16), size)

    def y_copy(w, dy):
        full, _, came, _, _ = sums[w]
        to = (y + dy) % ranks
        return remote(
            full.at[part_rows(full, to)],
            came.at[dy],
            r.y_send.at[w, dy],
            r.y_recv.at[w, dy],
            device(to, c, q, j),
        )

    def z_copy(w):
        _, part, _, came, _ = sums[w]
        return remote(
            part, came, r.z_send.at[w], r.z_recv.at[w], device(y, c, across, j)
        )

    def out_copy(w, dy):
        final = sums[w][4]
        at = part_rows(final, y)
        return remote(
            final.at[at],
            final.at[at],
            r.out_send.at[w, dy],
            r.out_recv.at[w, dy],
            device((y + dy) % ranks, c, q, j),
        )

    def chip_final(w, dy):
        final = sums[w][4]
        at = part_rows(final, (y + ranks - dy) % ranks)
        return remote(
            final.at[at],
            final.at[at],
            r.fin_send.at[w, dy],
            r.fin_recv.at[w, dy],
            sibling,
        )

    def sum_start(w):
        for dy in range(1, ranks):
            y_copy(w, dy).start()

    def sum_cross(w):
        full, part, came, _, _ = sums[w]
        total = full[part_rows(full, y), :].astype(F32)
        for dy in range(1, ranks):
            y_copy(w, dy).wait_recv()
            total = total + came[dy].astype(F32)
        part[...] = total.astype(BF16)

        @pl.when(moved)
        def _():
            z_copy(w).start()

    def sum_close(w):
        _, part, _, came, final = sums[w]

        @pl.when(owner)
        def _():
            z_copy(w).wait_recv()
            final[part_rows(final, y), :] = (
                part[...].astype(F32) + came[...].astype(F32)
            ).astype(BF16)
            for dy in range(1, ranks):
                out_copy(w, dy).start()
            chip_final(w, 0).start()

    def sum_finish(w):
        final = sums[w][4]

        @pl.when(owner)
        def _():
            for dy in range(1, ranks):
                at = part_rows(final, (y + ranks - dy) % ranks)
                remote(
                    final.at[at],
                    final.at[at],
                    r.out_send.at[w, dy],
                    r.out_recv.at[w, dy],
                    sibling,
                ).wait_recv()
                chip_final(w, dy).start()
            for dy in range(1, ranks):
                out_copy(w, dy).wait_send()
            for dy in range(ranks):
                chip_final(w, dy).wait_send()

        @pl.when(moved)
        def _():
            for dy in range(ranks):
                chip_final(w, dy).wait_recv()
            z_copy(w).wait_send()

        for dy in range(1, ranks):
            y_copy(w, dy).wait_send()

    def weight_grad(target, left, right, by_right=False):
        if by_right:
            target[0 : left.shape[1], :] = dot_tn(left[...], right[...]).astype(BF16)
            return

        def chunk(i, carry):
            at = pl.ds(pl.multiple_of(i * BLOCK, BLOCK), BLOCK)
            target[at, :] = dot_tn(left[:, at], right[...]).astype(BF16)
            return carry

        lax.fori_loop(0, D // BLOCK, chunk, 0)

    for grad, size in ((r.grad_dn, hidden), (r.grad_in, 3 * channels)):
        if grad.shape[0] > size:
            grad[size:, :] = jnp.zeros_like(grad[size:, :])
    weight_grad(r.grad_dn, r.active, r.g_out, True)
    sum_start(3)
    weight_grad(r.grad_up, r.g_two, r.hidden_grad)
    sum_start(2)
    lax.fori_loop(0, chunks, down_add, 0)

    seed = r.g_out[mine, :].astype(F32)
    ffn_back = scatter_finish(1)
    unit, scale = r.unit[...], jnp.concatenate([r.scale[...]] * (D // LANES), axis=1)
    middle_grad = seed + norm_back(ffn_back, line(r.ffn_gain), unit, scale)
    r.middle_grad[...] = middle_grad
    branch_grad = middle_grad.astype(BF16)
    r.g_back[mine, :] = branch_grad
    gather_start(3, r.g_back)
    vectors = [
        jnp.sum(ffn_back * unit, axis=0, keepdims=True),
        jnp.sum(branch_grad.astype(F32), axis=0, keepdims=True),
        jnp.sum(seed, axis=0, keepdims=True),
    ]
    r.pay[...] = jnp.zeros_like(r.pay)
    for v, vector in enumerate(vectors):
        for k in range(D // LANES):
            at = PAY_VEC + v * (D // LANES) + k
            r.pay[at : at + 1, :] = vector[:, k * LANES : (k + 1) * LANES]
    par_grad = r.par_grad
    par_grad[...] = jnp.zeros_like(par_grad)
    par_grad[5:6, 0:hidden] = jnp.sum(r.hidden_grad[...].astype(F32), axis=0, keepdims=True)
    sum_cross(3)
    sum_cross(2)
    gather_finish(3, r.g_back)
    for t in range(chunks):
        link_start(2, t)
    r.grad_out[...] = dot_tn(r.mixed[...], r.g_back[...]).astype(BF16)
    sum_start(1)

    skip_total = jnp.zeros((1, LANES), F32)
    for i in range(COUNT):
        at = slice(i * BLOCK, (i + 1) * BLOCK)
        lanes = slice(i * LANES, (i + 1) * LANES)
        mixed_grad = dot_nt(r.g_back[at, :], r.wout[...])
        r.short_grad[at, 0:LANES] = mixed_grad * r.direct[at, :]
        direct_grad = mixed_grad * r.short[at, 0:LANES]
        r.direct[at, :] = direct_grad
        r.direct_low[:, lanes] = direct_grad.astype(BF16)
        skip_total += jnp.sum(
            direct_grad * r.signal[:, lanes].astype(F32), axis=0, keepdims=True
        )
    par_grad[4:5, 0:LANES] = skip_total
    r.grad_wave[...] = dot(near, r.direct_low[...])
    r.back_product[...] = jnp.zeros_like(r.back_product)

    def backward_wave(n, carry):
        at = pl.multiple_of(n * step, step)
        kernels, signals = load_wave(r.kernel_wave, at), load_wave(r.signal_wave, at)
        grads = load_wave(r.grad_wave, at)
        for p in range(COUNT):
            terms = [(joined[i][p], times_conj(kernels[i - p], grads[i])) for i in range(p, COUNT)]
            store_wave(r.product, 0, at, p, weighted(terms))
        for d in range(COUNT):
            terms = [
                (joined[i][i - d], times_conj(signals[i - d], grads[i])) for i in range(d, COUNT)
            ]
            pair = weighted(terms)
            store_wave(r.back_product, 0, at, d, pair)
            if d:
                store_wave(r.back_product, BINS, at, d - 1, pair)
        return carry

    lax.fori_loop(0, BLOCK // step, backward_wave, 0)
    signal_grads = dot(unnear, r.product[0:BINS, :])
    for i in range(COUNT):
        at = slice(i * BLOCK, (i + 1) * BLOCK)
        lanes = slice(i * LANES, (i + 1) * LANES)
        signal_grad = (signal_grads[:, lanes] + skip * r.direct[at, :]) * valid[i]
        r.short_grad[at, LANES : 2 * LANES] = signal_grad * r.short[at, 2 * LANES :]
        r.short_grad[at, 2 * LANES :] = signal_grad * r.short[at, LANES : 2 * LANES]

    bias_total = jnp.zeros((1, WIDE), F32)
    tap_totals = [jnp.zeros((1, WIDE), F32) for _ in range(3)]
    for i in range(COUNT):
        at = slice(i * BLOCK, (i + 1) * BLOCK)
        now, one, two = back_rows(i)
        grad = r.short_grad[at, :]
        for t, value in enumerate((now, one, two)):
            tap_totals[t] += jnp.sum(grad * value, axis=0, keepdims=True)
        next_one = pltpu.roll(grad, BLOCK - 1, 0)
        next_two = pltpu.roll(grad, BLOCK - 2, 0)
        if i + 1 < COUNT:
            edge = r.short_grad[(i + 1) * BLOCK : (i + 1) * BLOCK + 8, :] * follows[i + 1]
            head, after = edge[0:1], edge[1:2]
        else:
            head = after = jnp.zeros((1, WIDE), F32)
        next_one = jnp.where(rows_here == BLOCK - 1, head, next_one)
        next_two = jnp.where(
            rows_here == BLOCK - 2, head, jnp.where(rows_here == BLOCK - 1, after, next_two)
        )
        low = (
            r.taps[1:2, :] * grad + r.taps[2:3, :] * next_one + r.taps[3:4, :] * next_two
        ).astype(BF16)
        bias_total += jnp.sum(low.astype(F32), axis=0, keepdims=True)
        r.projected_grad[at, :] = dot_nt(low, r.order[...]).astype(BF16)
    par_grad[0:1, :] = bias_total
    for t in range(3):
        par_grad[t + 1 : t + 2, :] = tap_totals[t]

    sum_cross(1)

    r.gain_sum[...] = jnp.zeros_like(r.gain_sum)

    def normed_back(at):
        value = dot(r.projected_grad[at, :], r.win[...])
        weighed = value * r.g_one[at, :].astype(F32)
        r.gain_sum[...] += jnp.sum(jnp.reshape(weighed, (BLOCK // 8, 8, D)), axis=0)
        return value

    scatter(3, normed_back)

    weight_grad(r.grad_in, r.projected_grad, r.g_one, True)
    sum_start(0)

    kernel_grads = dot(r.unwaves[...], r.back_product[...])
    decay_total = jnp.zeros((1, LANES), F32)
    penalty = jnp.zeros((1, LANES), F32)
    own_filter = r.own_filter[...]
    own_decay = r.own_decay[0:1, :]
    lead = jnp.where(pack == 0, 1.0 / D, 0.0).astype(F32)
    for i in range(COUNT):
        at = slice(i * BLOCK, (i + 1) * BLOCK)
        tau = (
            lax.broadcasted_iota(jnp.int32, (BLOCK, LANES), 0) + i * BLOCK
        ).astype(F32) * (1.0 / LONG)
        kernel = r.kernel[at, :]
        weighed = tau * kernel
        penalty += jnp.sum(weighed * kernel, axis=0, keepdims=True) * lead
        kernel_grad = (
            kernel_grads[:, i * LANES : (i + 1) * LANES] + weighed * (2.0 * lead)
        )
        decay_total -= jnp.sum(kernel_grad * weighed, axis=0, keepdims=True)
        r.raw_grad[at, :] = kernel_grad * jnp.exp(-tau * own_decay)
    sums_y, sums_q = r.shard_y, r.shard_q
    sums_y[y] = jnp.zeros((SHARD_ROWS, LANES), F32)
    sums_y[y, 0:FILT, :] = dot(r.second[...], r.raw_grad[...], precision=HIGH)
    sums_y[y, SHARD_DECAY : SHARD_DECAY + 1, :] = decay_total
    for k in range(3):
        at = SHARD_PAR + 8 * k
        sums_y[y, at : at + 8, :] = par_grad[:, k * LANES : (k + 1) * LANES]

    def shard_y(dy, back=False):
        at = sums_y.at[(y + ranks - dy) % ranks if back else y]
        return remote(
            at, at, r.sy_send.at[dy], r.sy_recv.at[dy], device((y + dy) % ranks, c, q, j)
        )

    def shard_q(back=False):
        at = sums_q.at[across if back else q]
        return remote(at, at, r.sq_send.at[0], r.sq_recv.at[0], device(y, c, across, j))

    for dy in range(1, ranks):
        shard_y(dy).start()
    r.pay[PAY_PEN : PAY_PEN + 1, :] = penalty
    gain_row = jnp.sum(r.gain_sum[...], axis=0, keepdims=True) / line(r.mixer_gain)
    for k in range(D // LANES):
        at = PAY_VEC + 3 * (D // LANES) + k
        r.pay[at : at + 1, :] = gain_row[:, k * LANES : (k + 1) * LANES]
    second_grad = dot_nt(own_filter, r.raw_grad[...], HIGH)
    angle_grad = second_grad * r.second_cos[...]
    freq_grad = jnp.sum(angle_grad * r.second_sum[...], axis=1, keepdims=True)
    sum_grad = angle_grad * column(line(r.hidden_freq))
    at = slice(PAY_HID, PAY_HID + FILT)
    r.pay[at, 0:FILT] = dot_nt(r.first[...], sum_grad, HIGH)
    r.pay[at, FILT : FILT + 1] = freq_grad
    r.pay[at, FILT + 1 : FILT + 2] = jnp.sum(sum_grad, axis=1, keepdims=True)
    angle_grad = dot(r.hidden_weight[...], sum_grad, precision=HIGH) * r.first_cos[...]
    r.pay[at, FILT + 2 : FILT + 3] = jnp.sum(
        angle_grad * r.first_sum[...], axis=1, keepdims=True
    )
    sum_grad = angle_grad * column(line(r.embed_freq))
    r.pay[at, FILT + 3 : FILT + 4] = jnp.sum(sum_grad, axis=1, keepdims=True)
    r.pay[PAY_EMB : PAY_EMB + EMB, 0:FILT] = dot_nt(features, sum_grad, HIGH)

    half_pay = PAY_ROWS // 2
    part_pay = half_pay // halves
    slot = y * 2 + q

    def pay_half(cc):
        return pl.ds(pl.multiple_of(cc * half_pay, half_pay), half_pay)

    def pay_chip():
        return remote(
            r.pay.at[pay_half(other)], r.pay_in, r.pay_send.at[0], r.pay_recv.at[0], sibling
        )

    def pay_link(jj):
        at = pl.ds(pl.multiple_of(jj * part_pay, part_pay), part_pay)
        return remote(
            r.pay_sum.at[at],
            r.pay_held.at[j],
            r.paylink_send.at[jj],
            r.paylink_recv.at[j],
            device(y, c, q, jj),
        )

    def slots_copies(n, held):
        out = []
        for dy in range(ranks):
            for dq in range(2):
                if dy or dq:
                    out.append(
                        remote(
                            held.at[slot],
                            held.at[slot],
                            r.cross_send.at[n, dy * 2 + dq],
                            r.cross_recv.at[n, dy * 2 + dq],
                            device((y + dy) % ranks, c, (q + dq) % 2, j),
                        )
                    )
        return out

    def slots_sum(n, held):
        for dy in range(ranks):
            for dq in range(2):
                if dy or dq:
                    yy, qq = (y + ranks - dy) % ranks, (q + dq) % 2
                    came = held.at[yy * 2 + qq]
                    remote(
                        came,
                        came,
                        r.cross_send.at[n, dy * 2 + dq],
                        r.cross_recv.at[n, dy * 2 + dq],
                        device(yy, c, qq, j),
                    ).wait_recv()
        return added(held, 2 * ranks)

    def added(held, count):
        total = held[0]
        for i in range(1, count):
            total = total + held[i]
        return total

    pay_chip().start()
    for w in (3, 2, 1):
        sum_close(w)

    pay_chip().wait_recv()
    r.pay_sum[...] = r.pay[pay_half(c), :] + r.pay_in[...]
    for k in range(1, halves):
        pay_link(ahead(k)).start()
    r.pay_held[j] = r.pay_sum[pl.ds(pl.multiple_of(j * part_pay, part_pay), part_pay), :]
    for dy in range(1, ranks):
        shard_y(dy, True).wait_recv()
    sums_q[q] = added(sums_y, ranks)
    shard_q().start()
    sum_cross(0)

    r.block_out[...] = (r.middle[...] + line(r.down_bias) + scatter_finish(2)).astype(BF16)
    gives = [(r.input_grad, r.input_any), (r.block_out, r.block_any)]

    def give(i):
        src, dst = gives[i]
        return remote(src, dst, r.give_send.at[i], r.give_recv.at[i], partner)

    def give_local(i):
        src, dst = gives[i]
        return pltpu.make_async_copy(src, dst, r.give_local.at[i])

    def give_start(i):
        @pl.when(moved)
        def _():
            give(i).start()

        @pl.when(owner)
        def _():
            give_local(i).start()

    give_start(1)

    for k in range(1, halves):
        jj = behind(k)
        remote(
            r.pay_held.at[jj],
            r.pay_held.at[jj],
            r.paylink_send.at[jj],
            r.paylink_recv.at[jj],
            device(y, c, q, jj),
        ).wait_recv()
    r.pay_cross[slot] = added(r.pay_held, halves)
    for copy in slots_copies(0, r.pay_cross):
        copy.start()
    shard_q(True).wait_recv()
    r.shards[pl.ds(pl.multiple_of(shard * SHARD_ROWS, SHARD_ROWS), SHARD_ROWS), :] = added(
        sums_q, 2
    )
    gather_start(4, r.shards)

    unit, scale = norm_parts(r.x_in[...].astype(F32))
    mixer_back = scatter_finish(3)
    r.input_grad[...] = (
        r.middle_grad[...] + norm_back(mixer_back, line(r.mixer_gain), unit, scale)
    ).astype(BF16)
    give_start(0)
    def store(name):
        i = s.stores.index(name)
        return pltpu.make_async_copy(
            getattr(r, name), getattr(r, name + "_out"), r.store_sem.at[i]
        )

    r.pay_total[seat(5, c, j), :] = slots_sum(0, r.pay_cross)
    gather_start(5, r.pay_total)
    sum_close(0)
    gather_finish(4, r.shards)
    store("shards").start()
    home = pl.multiple_of((q * halves + j) * SHARD_ROWS, SHARD_ROWS)
    wide = jnp.concatenate(
        [r.shards[pl.ds(home + SHARD_PAR + 8 * k, 8), :] for k in range(3)], axis=1
    )
    r.par_wide[...] = wide
    r.par_close[...] = dot_nt(wide, r.order_wide[...], HIGH)
    store("par_wide").start()
    store("par_close").start()
    for w, name in ((3, "gwdn"), (2, "gwup"), (1, "gwout")):
        sum_finish(w)
        store(name).start()
    gather_finish(5, r.pay_total)
    store("pay_total").start()
    sum_finish(0)
    store("gwin").start()
    for name in s.stores:
        store(name).wait()

    pay_chip().wait_send()
    for k in range(1, halves):
        pay_link(ahead(k)).wait_send()
    for dy in range(1, ranks):
        shard_y(dy).wait_send()
    shard_q().wait_send()
    for copy in slots_copies(0, r.pay_cross):
        copy.wait_send()

    @pl.when(moved)
    def _():
        for i in (w_out, w_up, w_down):
            take(i).wait_send()
        for i in range(len(gives)):
            give(i).wait()

    @pl.when(owner)
    def _():
        for i in range(len(gives)):
            give_local(i).wait()


def close(s, names, *refs):
    r = types.SimpleNamespace(**dict(zip(names, refs)))
    lines = D // LANES

    def load(name):
        i = s.loads.index(name)
        return pltpu.make_async_copy(
            getattr(r, name + "_any"), getattr(r, name), r.load_sem.at[i]
        )

    def store(name):
        i = s.stores.index(name)
        return pltpu.make_async_copy(getattr(r, name), getattr(r, name + "_out"), r.store_sem.at[i])

    def put(**values):
        for name, value in values.items():
            held = getattr(r, name)
            held[...] = value if value.shape == held.shape else jnp.reshape(value, held.shape)
            store(name).start()

    for name in s.loads:
        load(name).start()
    load("block").wait()
    through = pltpu.make_async_copy(r.block, r.block_out, r.block_sem)
    through.start()
    for name in ("gwin", "gwup", "gwdn", "gwout", "input"):
        load(name).wait()
        held = getattr(r, name)
        size = getattr(r, name + "_wide").shape[0]
        put(**{name + "_wide": held[0:size, :].astype(F32)})
    load("pay_total").wait()
    pay = r.pay_total

    def long_row(ref, at):
        return jnp.concatenate([ref[at + k : at + k + 1, :] for k in range(lines)], axis=1)

    same = lax.broadcasted_iota(jnp.int32, (FILT, FILT), 0) == lax.broadcasted_iota(
        jnp.int32, (FILT, FILT), 1
    )

    def vector_of(k):
        col = pay[PAY_HID : PAY_HID + FILT, FILT + k : FILT + k + 1]
        return jnp.sum(jnp.where(same, col, 0.0), axis=0, keepdims=True)

    put(ffn_gain=long_row(pay, PAY_VEC))
    put(out_bias=long_row(pay, PAY_VEC + lines))
    put(down_bias=long_row(pay, PAY_VEC + 2 * lines))
    put(embed_weight=pay[PAY_EMB : PAY_EMB + EMB, 0:FILT])
    put(embed_bias=vector_of(3))
    put(embed_freq=vector_of(2))
    put(hidden_weight=pay[PAY_HID : PAY_HID + FILT, 0:FILT])
    put(hidden_bias=vector_of(1))
    put(hidden_freq=vector_of(0))
    r.penalty_out[0] = jnp.sum(pay[PAY_PEN : PAY_PEN + 1, :])
    put(mixer_gain=long_row(pay, PAY_VEC + 3 * lines))
    load("par_wide").wait()
    load("par_close").wait()
    put(in_bias=r.par_close[0:1, :])
    put(short_taps=r.par_close[1:4, :])
    put(skip_gain=r.par_wide[4:5, 0 : s.channels])
    put(up_bias=r.par_wide[5:6, 0 : s.hidden])
    load("shards").wait()
    for i in range(2 * s.halves):
        at = slice(i * s.channels, (i + 1) * s.channels)
        base = i * SHARD_ROWS
        r.filter_weight[:, at] = r.shards[base : base + FILT, 0 : s.channels]
        r.decay_row[0:1, at] = r.shards[
            base + SHARD_DECAY : base + SHARD_DECAY + 1, 0 : s.channels
        ]
    store("filter_weight").start()
    put(decay_rate=r.decay_row[0:1, :])
    for name in s.stores:
        store(name).wait()
    through.wait()


def round_up(value, unit):
    return (value + unit - 1) // unit * unit


def solution(mesh):
    n_dp, n_mp = mesh.shape["dp"], mesh.shape["mp"]

    def per_device(
        block_input,
        mixer_gain,
        in_weight,
        in_bias,
        short_taps,
        skip_gain,
        out_weight,
        out_bias,
        ffn_gain,
        up_weight,
        up_bias,
        down_weight,
        down_bias,
        embed_weight,
        embed_bias,
        embed_freq,
        hidden_weight,
        hidden_bias,
        hidden_freq,
        filter_weight,
        decay_rate,
        out_grad,
        sequence_lengths,
        sequence_rank,
        sequence_offset,
    ):
        ranks, halves = n_dp // 2, n_mp // 2
        rows = block_input.shape[0]
        channels, hidden = skip_gain.shape[0], up_weight.shape[1]
        down_rows = round_up(hidden, 16 * ranks)
        in_rows = round_up(3 * channels, 16 * ranks)
        group = 2 * halves
        anywhere = pl.BlockSpec(memory_space=pl.ANY)
        scalar = pl.BlockSpec(memory_space=pltpu.SMEM)
        small = dict(
            mixer_gain=mixer_gain,
            ffn_gain=ffn_gain,
            out_bias=out_bias,
            down_bias=down_bias,
            in_bias=in_bias,
            short_taps=short_taps,
            skip_gain=skip_gain,
            embed_weight=embed_weight,
            embed_bias=embed_bias,
            embed_freq=embed_freq,
            hidden_weight=hidden_weight,
            hidden_bias=hidden_bias,
            hidden_freq=hidden_freq,
            filter_weight=filter_weight,
            decay_rate=decay_rate,
            features=jnp.asarray(position_features(), F32),
            waves=jnp.asarray(WAVES, BF16),
            unwaves=jnp.asarray(UNWAVES, BF16),
        )
        inputs = dict(
            x_any=(block_input, anywhere),
            og_any=(out_grad, anywhere),
            win_any=(in_weight.T, anywhere),
            wout_any=(out_weight, anywhere),
            wup_any=(up_weight, anywhere),
            wdn_any=(down_weight, anywhere),
            up_bias=(up_bias, pl.BlockSpec(memory_space=pltpu.VMEM)),
            lengths=(sequence_lengths, scalar),
            owners=(sequence_rank, scalar),
            offsets=(sequence_offset, scalar),
        )
        for name, value in small.items():
            inputs[name + "_any"] = (value, anywhere)
        kept = dict(
            gwin=((in_rows, D), BF16),
            gwout=((LANES, D), BF16),
            gwup=((D, hidden), BF16),
            gwdn=((down_rows, D), BF16),
            pay_total=((PAY_ROWS, LANES), F32),
            shards=((group * SHARD_ROWS, LANES), F32),
            par_wide=((8, WIDE), F32),
            par_close=((8, 3 * channels), F32),
        )
        outputs = dict(block_any=((rows, D), BF16), input_any=((rows, D), BF16))
        for name, kind in kept.items():
            outputs[name + "_out"] = kind
        sizes = types.SimpleNamespace(
            ranks=ranks,
            halves=halves,
            inner=n_mp // 4,
            rows=rows,
            channels=channels,
            hidden=hidden,
            sequences=sequence_lengths.shape[0],
            loads=list(small),
            late_loads=("features", "waves", "unwaves"),
            stores=list(kept),
        )
        dma = pltpu.SemaphoreType.DMA
        scratch = {}

        def hold(**held):
            for name, kind in held.items():
                scratch[name] = pltpu.VMEM(*kind)

        for name, value in small.items():
            scratch[name] = pltpu.VMEM(value.shape, value.dtype)
        for name, kind in kept.items():
            scratch[name] = pltpu.VMEM(*kind)
        hold(x_in=((rows, D), BF16))
        hold(unit=((rows, D), F32))
        hold(scale=((rows, LANES), F32))
        hold(par_own=((8, WIDE), F32))
        hold(par_in=((8, WIDE), F32))
        hold(par_grad=((8, WIDE), F32))
        hold(taps=((8, WIDE), F32))
        hold(win=((3 * channels, D), BF16))
        hold(win_apart=((WIDE, D), BF16))
        hold(wout=((LANES, D), BF16))
        hold(wup=((D, hidden), BF16))
        hold(wdn=((hidden, D), BF16))
        hold(order=((3 * channels, WIDE), BF16))
        hold(order_wide=((3 * channels, WIDE), F32))
        hold(first=((FILT, LONG), F32))
        hold(first_sum=((FILT, LONG), F32))
        hold(first_cos=((FILT, LONG), F32))
        hold(second=((FILT, LONG), F32))
        hold(second_sum=((FILT, LONG), F32))
        hold(second_cos=((FILT, LONG), F32))
        hold(own_filter=((FILT, LANES), F32))
        hold(own_decay=((8, LANES), F32))
        hold(kernel=((LONG, LANES), F32))
        hold(raw_grad=((LONG, LANES), F32))
        hold(spread=((BINS, COUNT * LANES), BF16))
        hold(kernel_wave=((BINS, COUNT * LANES), F32))
        hold(signal_wave=((BINS, COUNT * LANES), F32))
        hold(grad_wave=((BINS, COUNT * LANES), F32))
        hold(product=((BINS, COUNT * LANES), BF16))
        hold(back_product=((2 * BINS, COUNT * LANES), BF16))
        hold(g_one=((LONG, D), BF16))
        hold(g_out=((LONG, D), BF16))
        hold(g_two=((LONG, D), BF16))
        hold(g_back=((LONG, D), BF16))
        hold(projected=((LONG, WIDE), F32))
        hold(short=((LONG, WIDE), F32))
        hold(short_grad=((LONG, WIDE), F32))
        hold(signal=((BLOCK, COUNT * LANES), BF16))
        hold(direct_low=((BLOCK, COUNT * LANES), BF16))
        hold(direct=((LONG, LANES), F32))
        hold(mixed=((LONG, LANES), BF16))
        hold(middle=((rows, D), F32))
        hold(middle_grad=((rows, D), F32))
        hold(input_grad=((rows, D), BF16))
        hold(block_out=((rows, D), BF16))
        hold(active=((LONG, hidden), BF16))
        hold(hidden_grad=((LONG, hidden), BF16))
        hold(projected_grad=((LONG, 3 * channels), BF16))
        hold(chip_out=((4, LONG // 2, D), BF16))
        hold(chip_in=((4, LONG // 2, D), BF16))
        hold(link_out=((4, LONG // 2, D), BF16))
        hold(link_in=((4, LONG // 2, D), BF16))
        for name, full in dict(
            _in=(in_rows, D), _out=(LANES, D), _up=(D, hidden), _dn=(down_rows, D)
        ).items():
            part = (full[0] // ranks, full[1])
            for kind, shape in dict(grad=full, part=part, y=(ranks,) + part, z=part).items():
                scratch[kind + name] = pltpu.VMEM(shape, BF16)
        hold(gain_sum=((8, D), F32))
        hold(pay=((PAY_ROWS, LANES), F32))
        hold(pay_in=((PAY_ROWS // 2, LANES), F32))
        hold(pay_sum=((PAY_ROWS // 2, LANES), F32))
        hold(pay_held=((halves, PAY_ROWS // group, LANES), F32))
        hold(pay_cross=((2 * ranks, PAY_ROWS // group, LANES), F32))
        hold(shard_y=((ranks, SHARD_ROWS, LANES), F32))
        hold(shard_q=((2, SHARD_ROWS, LANES), F32))
        for name, shape in dict(
            take=(7,),
            give=(2,),
            cut=(7, ranks),
            gather=(6, halves),
            hop=(6, halves),
            chip=(4, LONG // 2 // BLOCK),
            link=(4, halves),
            y=(4, ranks),
            z=(4,),
            out=(4, ranks),
            fin=(4, ranks),
            pay=(1,),
            paylink=(halves,),
            sy=(ranks,),
            sq=(1,),
            cross=(2, 2 * ranks),
        ).items():
            scratch[name + "_send"] = dma(shape)
            scratch[name + "_recv"] = dma(shape)
        scratch["take_local"] = dma((7,))
        scratch["give_local"] = dma((2,))
        scratch["load_sem"] = dma((len(small),))
        scratch["store_sem"] = dma((len(kept),))
        names = list(inputs) + list(outputs) + list(scratch)
        results = pl.pallas_call(
            functools.partial(fused, sizes, names),
            out_shape=[jax.ShapeDtypeStruct(*kind) for kind in outputs.values()],
            in_specs=[i[1] for i in inputs.values()],
            out_specs=[anywhere for _ in outputs],
            scratch_shapes=list(scratch.values()),
            compiler_params=pltpu.CompilerParams(
                collective_id=0,
                has_side_effects=True,
                vmem_limit_bytes=60 * 2**20,
            ),
            name="block",
        )(*[i[0] for i in inputs.values()])
        finals = dict(
            gwin_wide=(3 * channels, D),
            gwout_wide=(channels, D),
            gwup_wide=(D, hidden),
            gwdn_wide=(hidden, D),
            input_wide=(rows, D),
            mixer_gain=(D,),
            in_bias=(3 * channels,),
            short_taps=(3, 3 * channels),
            skip_gain=(channels,),
            out_bias=(D,),
            ffn_gain=(D,),
            up_bias=(hidden,),
            down_bias=(D,),
            embed_weight=(EMB, FILT),
            embed_bias=(FILT,),
            embed_freq=(FILT,),
            hidden_weight=(FILT, FILT),
            hidden_bias=(FILT,),
            hidden_freq=(FILT,),
            filter_weight=(FILT, D),
            decay_rate=(D,),
        )
        loads = ["block", "input"] + list(kept)
        closing = types.SimpleNamespace(
            halves=halves, channels=channels, hidden=hidden, loads=loads, stores=list(finals)
        )
        scratch = dict(
            block=pltpu.VMEM((rows, D), BF16),
            input=pltpu.VMEM((rows, D), BF16),
            decay_row=pltpu.VMEM((8, D), F32),
        )
        for name, kind in kept.items():
            scratch[name] = pltpu.VMEM(*kind)
        for name, shape in finals.items():
            scratch[name] = pltpu.VMEM(shape, F32)
        scratch["load_sem"] = dma((len(loads),))
        scratch["store_sem"] = dma((len(finals),))
        scratch["block_sem"] = dma
        names = [name + "_any" for name in loads] + ["block_out"]
        names += [name + "_out" for name in finals] + ["penalty_out"] + list(scratch)
        done = pl.pallas_call(
            functools.partial(close, closing, names),
            out_shape=[jax.ShapeDtypeStruct((rows, D), BF16)]
            + [jax.ShapeDtypeStruct(shape, F32) for shape in finals.values()]
            + [jax.ShapeDtypeStruct((1,), F32)],
            in_specs=[anywhere] * len(loads),
            out_specs=[anywhere] * (1 + len(finals)) + [scalar],
            scratch_shapes=list(scratch.values()),
            compiler_params=pltpu.CompilerParams(vmem_limit_bytes=60 * 2**20),
            name="close",
        )(*results)
        out = types.SimpleNamespace(**dict(zip(finals, done[1:-1])))
        return (
            done[0],
            out.input_wide,
            done[-1].reshape(()),
            out.mixer_gain,
            out.gwin_wide.T,
            out.in_bias,
            out.short_taps,
            out.skip_gain,
            out.gwout_wide,
            out.out_bias,
            out.ffn_gain,
            out.gwup_wide,
            out.up_bias,
            out.gwdn_wide,
            out.down_bias,
            out.embed_weight,
            out.embed_bias,
            out.embed_freq,
            out.hidden_weight,
            out.hidden_bias,
            out.hidden_freq,
            out.filter_weight,
            out.decay_rate,
        )

    placed = (
        P(("dp", "mp"), None),
        P(),
        P(None, "mp"),
        P("mp"),
        P(None, "mp"),
        P("mp"),
        P("mp", None),
        P(),
        P(),
        P(None, "mp"),
        P("mp"),
        P("mp", None),
        P(),
        P(),
        P(),
        P(),
        P(),
        P(),
        P(),
        P(),
        P(),
        P(("dp", "mp"), None),
        P(),
        P(),
        P(),
    )
    return jax.shard_map(
        per_device,
        mesh=mesh,
        in_specs=placed,
        out_specs=(
            P(("dp", "mp"), None),
            P(("dp", "mp"), None),
            P(),
            P(),
            P(None, "mp"),
            P("mp"),
            P(None, "mp"),
            P("mp"),
            P("mp", None),
            P(),
            P(),
            P(None, "mp"),
            P("mp"),
            P("mp", None),
            P(),
            P(),
            P(),
            P(),
            P(),
            P(),
            P(),
            P(),
            P(),
        ),
        check_vma=False,
    )
```
